32 devices in a mesh: dp: 8 (over y, x, core), seq: 4 (over z).
Axes of the slice: x: 2, y: 2, z: 4, core: 2. Of those that a mesh axis runs over, the one named last changes fastest.
Arguments:
- inputs: bfloat16 [16, 16, 256, 768], P('dp', 'seq'), may hold values from -6 to 6
- norm_one_gain: bfloat16 [768], P(('dp', 'seq')), may hold values from 0.25 to 1.75
- norm_one_shift: bfloat16 [768], P(('dp', 'seq')), may hold values from -2 to 2
- space_qkv: bfloat16 [768, 2304], P(('dp', 'seq')), may hold values from -0.21875 to 0.21875
- space_qv_bias: bfloat16 [1536], P(('dp', 'seq')), may hold values from -2 to 2
- space_out: bfloat16 [768, 768], P(('dp', 'seq')), may hold values from -0.875 to 0.875
- space_out_bias: bfloat16 [768], P(('dp', 'seq')), may hold values from -2 to 2
- norm_two_gain: bfloat16 [768], P(('dp', 'seq')), may hold values from 0.25 to 1.75
- norm_two_shift: bfloat16 [768], P(('dp', 'seq')), may hold values from -2 to 2
- time_qkv: bfloat16 [768, 2304], P(('dp', 'seq')), may hold values from -0.21875 to 0.21875
- time_qv_bias: bfloat16 [1536], P(('dp', 'seq')), may hold values from -2 to 2
- time_out: bfloat16 [768, 768], P(('dp', 'seq')), may hold values from -0.4375 to 0.4375
- time_out_bias: bfloat16 [768], P(('dp', 'seq')), may hold values from -2 to 2
- norm_three_gain: bfloat16 [768], P(('dp', 'seq')), may hold values from 0.25 to 1.75
- norm_three_shift: bfloat16 [768], P(('dp', 'seq')), may hold values from -2 to 2
- mlp_in: bfloat16 [768, 3072], P(('dp', 'seq')), may hold values from -0.21875 to 0.21875
- mlp_in_bias: bfloat16 [3072], P(('dp', 'seq')), may hold values from -2 to 2
- mlp_out: bfloat16 [3072, 768], P(('dp', 'seq')), may hold values from -0.109375 to 0.109375
- mlp_out_bias: bfloat16 [768], P(('dp', 'seq')), may hold values from -2 to 2
- cotangent: bfloat16 [16, 16, 256, 768], P('dp', 'seq'), may hold values from -6 to 6
Outputs:
- output: bfloat16 [16, 16, 256, 768], P('dp', 'seq')
- grad_inputs: bfloat16 [16, 16, 256, 768], P('dp', 'seq')
- grad_norm_one_gain: float32 [768], P(('dp', 'seq'))
- grad_norm_one_shift: float32 [768], P(('dp', 'seq'))
- grad_space_qkv: float32 [768, 2304], P(('dp', 'seq'))
- grad_space_qv_bias: float32 [1536], P(('dp', 'seq'))
- grad_space_out: float32 [768, 768], P(('dp', 'seq'))
- grad_space_out_bias: float32 [768], P(('dp', 'seq'))
- grad_norm_two_gain: float32 [768], P(('dp', 'seq'))
- grad_norm_two_shift: float32 [768], P(('dp', 'seq'))
- grad_time_qkv: float32 [768, 2304], P(('dp', 'seq'))
- grad_time_qv_bias: float32 [1536], P(('dp', 'seq'))
- grad_time_out: float32 [768, 768], P(('dp', 'seq'))
- grad_time_out_bias: float32 [768], P(('dp', 'seq'))
- grad_norm_three_gain: float32 [768], P(('dp', 'seq'))
- grad_norm_three_shift: float32 [768], P(('dp', 'seq'))
- grad_mlp_in: float32 [768, 3072], P(('dp', 'seq'))
- grad_mlp_in_bias: float32 [3072], P(('dp', 'seq'))
- grad_mlp_out: float32 [3072, 768], P(('dp', 'seq'))
- grad_mlp_out_bias: float32 [768], P(('dp', 'seq'))
The draws below stay inside these ranges and needn't reach their ends.
All inputs are finite; a program needn't handle non-finite values.
Results may differ from the reference program's by a relative error of at most 0.023.
Values may be sent and summed in bfloat16 or wider, within the bound.
A program may use at most 448 MiB of HBM per device.

```python
import jax
import jax.numpy as jnp
from jax import lax

D = 768
HEADS = 12
HD = 64
FF = 3072
FRAMES = 16
PLACES = 256
CLIPS = 16


def steps_of(stream_key, shape, shards, least, top_value):
    level = 1.0
    for dim, blocks in shards:
        steps = jax.random.uniform(jax.random.fold_in(jax.random.fold_in(stream_key, 6), dim), (blocks,), jnp.float32, least / len(shards), top_value / len(shards))
        level = level * jnp.repeat(jnp.exp(steps), shape[dim] // blocks).reshape((-1,) + (1,) * (len(shape) - 1 - dim))
    return level


def gaussian(key, shape, deviation, bound, shards=(), held_as=jnp.bfloat16):
    entries = deviation * jax.random.normal(key, shape, jnp.float32)
    if shards:
        entries = entries * steps_of(key, shape, shards, -0.22, 0.18)
    return jnp.clip(entries, -bound, bound).astype(held_as)


def setup_inputs(seed: int = 0) -> dict:
    key_of = jax.random.split(jax.random.key(seed), 21)
    inputs = gaussian(key_of[0], (CLIPS, FRAMES, PLACES, D), 1.0, 6.0, ((0, 8), (1, 4)))
    norm_one_gain = jnp.clip(1.0 + 0.15 * jax.random.normal(key_of[1], (D,), jnp.float32), 0.25, 1.75).astype(jnp.bfloat16)
    norm_one_shift = gaussian(key_of[2], (D,), 0.3, 2.0, ((0, 32),))
    space_qkv = gaussian(key_of[3], (D, 3 * D), D ** -0.5, 0.21875, ((0, 32),))
    space_qv_bias = gaussian(key_of[4], (2 * D,), 0.3, 2.0, ((0, 32),))
    space_out = gaussian(key_of[5], (D, D), (D // 16) ** -0.5, 0.875, ((0, 32),))
    space_out_bias = gaussian(key_of[6], (D,), 0.3, 2.0, ((0, 32),))
    norm_two_gain = jnp.clip(1.0 + 0.15 * jax.random.normal(key_of[7], (D,), jnp.float32), 0.25, 1.75).astype(jnp.bfloat16)
    norm_two_shift = gaussian(key_of[8], (D,), 0.3, 2.0, ((0, 32),))
    time_qkv = gaussian(key_of[9], (D, 3 * D), D ** -0.5, 0.21875, ((0, 32),))
    time_qv_bias = gaussian(key_of[10], (2 * D,), 0.3, 2.0, ((0, 32),))
    time_out = gaussian(key_of[11], (D, D), (D // 4) ** -0.5, 0.4375, ((0, 32),))
    time_out_bias = gaussian(key_of[12], (D,), 0.3, 2.0, ((0, 32),))
    norm_three_gain = jnp.clip(1.0 + 0.15 * jax.random.normal(key_of[13], (D,), jnp.float32), 0.25, 1.75).astype(jnp.bfloat16)
    norm_three_shift = gaussian(key_of[14], (D,), 0.3, 2.0, ((0, 32),))
    mlp_in = gaussian(key_of[15], (D, FF), D ** -0.5, 0.21875, ((0, 32),))
    mlp_in_bias = gaussian(key_of[16], (FF,), 0.3, 2.0, ((0, 32),))
    mlp_out = gaussian(key_of[17], (FF, D), FF ** -0.5, 0.109375, ((0, 32),))
    mlp_out_bias = gaussian(key_of[18], (D,), 0.3, 2.0, ((0, 32),))
    cotangent = gaussian(key_of[19], (CLIPS, FRAMES, PLACES, D), 1.0, 6.0, ((0, 8), (1, 4)))
    return {"inputs": inputs, "norm_one_gain": norm_one_gain, "norm_one_shift": norm_one_shift, "space_qkv": space_qkv, "space_qv_bias": space_qv_bias, "space_out": space_out, "space_out_bias": space_out_bias, "norm_two_gain": norm_two_gain, "norm_two_shift": norm_two_shift, "time_qkv": time_qkv, "time_qv_bias": time_qv_bias, "time_out": time_out, "time_out_bias": time_out_bias, "norm_three_gain": norm_three_gain, "norm_three_shift": norm_three_shift, "mlp_in": mlp_in, "mlp_in_bias": mlp_in_bias, "mlp_out": mlp_out, "mlp_out_bias": mlp_out_bias, "cotangent": cotangent}


EPS = 1e-06
SCALE = 0.125
HIGH = lax.Precision.HIGHEST

@jax.custom_vjp
def low(v):
    return lax.optimization_barrier(v.astype(jnp.bfloat16)).astype(jnp.float32)

@jax.custom_vjp
def low_back(v):
    return v

def low_keep(v):
    return (low(v), None)

def low_pass(kept, grad):
    return (grad,)

def back_keep(v):
    return (v, None)

def back_low(kept, grad):
    return (low(grad),)
low.defvjp(low_keep, low_pass)
low_back.defvjp(back_keep, back_low)

def norm(rows, gain, shift):
    center = rows - lax.optimization_barrier(jnp.mean(rows, axis=-1, keepdims=True))
    rstd_val = lax.rsqrt(lax.optimization_barrier(jnp.mean(center * center, axis=-1, keepdims=True)) + EPS)
    return center * rstd_val * gain + shift

def attend(rows, w_qkv, b_qv, w_out, b_out):
    seq_count, length, width = rows.shape
    bias = jnp.concatenate([b_qv[:width], jnp.zeros_like(b_qv[:width]), b_qv[width:]])
    project = jnp.einsum('bld,de->ble', rows, w_qkv, precision=HIGH) + bias
    project = low(low_back(project)).reshape(seq_count, length, 3, HEADS, HD)
    query, keys, values = (project[:, :, 0], project[:, :, 1], project[:, :, 2])
    scores = low_back(jnp.einsum('blhd,bmhd->bhlm', query, keys, precision=HIGH) * SCALE)
    probs = low(jnp.exp(scores - jax.nn.logsumexp(scores, axis=-1, keepdims=True)))
    mixed = low(low_back(jnp.einsum('bhlm,bmhd->blhd', probs, values, precision=HIGH)))
    mixed = mixed.reshape(seq_count, length, width)
    return jnp.einsum('bld,de->ble', mixed, w_out, precision=HIGH) + b_out

def layer(clip, params):
    gain_one, shift_one, space_qkv, space_bias, space_out, space_out_b, gain_two, shift_two, time_qkv, time_bias, time_out, time_out_b, gain_three, shift_three, mlp_in, mlp_in_b, mlp_out, mlp_out_b = params
    space_rows = low(norm(clip, gain_one, shift_one))
    resid_one = clip + low_back(attend(space_rows, space_qkv, space_bias, space_out, space_out_b))
    time_rows = low(low_back(norm(resid_one, gain_two, shift_two)))
    branch = attend(jnp.transpose(time_rows, (1, 0, 2)), time_qkv, time_bias, time_out, time_out_b)
    resid_two = resid_one + jnp.transpose(low(low_back(branch)), (1, 0, 2))
    mlp_rows = low(norm(resid_two, gain_three, shift_three))
    hidden = low_back(jnp.einsum('fpd,de->fpe', mlp_rows, mlp_in, precision=HIGH) + mlp_in_b)
    active = low(jax.nn.gelu(hidden, approximate=False))
    result = low_back(jnp.einsum('fpe,ed->fpd', active, mlp_out, precision=HIGH) + mlp_out_b)
    return resid_two + result

def reference(inputs, norm_one_gain, norm_one_shift, space_qkv, space_qv_bias, space_out, space_out_bias, norm_two_gain, norm_two_shift, time_qkv, time_qv_bias, time_out, time_out_bias, norm_three_gain, norm_three_shift, mlp_in, mlp_in_bias, mlp_out, mlp_out_bias, cotangent):
    params = tuple((p.astype(jnp.float32) for p in (norm_one_gain, norm_one_shift, space_qkv, space_qv_bias, space_out, space_out_bias, norm_two_gain, norm_two_shift, time_qkv, time_qv_bias, time_out, time_out_bias, norm_three_gain, norm_three_shift, mlp_in, mlp_in_bias, mlp_out, mlp_out_bias)))

    def step(total, pair):
        clip, grad_clip = pair
        result, pull = jax.vjp(layer, clip.astype(jnp.float32), params)
        grad_in, grad_params = pull(grad_clip.astype(jnp.float32))
        total = jax.tree.map(lambda left, right: left + right, total, grad_params)
        return (total, (result.astype(jnp.bfloat16), grad_in.astype(jnp.bfloat16)))
    start = tuple((jnp.zeros_like(p) for p in params))
    total, stacked = lax.scan(step, start, (inputs, cotangent))
    results, grad_inputs = stacked
    g00, g01, g02, g03, g04, g05, g06, g07, g08, g09, g10, g11, g12, g13, g14, g15, g16, g17 = total
    return (results, grad_inputs, g00, g01, g02, g03, g04, g05, g06, g07, g08, g09, g10, g11, g12, g13, g14, g15, g16, g17)
```

```python
import functools
import jax
import jax.numpy as jnp
from jax import lax
from jax.experimental import pallas as pl
from jax.experimental.pallas import tpu as pltpu
from jax.sharding import PartitionSpec as P

HEADS = 12
HD = 64
EPS = 1e-06
SCALE = 0.125
F32 = jnp.float32
BF16 = jnp.bfloat16
RSQRT2 = 0.7071067811865476
RSQRT2PI = 0.3989422804014327


def dot(a, b):
    return jnp.dot(a, b, preferred_element_type=F32)


def dot_nt(a, b):
    return lax.dot_general(a, b, (((1,), (1,)), ((), ())), preferred_element_type=F32)


def fold(rows):
    return jnp.sum(rows.reshape(rows.shape[0] // 8, 8, rows.shape[1]), axis=0)


def norm(rows):
    center = rows - jnp.mean(rows, axis=-1, keepdims=True)
    rstd = lax.rsqrt(jnp.mean(center * center, axis=-1, keepdims=True) + EPS)
    return center * rstd, rstd


def norm_back(du, hat, rstd, gain):
    e = du * gain
    return rstd * (
        e - jnp.mean(e, axis=-1, keepdims=True) - hat * jnp.mean(e * hat, axis=-1, keepdims=True)
    )


def split_heads(pair):
    low = lax.broadcasted_iota(jnp.int32, (1, 2 * HD), 1) < HD
    zero = jnp.zeros_like(pair)
    return jnp.concatenate([jnp.where(low, pair, zero), jnp.where(low, zero, pair)], axis=0)


def join_heads(both):
    n = both.shape[0] // 2
    low = lax.broadcasted_iota(jnp.int32, (1, 2 * HD), 1) < HD
    return jnp.where(low, both[:n], both[n:])


def by_head(left, right):
    n = right.shape[0] // 2
    top = dot(left[:HD], right[:n])
    bottom = dot(left[HD:], right[n:])
    return jnp.concatenate([top, bottom], axis=0)


def attend(qkv_ref, pt_ref, o_ref, period):
    width = HEADS * HD
    n = qkv_ref.shape[0]
    for pair in range(HEADS // 2):
        at = pair * 2 * HD
        q = qkv_ref[:, at : at + 2 * HD] * jnp.asarray(SCALE, BF16)
        k = qkv_ref[:, width + at : width + at + 2 * HD]
        v = qkv_ref[:, 2 * width + at : 2 * width + at + 2 * HD]
        s = dot_nt(split_heads(k), q)
        if period:
            keys = lax.broadcasted_iota(jnp.int32, s.shape, 0) % period
            queries = lax.broadcasted_iota(jnp.int32, s.shape, 1) % period
            s = jnp.where(keys == queries, s, -1e30)
        probs = []
        for half in (s[:n], s[n:]):
            e = jnp.exp(half - jnp.max(half, axis=0, keepdims=True))
            probs.append((e * (1.0 / jnp.sum(e, axis=0, keepdims=True))).astype(BF16))
        p = jnp.concatenate(probs, axis=0)
        pt_ref[pair] = p
        o_ref[:, at : at + 2 * HD] = by_head(v.T, p).astype(BF16).T


def attend_back(qkv_ref, pt_ref, do, dp_ref):
    width = HEADS * HD
    n = qkv_ref.shape[0]
    for pair in range(HEADS // 2):
        at = pair * 2 * HD
        q = qkv_ref[:, at : at + 2 * HD] * jnp.asarray(SCALE, BF16)
        k = qkv_ref[:, width + at : width + at + 2 * HD]
        v = qkv_ref[:, 2 * width + at : 2 * width + at + 2 * HD]
        g = do[:, at : at + 2 * HD]
        p = pt_ref[pair]
        dp = dot_nt(split_heads(v), g)
        wide = p.astype(F32)
        ds = []
        for sl in (slice(0, n), slice(n, 2 * n)):
            t = wide[sl] * dp[sl]
            ds.append((t - wide[sl] * jnp.sum(t, axis=0, keepdims=True)).astype(BF16))
        ds = jnp.concatenate(ds, axis=0)
        dp_ref[:, 2 * width + at : 2 * width + at + 2 * HD] = join_heads(dot(p, g)).astype(BF16)
        dp_ref[:, width + at : width + at + 2 * HD] = join_heads(dot(ds, q)).astype(BF16)
        dp_ref[:, at : at + 2 * HD] = (by_head(k.T, ds) * SCALE).astype(BF16).T


GAIN1, SHIFT1, BO1, GAIN2, SHIFT2, BO2, GAIN3, SHIFT3, BOUT, BQ1, BV1, BQ2, BV2, BIN = range(14)
NARROW = (0, 1, 3, 4, 5, 7, 8, 9, 11)
WIDE = (2, 6)
LONG = 10
VEC_ROWS = 32
SUM_ROWS = 24
VMEM_LIMIT = 60 * 2**20


def row(vec_ref, i):
    return vec_ref[i : i + 1]


def project(a, wqkv_ref, bq, bv, qkv_ref):
    width = a.shape[1]
    for i, bias in enumerate((bq, None, bv)):
        sl = slice(i * width, (i + 1) * width)
        part = dot(a, wqkv_ref[:, sl])
        qkv_ref[:, sl] = (part if bias is None else part + bias).astype(BF16)


def space_rows(x, vec_ref, wqkv_ref, wo_ref, a_ref, qkv_ref, pt_ref, o_ref):
    hat, _ = norm(x)
    a = (hat * row(vec_ref, GAIN1) + row(vec_ref, SHIFT1)).astype(BF16)
    a_ref[...] = a
    project(a, wqkv_ref, row(vec_ref, BQ1), row(vec_ref, BV1), qkv_ref)
    attend(qkv_ref, pt_ref, o_ref, 0)
    return (x + dot(o_ref[...], wo_ref[...]) + row(vec_ref, BO1)).astype(BF16)


def place_rows(
    x1, g16, period, vec_ref, wqkv_ref, wo_ref, win_ref, wout_ref, a2_ref, dp_ref, o_ref, gt_ref, a3_ref, z_ref, dh_ref,
    sum_ref, qkv_ref, pt_ref,
):
    rows, width = x1.shape
    hat2, rstd2 = norm(x1)
    a2 = (hat2 * row(vec_ref, GAIN2) + row(vec_ref, SHIFT2)).astype(BF16)
    a2_ref[...] = a2
    project(a2, wqkv_ref, row(vec_ref, BQ2), row(vec_ref, BV2), qkv_ref)
    attend(qkv_ref, pt_ref, o_ref, period)
    t = (dot(o_ref[...], wo_ref[...]) + row(vec_ref, BO2)).astype(BF16).astype(F32)
    x2 = x1 + t
    hat3, rstd3 = norm(x2)
    a3 = (hat3 * row(vec_ref, GAIN3) + row(vec_ref, SHIFT3)).astype(BF16)
    a3_ref[...] = a3
    g = g16.astype(F32)
    sum_ref[BOUT] += fold(g)
    y = x2 + row(vec_ref, BOUT)
    da3 = jnp.zeros((rows, width), F32)
    for i in range(win_ref.shape[1] // width):
        sl = slice(i * width, (i + 1) * width)
        h = dot(a3, win_ref[:, sl]) + row(vec_ref, BIN + i)
        cdf = 0.5 + 0.5 * lax.erf(h * RSQRT2)
        z = (h * cdf).astype(BF16)
        z_ref[:, sl] = z
        y = y + dot(z, wout_ref[sl, :])
        dz = dot_nt(g16, wout_ref[sl, :])
        dh = (dz * (cdf + h * (RSQRT2PI * jnp.exp(-0.5 * h * h)))).astype(BF16)
        dh_ref[:, sl] = dh
        sum_ref[BIN + i] += fold(dh.astype(F32))
        da3 = da3 + dot_nt(dh, win_ref[:, sl])
    sum_ref[GAIN3] += fold(da3 * hat3)
    sum_ref[SHIFT3] += fold(da3)
    dx2 = g + norm_back(da3, hat3, rstd3, row(vec_ref, GAIN3))
    gt = dx2.astype(BF16)
    gt_ref[...] = gt
    sum_ref[BO2] += fold(gt.astype(F32))
    do = dot_nt(gt, wo_ref[...]).astype(BF16)
    attend_back(qkv_ref, pt_ref, do, dp_ref)
    sum_ref[BQ2] += fold(dp_ref[:, :width].astype(F32))
    sum_ref[BV2] += fold(dp_ref[:, 2 * width :].astype(F32))
    da2 = dot_nt(dp_ref[...], wqkv_ref[...]).astype(BF16).astype(F32)
    sum_ref[GAIN2] += fold(da2 * hat2)
    sum_ref[SHIFT2] += fold(da2)
    dx1 = dx2 + norm_back(da2, hat2, rstd2, row(vec_ref, GAIN2))
    return y.astype(BF16), dx1.astype(BF16)


def space_back_rows(x, g, qkv_ref, pt_ref, vec_ref, wqkv_ref, wo_ref, dp_ref, sum_ref):
    width = x.shape[1]
    sum_ref[BO1] += fold(g.astype(F32))
    do = dot_nt(g, wo_ref[...]).astype(BF16)
    attend_back(qkv_ref, pt_ref, do, dp_ref)
    sum_ref[BQ1] += fold(dp_ref[:, :width].astype(F32))
    sum_ref[BV1] += fold(dp_ref[:, 2 * width :].astype(F32))
    da = dot_nt(dp_ref[...], wqkv_ref[...])
    hat, rstd = norm(x)
    sum_ref[GAIN1] += fold(da * hat)
    sum_ref[SHIFT1] += fold(da)
    return (g.astype(F32) + norm_back(da, hat, rstd, row(vec_ref, GAIN1))).astype(BF16)


def params(collective=None):
    extra = {} if collective is None else {"collective_id": collective, "has_side_effects": True}
    return pltpu.CompilerParams(vmem_limit_bytes=VMEM_LIMIT, dimension_semantics=("arbitrary",), **extra)


def whole(shape):
    return pl.BlockSpec(shape, lambda b: (0,) * len(shape), pipeline_mode=pl.Buffered(1))


def rows_spec(rows, cols):
    return pl.BlockSpec((rows, cols), lambda b: (b, 0))


def sds(*shape, dtype=BF16):
    return jax.ShapeDtypeStruct(shape, dtype)


ANYWHERE = pl.BlockSpec(memory_space=pl.ANY)


def space_kernel(x_ref, vec_ref, wqkv_ref, wo_ref, x1_ref, a_ref, qkv_ref, pt_ref, o_ref):
    x1_ref[0] = space_rows(x_ref[0].astype(F32), vec_ref, wqkv_ref, wo_ref, a_ref, qkv_ref, pt_ref.at[0], o_ref)


def place_kernel(x1_ref, g_ref, vec_ref, wqkv_ref, wo_ref, win_ref, wout_ref, out_ref, dx1_ref, *rest):
    _, frames, places, width = x1_ref.shape
    rows = frames * places
    sum_ref = rest[7]

    @pl.when(pl.program_id(0) == 0)
    def _():
        sum_ref[...] = jnp.zeros_like(sum_ref)

    x1 = x1_ref[0].reshape(rows, width).astype(F32)
    g16 = g_ref[0].reshape(rows, width)
    out, dx1 = place_rows(x1, g16, places, vec_ref, wqkv_ref, wo_ref, win_ref, wout_ref, *rest)
    out_ref[0] = out.reshape(frames, places, width)
    dx1_ref[0] = dx1.reshape(frames, places, width)


def space_back_kernel(x_ref, g_ref, qkv_ref, pt_ref, vec_ref, wqkv_ref, wo_ref, dx_ref, dp_ref, sum_ref):
    @pl.when(pl.program_id(0) == 0)
    def _():
        sum_ref[...] = jnp.zeros_like(sum_ref)

    dx_ref[0] = space_back_rows(
        x_ref[0].astype(F32), g_ref[0], qkv_ref, pt_ref.at[0], vec_ref, wqkv_ref, wo_ref, dp_ref, sum_ref
    )


def probs_spec(rows):
    return pl.BlockSpec((1, HEADS // 2, 2 * rows, rows), lambda b: (b, 0, 0, 0))


def space_fwd(x, vec, wqkv, wo):
    blocks, rows, width = x.shape
    tok = blocks * rows
    seq = pl.BlockSpec((1, rows, width), lambda b: (b, 0, 0))
    return pl.pallas_call(
        space_kernel,
        grid=(blocks,),
        in_specs=[seq, whole(vec.shape), whole(wqkv.shape), whole(wo.shape)],
        out_specs=[seq, rows_spec(rows, width), rows_spec(rows, 3 * width), probs_spec(rows), rows_spec(rows, width)],
        out_shape=[
            sds(*x.shape), sds(tok, width), sds(tok, 3 * width), sds(blocks, HEADS // 2, 2 * rows, rows), sds(tok, width)
        ],
        compiler_params=params(),
        name="space_fwd",
    )(x, vec, wqkv, wo)


def place_all(x1, g, vec, wqkv, wo, win, wout):
    clips, frames, places, width = x1.shape
    rows = 256
    part = rows // frames
    per = places // part
    blocks = clips * per
    tok = blocks * rows
    ff = win.shape[1]
    spec = pl.BlockSpec((1, frames, part, width), lambda b: (b // per, 0, b % per, 0))
    n = rows_spec(rows, width)
    return pl.pallas_call(
        place_kernel,
        grid=(blocks,),
        in_specs=[spec, spec] + [whole(w.shape) for w in (vec, wqkv, wo, win, wout)],
        out_specs=[
            spec, spec, n, rows_spec(rows, 3 * width), n, n, n, rows_spec(rows, ff), rows_spec(rows, ff),
            pl.BlockSpec((SUM_ROWS, 8, width), lambda b: (0, 0, 0)),
        ],
        out_shape=[
            sds(*x1.shape), sds(*x1.shape), sds(tok, width), sds(tok, 3 * width), sds(tok, width), sds(tok, width),
            sds(tok, width), sds(tok, ff), sds(tok, ff), sds(SUM_ROWS, 8, width, dtype=F32),
        ],
        scratch_shapes=[pltpu.VMEM((rows, 3 * width), BF16), pltpu.VMEM((HEADS // 2, 2 * rows, rows), BF16)],
        compiler_params=params(),
        name="place_all",
    )(x1, g, vec, wqkv, wo, win, wout)


def space_bwd(x, g, qkv, pt, vec, wqkv, wo):
    blocks, rows, width = x.shape
    tok = blocks * rows
    seq = pl.BlockSpec((1, rows, width), lambda b: (b, 0, 0))
    return pl.pallas_call(
        space_back_kernel,
        grid=(blocks,),
        in_specs=[
            seq, seq, rows_spec(rows, 3 * width), probs_spec(rows), whole(vec.shape), whole(wqkv.shape), whole(wo.shape)
        ],
        out_specs=[seq, rows_spec(rows, 3 * width), pl.BlockSpec((SUM_ROWS, 8, width), lambda b: (0, 0, 0))],
        out_shape=[sds(*x.shape), sds(tok, 3 * width), sds(SUM_ROWS, 8, width, dtype=F32)],
        compiler_params=params(),
        name="space_bwd",
    )(x, g, qkv, pt, vec, wqkv, wo)


def outer_sum(left, right):
    return lax.dot_general(left, right, (((0,), (0,)), ((), ())), preferred_element_type=F32)


def plain_layer(inputs, cotangent, shards, vec):
    clips, frames, places, width = inputs.shape

    def out_there(rows):
        return lax.all_to_all(rows, "seq", split_axis=2, concat_axis=1, tiled=True)

    def back_home(rows):
        return lax.all_to_all(rows, "seq", split_axis=1, concat_axis=2, tiled=True)

    wqkv, wo, tqkv, to, win, wout = [lax.all_gather(s, ("dp", "seq"), axis=0, tiled=True) for s in shards]
    vec = lax.psum(vec, ("dp", "seq"))
    x = inputs.reshape(clips * frames, places, width)
    cot = out_there(cotangent)
    x1, a1, qkv, pt, o = space_fwd(x, vec, wqkv, wo)
    x1 = out_there(x1.reshape(inputs.shape))
    out, dx1, a2, dp, ot, gt, a3, z, dh, sums = place_all(x1, cot, vec, tqkv, to, win, wout)
    output = back_home(out)
    g1 = back_home(dx1).reshape(x.shape)
    dx, dps, space_sums = space_bwd(x, g1, qkv, pt, vec, wqkv, wo)
    part = 256 // cot.shape[1]
    g = cot.reshape(clips, cot.shape[1], -1, part, width).transpose(0, 2, 1, 3, 4).reshape(-1, width)
    pairs = ((a1, dps), (o, g1.reshape(-1, width)), (a2, dp), (ot, gt), (a3, dh), (z, g))
    grads = []
    for left, right in pairs:
        part = lax.psum_scatter(outer_sum(left, right).astype(BF16), "dp", scatter_dimension=0, tiled=True)
        grads.append(lax.psum_scatter(part, "seq", scatter_dimension=0, tiled=True).astype(F32))
    return output, dx.reshape(inputs.shape), grads, lax.psum((sums + space_sums).sum(1), ("dp", "seq"))


MESH = pl.DeviceIdType.MESH


def position():
    d, z = lax.axis_index("dp"), lax.axis_index("seq")
    return d // 4, lax.rem(d // 2, 2), lax.rem(d, 2), z


def partners():
    y, x, c, z = position()
    return {
        "x": (4 * y + 2 * (1 - x) + c, z),
        "y": (4 * (1 - y) + 2 * x + c, z),
        "core": (4 * y + 2 * x + 1 - c, z),
        "z1": (4 * y + 2 * x + c, lax.rem(z + 1, 4)),
        "z2": (4 * y + 2 * x + c, lax.rem(z + 2, 4)),
        "z3": (4 * y + 2 * x + c, lax.rem(z + 3, 4)),
    }


def enter(peers):
    barrier = pltpu.get_barrier_semaphore()
    for peer in peers.values():
        pl.semaphore_signal(barrier, inc=1, device_id=peer, device_id_type=MESH)
    pl.semaphore_wait(barrier, len(peers))


class Sum:
    def __init__(self, peers, held, got, send, recv):
        self.peers, self.held, self.got, self.send, self.recv = peers, held, got, send, recv

    def copy(self, i, kind, level):
        return pltpu.make_async_remote_copy(
            src_ref=self.held.at[level], dst_ref=self.got.at[i], send_sem=self.send.at[i], recv_sem=self.recv.at[i],
            device_id=self.peers[kind], device_id_type=MESH,
        )

    STAGES = ((("z1", 0), ("z2", 1), ("z3", 2)), (("x", 3),), (("y", 4),), (("core", 5),))

    def start(self, level):
        for kind, i in self.STAGES[level]:
            self.copy(i, kind, level).start()

    def finish(self, level):
        total = self.held[level].astype(F32)
        for kind, i in self.STAGES[level]:
            self.copy(i, kind, level).wait_recv()
            total = total + self.got[i].astype(F32)
        self.held[level + 1] = total.astype(self.held.dtype)

    def drain(self):
        for level, stage in enumerate(self.STAGES):
            for kind, i in stage:
                self.copy(i, kind, level).wait_send()


class Gather:
    def __init__(self, peers, shard, zbuf, group, full, local, send, recv):
        self.peers, self.shard, self.zbuf, self.group, self.full = peers, shard, zbuf, group, full
        self.local, self.send, self.recv = local, send, recv
        self.rows, self.cols = group.shape

    def place(self, which, half):
        y, x, c, _ = position()
        y, x = {"own": (y, x), "x": (y, 1 - x), "y": (1 - y, x), "xy": (1 - y, 1 - x)}[which]
        rows = pl.ds(pl.multiple_of((4 * y + 2 * x + c) * self.rows, self.rows), self.rows)
        n = self.cols // 2
        return (rows, slice(None)) if half is None else (rows, pl.ds(half * n, n))

    PLAN = {
        3: ("own", 0, "x"), 4: ("own", 1, "y"), 5: ("own", 0, "y"), 6: ("x", 0, "y"), 7: ("own", 1, "x"), 8: ("y", 1, "x"),
        9: ("own", None, "core"), 10: ("x", 0, "core"), 11: ("y", 1, "core"), 12: ("y", 0, "core"), 13: ("xy", 0, "core"),
        14: ("x", 1, "core"), 15: ("xy", 1, "core"),
    }

    def copy(self, i):
        if i < 3:
            z = lax.axis_index("seq")
            src, dst, kind = self.shard, self.zbuf.at[z], ("z1", "z2", "z3")[i]
        else:
            which, half, kind = self.PLAN[i]
            at = self.place(which, half)
            src = dst = self.full.at[at]
            if which == "own":
                src = self.group if half is None else self.group.at[:, pl.ds(half * (self.cols // 2), self.cols // 2)]
        return pltpu.make_async_remote_copy(
            src_ref=src, dst_ref=dst, send_sem=self.send.at[i], recv_sem=self.recv.at[i], device_id=self.peers[kind],
            device_id_type=MESH,
        )

    def own_in(self):
        return pltpu.make_async_copy(self.shard, self.zbuf.at[lax.axis_index("seq")], self.local.at[0])

    def own_out(self):
        return pltpu.make_async_copy(self.group, self.full.at[self.place("own", None)], self.local.at[1])

    def start(self, items):
        for i in items:
            self.copy(i).start()

    def arrive(self, items):
        for i in items:
            self.copy(i).wait_recv()

    def step0(self):
        self.own_in().start()
        self.start((0, 1, 2))

    def step1(self):
        self.own_in().wait()
        self.arrive((0, 1, 2))
        self.group[...] = jnp.concatenate([self.zbuf[i].astype(F32) for i in range(4)], axis=0).astype(BF16)
        self.own_out().start()
        self.start((3, 4, 5, 7, 9))

    def step2(self):
        self.arrive((3, 4))
        self.start((6, 8, 10, 11))

    def step3(self):
        self.arrive((5, 7, 6, 8))
        self.start((12, 14, 13, 15))

    def step4(self):
        self.arrive((9, 10, 11, 12, 14, 13, 15))
        self.own_out().wait()

    def drain(self):
        for i in range(16):
            self.copy(i).wait_send()


class Swap:
    def __init__(self, peers, pick, land, local, send, recv):
        self.peers, self.pick, self.land, self.local, self.send, self.recv = peers, pick, land, local, send, recv

    def copies(self):
        z = lax.axis_index("seq")
        for j in range(3):
            yield pltpu.make_async_remote_copy(
                src_ref=self.pick(lax.rem(z + j + 1, 4)), dst_ref=self.land, send_sem=self.send.at[j], recv_sem=self.recv.at[j],
                device_id=self.peers[f"z{j + 1}"], device_id_type=MESH,
            )

    def own(self):
        return pltpu.make_async_copy(self.pick(lax.axis_index("seq")), self.land, self.local)

    def start(self):
        for copy in self.copies():
            copy.start()
        self.own().start()

    def arrive(self):
        for copy in self.copies():
            copy.wait_recv()
        self.own().wait()

    def drain(self):
        for copy in self.copies():
            copy.wait_send()


def rows_at(start, size):
    return pl.ds(pl.multiple_of(start, size), size)


BEFORE = {
    0: ("1 0", "1 1", "2 0", "2 1", "1 2", "3 0", "3 1", "1 3", "4 0", "4 1"),
    1: ("2 2", "2 3", "1 4"), 3: ("3 2", "3 3", "1 5"), 5: ("2 4", "4 2", "4 3"), 7: ("2 5", "3 4"),
}
AFTER = ("3 5", "4 4", "4 5")


def first_kernel(x_ref, vec_ref, *refs):
    shards = refs[:6]
    a_ref, qkv_ref, pt_ref, o_ref, land_ref = refs[6:11]
    fulls, vec_out = refs[11:17], refs[17]
    wqkv_ref, wo_ref, x1_ref = refs[18:21]
    zbufs, groups = refs[21:27], refs[27:33]
    held, got, local, send, recv, vsend, vrecv, keep, xlocal, xsend, xrecv = refs[33:]
    step = pl.program_id(0)
    blocks, rows, width = x1_ref.shape
    per = land_ref.shape[1] // 4
    part = rows // 4
    z = lax.axis_index("seq")
    peers = partners()
    vec = Sum(peers, held, got, vsend, vrecv)
    homes = (wqkv_ref, wo_ref) + tuple(fulls[2:])
    work = [
        Gather(peers, shards[i], zbufs[i], groups[i], homes[i], local.at[i], send.at[i], recv.at[i]) for i in range(6)
    ]

    def swap(b):
        return Swap(
            peers, lambda to: x1_ref.at[b, rows_at(to * part, part)], land_ref.at[b // per, z * per + lax.rem(b, per)],
            xlocal.at[b], xsend.at[b], xrecv.at[b],
        )

    def kept(i):
        return pltpu.make_async_copy(homes[i], fulls[i], keep.at[i])

    def event(name):
        stage, i = name.split()
        getattr(work[int(i)], "step" + stage)()

    @pl.when(step == 0)
    def _():
        held[0] = vec_ref[...]
        enter(peers)
        vec.start(0)
        for w in work:
            w.step0()
        at = 0
        for k, name in enumerate(BEFORE[0]):
            event(name)
            if k % 2 and at < 4:
                vec.finish(at)
                if at < 3:
                    vec.start(at + 1)
                at += 1
        vec_out[...] = held[4].astype(F32)
        kept(0).start()
        kept(1).start()

    for k in (1, 3, 5, 7):

        @pl.when(step == k)
        def _(k=k):
            for name in BEFORE[k]:
                event(name)

    x1_ref[step] = space_rows(
        x_ref[0].astype(F32), vec_out, wqkv_ref, wo_ref, a_ref, qkv_ref, pt_ref.at[0], o_ref
    )
    swap(step).start()

    @pl.when(step == blocks - 1)
    def _():
        for name in AFTER:
            event(name)
        kept(0).wait()
        kept(1).wait()
        vec.drain()
        for w in work:
            w.drain()

        def finish(b, _):
            swap(b).arrive()
            swap(b).drain()
            return 0

        lax.fori_loop(0, blocks, finish, 0)


def first(x, vec, shards, clips):
    blocks, rows, width = x.shape
    tok = blocks * rows
    frames = blocks // clips
    dma = pltpu.SemaphoreType.DMA
    seq = pl.BlockSpec((1, rows, width), lambda b: (b, 0, 0))
    fixed = pl.BlockSpec((VEC_ROWS, width), lambda b: (0, 0))
    out = pl.pallas_call(
        first_kernel,
        grid=(blocks,),
        in_specs=[seq, whole(vec.shape)] + [ANYWHERE] * 6,
        out_specs=[rows_spec(rows, width), rows_spec(rows, 3 * width), probs_spec(rows), rows_spec(rows, width), ANYWHERE]
        + [ANYWHERE] * 6 + [fixed],
        out_shape=[
            sds(tok, width), sds(tok, 3 * width), sds(blocks, HEADS // 2, 2 * rows, rows), sds(tok, width),
            sds(clips, 4 * frames, rows // 4, width),
        ] + [sds(32 * s.shape[0], s.shape[1]) for s in shards] + [sds(VEC_ROWS, width, dtype=F32)],
        scratch_shapes=[
            pltpu.VMEM((width, 3 * width), BF16), pltpu.VMEM((width, width), BF16), pltpu.VMEM((blocks, rows, width), BF16)
        ]
        + [pltpu.VMEM((4, *s.shape), BF16) for s in shards]
        + [pltpu.VMEM((4 * s.shape[0], s.shape[1]), BF16) for s in shards]
        + [
            pltpu.VMEM((5, *vec.shape), BF16), pltpu.VMEM((6, *vec.shape), BF16), dma((6, 2)), dma((6, 16)), dma((6, 16)),
            dma((6,)), dma((6,)), dma((2,)), dma((blocks,)), dma((blocks, 3)), dma((blocks, 3)),
        ],
        compiler_params=params(0),
        name="first",
    )(x, vec.astype(BF16), *shards)
    return out[:4], out[4], out[5:11], out[11]


def middle_kernel(x1_ref, cot_ref, vec_ref, wqkv_ref, wo_ref, win_ref, wout_ref, *refs):
    out_ref, home_ref, g_ref = refs[:3]
    rest = refs[3:11]
    sum_ref = rest[7]
    qkv_ref, pt_ref, gland, dx1_ref, glocal, gsend, grecv, xlocal, xsend, xrecv = refs[11:]
    step = pl.program_id(0)
    blocks, frames, part, width = gland.shape
    rows = frames * part
    clips, per, places, _ = cot_ref.shape
    chunks = blocks // clips
    mine = places // 4
    z = lax.axis_index("seq")
    peers = partners()

    def swap_in(b):
        clip, chunk = b // chunks, b % chunks
        return Swap(
            peers, lambda to: cot_ref.at[clip, :, rows_at(to * mine + chunk * part, part)],
            gland.at[b, pl.ds(z * per, per)], glocal.at[b], gsend.at[b], grecv.at[b],
        )

    def swap_out(b):
        clip, chunk = b // chunks, b % chunks
        return Swap(
            peers, lambda to: dx1_ref.at[b, pl.ds(to * per, per)],
            home_ref.at[clip, :, rows_at(z * mine + chunk * part, part)], xlocal.at[b], xsend.at[b], xrecv.at[b],
        )

    @pl.when(step == 0)
    def _():
        sum_ref[...] = jnp.zeros_like(sum_ref)
        enter({k: v for k, v in peers.items() if k[0] == "z"})

        def begin(b, _):
            swap_in(b).start()
            return 0

        lax.fori_loop(0, blocks, begin, 0)

    swap_in(step).arrive()
    g16 = gland[step].reshape(rows, width)
    g_ref[...] = g16
    x1 = x1_ref[0].reshape(rows, width).astype(F32)
    out, dx1 = place_rows(x1, g16, part, vec_ref, wqkv_ref, wo_ref, win_ref, wout_ref, *rest, qkv_ref, pt_ref)
    out_ref[0] = out.reshape(frames, part, width)
    dx1_ref[step] = dx1.reshape(frames, part, width)
    swap_out(step).start()

    @pl.when(step == blocks - 1)
    def _():
        def finish(b, _):
            swap_in(b).drain()
            swap_out(b).arrive()
            swap_out(b).drain()
            return 0

        lax.fori_loop(0, blocks, finish, 0)


def middle(x1, cot, vec, wqkv, wo, win, wout):
    clips, frames, mine, width = x1.shape
    rows = 256
    part = rows // frames
    per = mine // part
    blocks = clips * per
    tok = blocks * rows
    ff = win.shape[1]
    dma = pltpu.SemaphoreType.DMA
    n = rows_spec(rows, width)
    return pl.pallas_call(
        middle_kernel,
        grid=(blocks,),
        in_specs=[pl.BlockSpec((1, frames, part, width), lambda b: (b // per, 0, b % per, 0)), ANYWHERE]
        + [whole(w.shape) for w in (vec, wqkv, wo, win, wout)],
        out_specs=[
            pl.BlockSpec((1, frames, part, width), lambda b: (b, 0, 0, 0)), ANYWHERE, n, n, rows_spec(rows, 3 * width), n, n,
            n, rows_spec(rows, ff), rows_spec(rows, ff), pl.BlockSpec((SUM_ROWS, 8, width), lambda b: (0, 0, 0)),
        ],
        out_shape=[
            sds(blocks, frames, part, width), sds(*cot.shape), sds(tok, width), sds(tok, width), sds(tok, 3 * width),
            sds(tok, width), sds(tok, width), sds(tok, width), sds(tok, ff), sds(tok, ff),
            sds(SUM_ROWS, 8, width, dtype=F32),
        ],
        scratch_shapes=[
            pltpu.VMEM((rows, 3 * width), BF16), pltpu.VMEM((HEADS // 2, 2 * rows, rows), BF16),
            pltpu.VMEM((blocks, frames, part, width), BF16), pltpu.VMEM((blocks, frames, part, width), BF16),
            dma((blocks,)), dma((blocks, 3)), dma((blocks, 3)), dma((blocks,)), dma((blocks, 3)), dma((blocks, 3)),
        ],
        compiler_params=params(1),
        name="middle",
    )(x1, cot, vec, wqkv, wo, win, wout)


class Scatter:
    def __init__(self, peers, unit, piece, core, first, second, zsend, zgot, out, send, recv):
        self.peers, self.unit, self.piece, self.core = peers, unit, piece, core
        self.first, self.second, self.zsend, self.zgot, self.out = first, second, zsend, zgot, out
        self.send, self.recv = send, recv
        self.rows = core.shape[1]

    def block(self, i, c):
        return rows_at((2 * i + c) * self.rows, self.rows)

    def copy(self, i):
        y, x, c, z = position()
        along_x = self.unit % 2 == 0
        if i < 4:
            src, dst, kind = self.piece.at[self.block(i, 1 - c)], self.core.at[i], "core"
        elif i < 6:
            k = i - 4
            src = self.core.at[2 * k + 1 - x] if along_x else self.core.at[2 * (1 - y) + k]
            dst, kind = self.first.at[k], "x" if along_x else "y"
        elif i == 6:
            src, dst = self.first.at[1 - y if along_x else 1 - x], self.second
            kind = "y" if along_x else "x"
        else:
            j = i - 6
            src, dst, kind = self.zsend.at[lax.rem(z + j, 4)], self.zgot.at[j - 1], f"z{j}"
        return pltpu.make_async_remote_copy(
            src_ref=src, dst_ref=dst, send_sem=self.send.at[i], recv_sem=self.recv.at[i], device_id=self.peers[kind],
            device_id_type=MESH,
        )

    def start(self, items):
        for i in items:
            self.copy(i).start()

    def arrive(self, items):
        for i in items:
            self.copy(i).wait_recv()

    def sent(self, items):
        for i in items:
            self.copy(i).wait_send()

    def step0(self):
        self.start(range(4))

    def step1(self):
        _, _, c, _ = position()
        self.arrive(range(4))

        def add(i, _):
            self.core[i] = (self.piece[self.block(i, c)].astype(F32) + self.core[i].astype(F32)).astype(BF16)
            return 0

        lax.fori_loop(0, 4, add, 0)
        self.start((4, 5))
        self.sent(range(4))

    def step2(self):
        y, x, _, _ = position()
        self.arrive((4, 5))
        for i in range(2):
            own = self.core[2 * i + x] if self.unit % 2 == 0 else self.core[2 * y + i]
            self.first[i] = (self.first[i].astype(F32) + own.astype(F32)).astype(BF16)
        self.start((6,))

    def step3(self):
        y, x, _, _ = position()
        self.arrive((6,))
        r = self.zsend.shape[1]
        total = self.first[y if self.unit % 2 == 0 else x].astype(F32) + self.second[...].astype(F32)
        for i in range(4):
            self.zsend[i] = total[i * r : (i + 1) * r].astype(BF16)
        self.start((7, 8, 9))

    def step4(self):
        self.arrive((7, 8, 9))
        total = self.zsend[lax.axis_index("seq")].astype(F32)
        for i in range(3):
            total = total + self.zgot[i].astype(F32)
        self.out[...] = total

    def drain(self):
        self.sent(range(4, 10))


PANELS, BLOCKS, UNITS, SLOTS = 12, 8, 16, 6
STEPS = PANELS + BLOCKS + UNITS - PANELS
AFTER_STEP = {
    3: ("0 0", "0 1", "0 2", "0 3"), 4: ("1 0", "1 1", "0 4"), 5: ("1 2", "1 3", "0 5"), 6: ("2 0", "2 1", "0 6"), 7: ("0 7",),
    8: ("2 2", "2 3", "3 0", "3 1", "1 4", "1 5", "0 8"), 9: ("4 0", "4 1", "0 9"),
    10: ("3 2", "3 3", "2 4", "2 5", "1 6", "1 7", "0 10"), 11: ("4 2", "4 3", "0 11"),
    12: ("3 4", "3 5", "2 6", "2 7", "1 8", "1 9"), 13: ("4 4", "4 5", "3 6", "3 7", "1 10", "1 11"),
    14: ("2 8", "2 9", "4 6", "4 7"), 16: ("3 8", "3 9", "2 10", "2 11"), 17: ("4 8", "4 9"), 18: ("3 10", "3 11"),
    19: ("4 10", "4 11"), 20: ("0 12",), 21: ("1 12", "0 13"), 22: ("1 13", "2 12", "0 14"), 23: ("2 13", "1 14", "0 15"),
}
TAIL = ("1 15", "3 12", "3 13", "2 14", "2 15", "4 12", "4 13", "3 14", "3 15", "4 14", "4 15")
OUT_AT = (0, 2, 5, 7, 10, 12, 14, 16)


def last_kernel(
    x_ref, g1_ref, qkv_ref, pt_ref, vec_ref, sums_ref, wqkv_ref, wo_ref, z_ref, g_ref, a3_ref, dh_ref, ot_ref, gt_ref, a2_ref,
    dp_ref, a1_ref, o_ref, g1_all, out_ref, dx_ref, sqkv_out, so_out, tqkv_out, to_out, win_out, wout_out, vec_out, home_ref,
    dps_ref, lbuf, rbuf, pieces, core, one, two, zsend, zgot, dpbuf, ssum, held, got, lsem, rsem, send, recv, vsend, vrecv,
    dpsem, olocal, osend, orecv,
):
    step = pl.program_id(0)
    z = lax.axis_index("seq")
    peers = partners()
    width = x_ref.shape[2]
    rows = core.shape[2]
    small = zsend.shape[2]
    blocks, frames, part, _ = out_ref.shape
    clips, per, places, _ = home_ref.shape
    chunks, mine = blocks // clips, places // 4
    vec = Sum(peers, held, got, vsend, vrecv)

    def columns(i):
        return pl.ds(pl.multiple_of(i * width, width), width)

    def out_of(u):
        if u < 4:
            return wout_out.at[pl.ds(u * small, small)]
        if u == 8:
            return to_out
        if u == 12:
            return so_out
        ref, i = (win_out, u - 4) if u < 8 else (tqkv_out, u - 9) if u < 12 else (sqkv_out, u - 13)
        return ref.at[:, pl.ds(i * width, width)]

    work = [
        Scatter(
            peers, u, pieces.at[u % SLOTS], core.at[u], one.at[u], two.at[u], zsend.at[u], zgot.at[u], out_of(u), send.at[u],
            recv.at[u],
        )
        for u in range(UNITS)
    ]

    def event(name):
        stage, u = name.split()
        getattr(work[int(u)], "step" + stage)()

    def swap(b):
        return Swap(
            peers, lambda to: out_ref.at[b, pl.ds(to * per, per)],
            home_ref.at[b // chunks, :, rows_at(z * mine + (b % chunks) * part, part)], olocal.at[b], osend.at[b], orecv.at[b],
        )

    def load(ref, at, buf, sem, slot):
        src = ref if at is None else ref.at[:, columns(at)]
        return pltpu.make_async_copy(src, buf.at[slot], sem.at[slot])

    def fetch(p, left, l_at, right, r_at):
        slot = lax.rem(p, 2)
        load(left, l_at, lbuf, lsem, slot).start()
        load(right, r_at, rbuf, rsem, slot).start()

    def fetch_panel(p):
        for least, most, left, right, which in (
            (0, 4, z_ref, g_ref, "l"), (4, 8, a3_ref, dh_ref, "r"), (8, 9, ot_ref, gt_ref, ""), (9, 12, a2_ref, dp_ref, "r"),
            (12, 13, o_ref, g1_all, ""), (13, 16, a1_ref, dps_ref, "r"),
        ):

            @pl.when((p >= least) & (p < most))
            def _():
                at = p - least
                fetch(p, left, at if which == "l" else None, right, at if which == "r" else None)

    def dp_out(b):
        return pltpu.make_async_copy(dpbuf.at[b % 2], dps_ref.at[rows_at(b * x_ref.shape[1], x_ref.shape[1])], dpsem.at[b % 2])

    is_block = (step >= PANELS) & (step < PANELS + BLOCKS)
    panel = jnp.where(step < PANELS, step, step - BLOCKS)

    @pl.when(step == 0)
    def _():
        ssum[...] = sums_ref[...]
        enter(peers)
        fetch_panel(step)

    for b, at in enumerate(OUT_AT):

        @pl.when(step == at)
        def _(b=b):
            swap(b).start()

    @pl.when((step < PANELS - 1) | (step >= PANELS + BLOCKS - 1) & (step < STEPS - 1))
    def _():
        fetch_panel(jnp.where(step < PANELS, step + 1, step + 1 - BLOCKS))

    @pl.when(jnp.logical_not(is_block))
    def _():
        slot = lax.rem(panel, 2)
        load(z_ref, 0, lbuf, lsem, slot).wait()
        load(z_ref, 0, rbuf, rsem, slot).wait()
        total = outer_sum(lbuf[slot], rbuf[slot])

        @pl.when(panel >= 4)
        def _():
            pieces[lax.rem(panel, SLOTS)] = total.astype(BF16)

        @pl.when(panel < 4)
        def _():
            cut = total.reshape(2, 4, 4, small, width)
            for d in range(2):
                for i in range(4):
                    both = jnp.concatenate([cut[d, k, i] for k in range(4)], axis=0)
                    pieces[i, rows_at((2 * panel + d) * rows, rows)] = both.astype(BF16)

    @pl.when(is_block)
    def _():
        b = step - PANELS

        @pl.when(b >= 2)
        def _():
            dp_out(b - 2).wait()

        dx_ref[0] = space_back_rows(
            x_ref[0].astype(F32), g1_ref[0], qkv_ref, pt_ref.at[0], vec_ref, wqkv_ref, wo_ref, dpbuf.at[lax.rem(b, 2)], ssum
        )
        dp_out(b).start()

    @pl.when(step == PANELS + BLOCKS - 1)
    def _():
        dp_out(step - PANELS - 1).wait()
        dp_out(step - PANELS).wait()
        held[0] = jnp.concatenate([jnp.sum(ssum[i], axis=0, keepdims=True) for i in range(SUM_ROWS)], axis=0)
        vec.start(0)

    for k, names in AFTER_STEP.items():

        @pl.when(step == k)
        def _(k=k, names=names):
            for name in names:
                event(name)
            if k >= PANELS + BLOCKS:
                level = k - PANELS - BLOCKS
                vec.finish(level)
                if level < 3:
                    vec.start(level + 1)

    @pl.when(step == STEPS - 1)
    def _():
        for name in TAIL:
            event(name)
        vec_out[...] = held[4]
        vec.drain()
        for w in work:
            w.drain()

        def finish(b, _):
            swap(b).arrive()
            swap(b).drain()
            return 0

        lax.fori_loop(0, blocks, finish, 0)


def last(x, g1, home, saved, vec, wqkv, wo, out, shapes):
    z, g, a3, dh, ot, gt, a2, dp, a1, o, qkv, pt, sums = saved
    blocks, rows, width = x.shape
    tok = blocks * rows
    dma = pltpu.SemaphoreType.DMA
    in_vmem = pl.BlockSpec(memory_space=pltpu.VMEM)

    def at(s):
        return jnp.minimum(jnp.maximum(s - PANELS, 0), BLOCKS - 1)

    seq = pl.BlockSpec((1, rows, width), lambda s: (at(s), 0, 0))
    small = width // 32
    result = pl.pallas_call(
        last_kernel,
        grid=(STEPS,),
        in_specs=[
            seq, seq, pl.BlockSpec((rows, 3 * width), lambda s: (at(s), 0)),
            pl.BlockSpec((1, HEADS // 2, 2 * rows, rows), lambda s: (at(s), 0, 0, 0)),
        ] + [whole(v.shape) for v in (vec, sums, wqkv, wo)] + [ANYWHERE] * 12,
        out_specs=[seq] + [in_vmem] * 7 + [ANYWHERE] * 2,
        out_shape=[sds(*x.shape)] + [sds(*s, dtype=F32) for s in shapes]
        + [sds(SUM_ROWS, width, dtype=F32), sds(*home), sds(tok, 3 * width)],
        scratch_shapes=[
            pltpu.VMEM((2, tok, width), BF16), pltpu.VMEM((2, tok, width), BF16), pltpu.VMEM((SLOTS, width, width), BF16),
            pltpu.VMEM((UNITS, 4, 4 * small, width), BF16), pltpu.VMEM((UNITS, 2, 4 * small, width), BF16),
            pltpu.VMEM((UNITS, 4 * small, width), BF16), pltpu.VMEM((UNITS, 4, small, width), BF16),
            pltpu.VMEM((UNITS, 3, small, width), BF16), pltpu.VMEM((2, rows, 3 * width), BF16),
            pltpu.VMEM((SUM_ROWS, 8, width), F32), pltpu.VMEM((5, SUM_ROWS, width), F32), pltpu.VMEM((6, SUM_ROWS, width), F32),
            dma((2,)), dma((2,)), dma((UNITS, 10)), dma((UNITS, 10)), dma((6,)), dma((6,)), dma((2,)), dma((blocks,)),
            dma((blocks, 3)), dma((blocks, 3)),
        ],
        compiler_params=params(2),
        name="last",
    )(x, g1, qkv, pt, vec, sums, wqkv, wo, z, g, a3, dh, ot, gt, a2, dp, a1, o, g1.reshape(tok, width), out)
    return result[0], result[1:7], result[7], result[8]


def ring_layer(inputs, cotangent, shards, vec):
    clips, frames, places, width = inputs.shape
    x = inputs.reshape(clips * frames, places, width)
    (a1, qkv, pt, o), x1, (wqkv, wo, tqkv, to, win, wout), vec = first(x, vec, shards, clips)
    out, g1, g, a2, dp, ot, gt, a3, z, dh, sums = middle(x1, cotangent, vec, tqkv, to, win, wout)
    saved = (z, g, a3, dh, ot, gt, a2, dp, a1, o, qkv, pt, sums)
    dx, grads, rows, output = last(
        x, g1.reshape(x.shape), inputs.shape, saved, vec, wqkv, wo, out, [s.shape for s in shards]
    )
    return output, dx.reshape(inputs.shape), grads, rows


def my_index():
    return lax.axis_index("dp") * lax.axis_size("seq") + lax.axis_index("seq")


def spread_vectors(shards, width):
    devices = lax.axis_size("dp") * lax.axis_size("seq")
    me = my_index()
    rows = []
    for items in (NARROW, WIDE, (LONG,)):
        part = jnp.stack([shards[i] for i in items]).astype(F32)
        size = part.shape[1]
        zero = jnp.zeros((len(items), devices * size), F32)
        rows.append(lax.dynamic_update_slice(zero, part, (0, me * size)).reshape(-1, width))
    rows = jnp.concatenate(rows)
    return jnp.pad(rows, ((0, VEC_ROWS - rows.shape[0]), (0, 0)))


def own_vectors(rows):
    devices = lax.axis_size("dp") * lax.axis_size("seq")
    me = my_index()
    out, at = {}, 0
    width = rows.shape[1]
    for items, height in ((NARROW, 1), (WIDE, 2), ((LONG,), 4)):
        block = rows[at : at + height * len(items)].reshape(len(items), height * width)
        size = height * width // devices
        part = lax.dynamic_slice(block, (0, me * size), (len(items), size))
        for k, item in enumerate(items):
            out[item] = part[k]
        at += height * len(items)
    return [out[i] for i in range(12)]


def on_device(
    ring, inputs, norm_one_gain, norm_one_shift, space_qkv, space_qv_bias, space_out, space_out_bias,
    norm_two_gain, norm_two_shift, time_qkv, time_qv_bias, time_out, time_out_bias,
    norm_three_gain, norm_three_shift, mlp_in, mlp_in_bias, mlp_out, mlp_out_bias, cotangent,
):
    width = inputs.shape[-1]
    vec = spread_vectors(
        (norm_one_gain, norm_one_shift, space_qv_bias, space_out_bias, norm_two_gain, norm_two_shift,
         time_qv_bias, time_out_bias, norm_three_gain, norm_three_shift, mlp_in_bias, mlp_out_bias), width
    )
    shards = (space_qkv, space_out, time_qkv, time_out, mlp_in, mlp_out)
    layer = ring_layer if ring else plain_layer
    output, dx, grads, rows = layer(inputs, cotangent, shards, vec)
    gsqkv, gso, gtqkv, gto, gin, gout = grads
    vecs = own_vectors(rows)
    return (
        output, dx, vecs[0], vecs[1], gsqkv, vecs[2], gso, vecs[3], vecs[4], vecs[5], gtqkv,
        vecs[6], gto, vecs[7], vecs[8], vecs[9], gin, vecs[10], gout, vecs[11],
    )


def solution(mesh):
    tokens = P("dp", "seq", None, None)
    vector, matrix = P(("dp", "seq")), P(("dp", "seq"), None)
    weights = (vector, vector, matrix, vector, matrix, vector) * 3
    ring = mesh.shape["dp"] == 8 and mesh.shape["seq"] == 4
    return jax.shard_map(
        functools.partial(on_device, ring),
        mesh=mesh,
        in_specs=(tokens,) + weights + (tokens,),
        out_specs=(tokens, tokens) + weights,
        check_vma=False,
    )
```

```python
import functools
import jax
import jax.numpy as jnp
from jax import lax
from jax.experimental import pallas as pl
from jax.experimental.pallas import tpu as pltpu
from jax.sharding import PartitionSpec as P

HEADS = 12
HD = 64
EPS = 1e-06
SCALE = 0.125
F32 = jnp.float32
BF16 = jnp.bfloat16
RSQRT2 = 0.7071067811865476
RSQRT2PI = 0.3989422804014327


def dot(a, b):
    return jnp.dot(a, b, preferred_element_type=F32)


def dot_nt(a, b):
    return lax.dot_general(a, b, (((1,), (1,)), ((), ())), preferred_element_type=F32)


def fold(rows):
    return jnp.sum(rows.reshape(rows.shape[0] // 8, 8, rows.shape[1]), axis=0)


def norm(rows):
    center = rows - jnp.mean(rows, axis=-1, keepdims=True)
    rstd = lax.rsqrt(jnp.mean(center * center, axis=-1, keepdims=True) + EPS)
    return center * rstd, rstd


def norm_back(du, hat, rstd, gain):
    e = du * gain
    return rstd * (
        e - jnp.mean(e, axis=-1, keepdims=True) - hat * jnp.mean(e * hat, axis=-1, keepdims=True)
    )


def split_heads(pair):
    low = lax.broadcasted_iota(jnp.int32, (1, 2 * HD), 1) < HD
    zero = jnp.zeros_like(pair)
    return jnp.concatenate([jnp.where(low, pair, zero), jnp.where(low, zero, pair)], axis=0)


def join_heads(both):
    n = both.shape[0] // 2
    low = lax.broadcasted_iota(jnp.int32, (1, 2 * HD), 1) < HD
    return jnp.where(low, both[:n], both[n:])


def by_head(left, right):
    n = right.shape[0] // 2
    top = dot(left[:HD], right[:n])
    bottom = dot(left[HD:], right[n:])
    return jnp.concatenate([top, bottom], axis=0)


def attend(qkv_ref, pt_ref, o_ref, period):
    width = HEADS * HD
    n = qkv_ref.shape[0]
    for pair in range(HEADS // 2):
        at = pair * 2 * HD
        q = qkv_ref[:, at : at + 2 * HD] * jnp.asarray(SCALE, BF16)
        k = qkv_ref[:, width + at : width + at + 2 * HD]
        v = qkv_ref[:, 2 * width + at : 2 * width + at + 2 * HD]
        s = dot_nt(split_heads(k), q)
        if period:
            keys = lax.broadcasted_iota(jnp.int32, s.shape, 0) % period
            queries = lax.broadcasted_iota(jnp.int32, s.shape, 1) % period
            s = jnp.where(keys == queries, s, -1e30)
        probs = []
        for half in (s[:n], s[n:]):
            e = jnp.exp(half - jnp.max(half, axis=0, keepdims=True))
            probs.append((e * (1.0 / jnp.sum(e, axis=0, keepdims=True))).astype(BF16))
        p = jnp.concatenate(probs, axis=0)
        pt_ref[pair] = p
        o_ref[:, at : at + 2 * HD] = by_head(v.T, p).astype(BF16).T


def attend_back(qkv_ref, pt_ref, do, dp_ref):
    width = HEADS * HD
    n = qkv_ref.shape[0]
    for pair in range(HEADS // 2):
        at = pair * 2 * HD
        q = qkv_ref[:, at : at + 2 * HD] * jnp.asarray(SCALE, BF16)
        k = qkv_ref[:, width + at : width + at + 2 * HD]
        v = qkv_ref[:, 2 * width + at : 2 * width + at + 2 * HD]
        g = do[:, at : at + 2 * HD]
        p = pt_ref[pair]
        dp = dot_nt(split_heads(v), g)
        wide = p.astype(F32)
        ds = []
        for sl in (slice(0, n), slice(n, 2 * n)):
            t = wide[sl] * dp[sl]
            ds.append((t - wide[sl] * jnp.sum(t, axis=0, keepdims=True)).astype(BF16))
        ds = jnp.concatenate(ds, axis=0)
        dp_ref[:, 2 * width + at : 2 * width + at + 2 * HD] = join_heads(dot(p, g)).astype(BF16)
        dp_ref[:, width + at : width + at + 2 * HD] = join_heads(dot(ds, q)).astype(BF16)
        dp_ref[:, at : at + 2 * HD] = (by_head(k.T, ds) * SCALE).astype(BF16).T


GAIN1, SHIFT1, BO1, GAIN2, SHIFT2, BO2, GAIN3, SHIFT3, BOUT, BQ1, BV1, BQ2, BV2, BIN = range(14)
NARROW = (0, 1, 3, 4, 5, 7, 8, 9, 11)
WIDE = (2, 6)
LONG = 10
VEC_ROWS = 32
SUM_ROWS = 24
VMEM_LIMIT = 61 * 2**20


def row(vec_ref, i):
    return vec_ref[i : i + 1]


def project(a, wqkv_ref, bq, bv, qkv_ref):
    width = a.shape[1]
    for i, bias in enumerate((bq, None, bv)):
        sl = slice(i * width, (i + 1) * width)
        part = dot(a, wqkv_ref[:, sl])
        qkv_ref[:, sl] = (part if bias is None else part + bias).astype(BF16)


def space_rows(x, vec_ref, wqkv_ref, wo_ref, a_ref, qkv_ref, pt_ref, o_ref):
    hat, _ = norm(x)
    a = (hat * row(vec_ref, GAIN1) + row(vec_ref, SHIFT1)).astype(BF16)
    a_ref[...] = a
    project(a, wqkv_ref, row(vec_ref, BQ1), row(vec_ref, BV1), qkv_ref)
    attend(qkv_ref, pt_ref, o_ref, 0)
    return (x + dot(o_ref[...], wo_ref[...]) + row(vec_ref, BO1)).astype(BF16)


def place_rows(
    x1, take_g, period, vec_ref, wqkv_ref, wo_ref, win_ref, wout_ref, a2_ref, dp_ref, o_ref, gt_ref, a3_ref, z_ref, dh_ref,
    sum_ref, qkv_ref, pt_ref,
):
    rows, width = x1.shape
    hat2, rstd2 = norm(x1)
    a2 = (hat2 * row(vec_ref, GAIN2) + row(vec_ref, SHIFT2)).astype(BF16)
    a2_ref[...] = a2
    project(a2, wqkv_ref, row(vec_ref, BQ2), row(vec_ref, BV2), qkv_ref)
    attend(qkv_ref, pt_ref, o_ref, period)
    t = (dot(o_ref[...], wo_ref[...]) + row(vec_ref, BO2)).astype(BF16).astype(F32)
    x2 = x1 + t
    hat3, rstd3 = norm(x2)
    a3 = (hat3 * row(vec_ref, GAIN3) + row(vec_ref, SHIFT3)).astype(BF16)
    a3_ref[...] = a3
    g16 = take_g()
    g = g16.astype(F32)
    sum_ref[BOUT] += fold(g)
    y = x2 + row(vec_ref, BOUT)
    da3 = jnp.zeros((rows, width), F32)
    for i in range(win_ref.shape[1] // width):
        sl = slice(i * width, (i + 1) * width)
        h = dot(a3, win_ref[:, sl]) + row(vec_ref, BIN + i)
        cdf = 0.5 + 0.5 * lax.erf(h * RSQRT2)
        z = (h * cdf).astype(BF16)
        z_ref[:, sl] = z
        y = y + dot(z, wout_ref[sl, :])
        dz = dot_nt(g16, wout_ref[sl, :])
        dh = (dz * (cdf + h * (RSQRT2PI * jnp.exp(-0.5 * h * h)))).astype(BF16)
        dh_ref[:, sl] = dh
        sum_ref[BIN + i] += fold(dh.astype(F32))
        da3 = da3 + dot_nt(dh, win_ref[:, sl])
    sum_ref[GAIN3] += fold(da3 * hat3)
    sum_ref[SHIFT3] += fold(da3)
    dx2 = g + norm_back(da3, hat3, rstd3, row(vec_ref, GAIN3))
    gt = dx2.astype(BF16)
    gt_ref[...] = gt
    sum_ref[BO2] += fold(gt.astype(F32))
    do = dot_nt(gt, wo_ref[...]).astype(BF16)
    attend_back(qkv_ref, pt_ref, do, dp_ref)
    sum_ref[BQ2] += fold(dp_ref[:, :width].astype(F32))
    sum_ref[BV2] += fold(dp_ref[:, 2 * width :].astype(F32))
    da2 = dot_nt(dp_ref[...], wqkv_ref[...]).astype(BF16).astype(F32)
    sum_ref[GAIN2] += fold(da2 * hat2)
    sum_ref[SHIFT2] += fold(da2)
    dx1 = dx2 + norm_back(da2, hat2, rstd2, row(vec_ref, GAIN2))
    return y.astype(BF16), dx1.astype(BF16)


def space_back_rows(x, g, qkv_ref, pt_ref, vec_ref, wqkv_ref, wo_ref, dp_ref, sum_ref):
    width = x.shape[1]
    sum_ref[BO1] += fold(g.astype(F32))
    do = dot_nt(g, wo_ref[...]).astype(BF16)
    attend_back(qkv_ref, pt_ref, do, dp_ref)
    sum_ref[BQ1] += fold(dp_ref[:, :width].astype(F32))
    sum_ref[BV1] += fold(dp_ref[:, 2 * width :].astype(F32))
    da = dot_nt(dp_ref[...], wqkv_ref[...])
    hat, rstd = norm(x)
    sum_ref[GAIN1] += fold(da * hat)
    sum_ref[SHIFT1] += fold(da)
    return (g.astype(F32) + norm_back(da, hat, rstd, row(vec_ref, GAIN1))).astype(BF16)


def params(collective=None):
    extra = {} if collective is None else {"collective_id": collective, "has_side_effects": True}
    return pltpu.CompilerParams(vmem_limit_bytes=VMEM_LIMIT, dimension_semantics=("arbitrary",), **extra)


def whole(shape):
    return pl.BlockSpec(shape, lambda b: (0,) * len(shape), pipeline_mode=pl.Buffered(1))


def rows_spec(rows, cols):
    return pl.BlockSpec((rows, cols), lambda b: (b, 0))


def sds(*shape, dtype=BF16):
    return jax.ShapeDtypeStruct(shape, dtype)


ANYWHERE = pl.BlockSpec(memory_space=pl.ANY)


def space_kernel(x_ref, vec_ref, wqkv_ref, wo_ref, x1_ref, a_ref, qkv_ref, pt_ref, o_ref):
    x1_ref[0] = space_rows(x_ref[0].astype(F32), vec_ref, wqkv_ref, wo_ref, a_ref, qkv_ref, pt_ref.at[0], o_ref)


def place_kernel(x1_ref, g_ref, vec_ref, wqkv_ref, wo_ref, win_ref, wout_ref, out_ref, dx1_ref, *rest):
    _, frames, places, width = x1_ref.shape
    rows = frames * places
    sum_ref = rest[7]

    @pl.when(pl.program_id(0) == 0)
    def _():
        sum_ref[...] = jnp.zeros_like(sum_ref)

    x1 = x1_ref[0].reshape(rows, width).astype(F32)

    def take_g():
        return g_ref[0].reshape(rows, width)

    out, dx1 = place_rows(x1, take_g, places, vec_ref, wqkv_ref, wo_ref, win_ref, wout_ref, *rest)
    out_ref[0] = out.reshape(frames, places, width)
    dx1_ref[0] = dx1.reshape(frames, places, width)


def space_back_kernel(x_ref, g_ref, qkv_ref, pt_ref, vec_ref, wqkv_ref, wo_ref, dx_ref, dp_ref, sum_ref):
    @pl.when(pl.program_id(0) == 0)
    def _():
        sum_ref[...] = jnp.zeros_like(sum_ref)

    dx_ref[0] = space_back_rows(
        x_ref[0].astype(F32), g_ref[0], qkv_ref, pt_ref.at[0], vec_ref, wqkv_ref, wo_ref, dp_ref, sum_ref
    )


def probs_spec(rows):
    return pl.BlockSpec((1, HEADS // 2, 2 * rows, rows), lambda b: (b, 0, 0, 0))


def space_fwd(x, vec, wqkv, wo):
    blocks, rows, width = x.shape
    tok = blocks * rows
    seq = pl.BlockSpec((1, rows, width), lambda b: (b, 0, 0))
    return pl.pallas_call(
        space_kernel,
        grid=(blocks,),
        in_specs=[seq, whole(vec.shape), whole(wqkv.shape), whole(wo.shape)],
        out_specs=[seq, rows_spec(rows, width), rows_spec(rows, 3 * width), probs_spec(rows), rows_spec(rows, width)],
        out_shape=[
            sds(*x.shape), sds(tok, width), sds(tok, 3 * width), sds(blocks, HEADS // 2, 2 * rows, rows), sds(tok, width)
        ],
        compiler_params=params(),
        name="space_fwd",
    )(x, vec, wqkv, wo)


def place_all(x1, g, vec, wqkv, wo, win, wout):
    clips, frames, places, width = x1.shape
    rows = 256
    part = rows // frames
    per = places // part
    blocks = clips * per
    tok = blocks * rows
    ff = win.shape[1]
    spec = pl.BlockSpec((1, frames, part, width), lambda b: (b // per, 0, b % per, 0))
    n = rows_spec(rows, width)
    return pl.pallas_call(
        place_kernel,
        grid=(blocks,),
        in_specs=[spec, spec] + [whole(w.shape) for w in (vec, wqkv, wo, win, wout)],
        out_specs=[
            spec, spec, n, rows_spec(rows, 3 * width), n, n, n, rows_spec(rows, ff), rows_spec(rows, ff),
            pl.BlockSpec((SUM_ROWS, 8, width), lambda b: (0, 0, 0)),
        ],
        out_shape=[
            sds(*x1.shape), sds(*x1.shape), sds(tok, width), sds(tok, 3 * width), sds(tok, width), sds(tok, width),
            sds(tok, width), sds(tok, ff), sds(tok, ff), sds(SUM_ROWS, 8, width, dtype=F32),
        ],
        scratch_shapes=[pltpu.VMEM((rows, 3 * width), BF16), pltpu.VMEM((HEADS // 2, 2 * rows, rows), BF16)],
        compiler_params=params(),
        name="place_all",
    )(x1, g, vec, wqkv, wo, win, wout)


def space_bwd(x, g, qkv, pt, vec, wqkv, wo):
    blocks, rows, width = x.shape
    tok = blocks * rows
    seq = pl.BlockSpec((1, rows, width), lambda b: (b, 0, 0))
    return pl.pallas_call(
        space_back_kernel,
        grid=(blocks,),
        in_specs=[
            seq, seq, rows_spec(rows, 3 * width), probs_spec(rows), whole(vec.shape), whole(wqkv.shape), whole(wo.shape)
        ],
        out_specs=[seq, rows_spec(rows, 3 * width), pl.BlockSpec((SUM_ROWS, 8, width), lambda b: (0, 0, 0))],
        out_shape=[sds(*x.shape), sds(tok, 3 * width), sds(SUM_ROWS, 8, width, dtype=F32)],
        compiler_params=params(),
        name="space_bwd",
    )(x, g, qkv, pt, vec, wqkv, wo)


def outer_sum(left, right):
    return lax.dot_general(left, right, (((0,), (0,)), ((), ())), preferred_element_type=F32)


def plain_layer(inputs, cotangent, shards, vec):
    clips, frames, places, width = inputs.shape

    def out_there(rows):
        return lax.all_to_all(rows, "seq", split_axis=2, concat_axis=1, tiled=True)

    def back_home(rows):
        return lax.all_to_all(rows, "seq", split_axis=1, concat_axis=2, tiled=True)

    wqkv, wo, tqkv, to, win, wout = [lax.all_gather(s, ("dp", "seq"), axis=0, tiled=True) for s in shards]
    vec = lax.psum(vec, ("dp", "seq"))
    x = inputs.reshape(clips * frames, places, width)
    cot = out_there(cotangent)
    x1, a1, qkv, pt, o = space_fwd(x, vec, wqkv, wo)
    x1 = out_there(x1.reshape(inputs.shape))
    out, dx1, a2, dp, ot, gt, a3, z, dh, sums = place_all(x1, cot, vec, tqkv, to, win, wout)
    output = back_home(out)
    g1 = back_home(dx1).reshape(x.shape)
    dx, dps, space_sums = space_bwd(x, g1, qkv, pt, vec, wqkv, wo)
    part = 256 // cot.shape[1]
    g = cot.reshape(clips, cot.shape[1], -1, part, width).transpose(0, 2, 1, 3, 4).reshape(-1, width)
    pairs = ((a1, dps), (o, g1.reshape(-1, width)), (a2, dp), (ot, gt), (a3, dh), (z, g))
    grads = []
    for left, right in pairs:
        part = lax.psum_scatter(outer_sum(left, right).astype(BF16), "dp", scatter_dimension=0, tiled=True)
        grads.append(lax.psum_scatter(part, "seq", scatter_dimension=0, tiled=True).astype(F32))
    return output, dx.reshape(inputs.shape), grads, lax.psum((sums + space_sums).sum(1), ("dp", "seq"))


MESH = pl.DeviceIdType.MESH


def position():
    d, z = lax.axis_index("dp"), lax.axis_index("seq")
    return d // 4, lax.rem(d // 2, 2), lax.rem(d, 2), z


def partner(z):
    return z + 1 - 2 * lax.rem(z, 2)


def partners():
    y, x, c, z = position()
    return {
        "x": (4 * y + 2 * (1 - x) + c, z),
        "y": (4 * (1 - y) + 2 * x + c, z),
        "core": (4 * y + 2 * x + 1 - c, z),
        "pair": (4 * y + 2 * x + c, partner(z)),
        "across": (4 * y + 2 * x + c, 3 - z),
        "z1": (4 * y + 2 * x + c, lax.rem(z + 1, 4)),
        "z2": (4 * y + 2 * x + c, lax.rem(z + 2, 4)),
        "z3": (4 * y + 2 * x + c, lax.rem(z + 3, 4)),
    }


def enter(peers):
    barrier = pltpu.get_barrier_semaphore()
    greeted = [peer for kind, peer in peers.items() if kind not in ("pair", "across")]
    for peer in greeted:
        pl.semaphore_signal(barrier, inc=1, device_id=peer, device_id_type=MESH)
    pl.semaphore_wait(barrier, len(greeted))


class Sum:
    def __init__(self, peers, held, got, send, recv):
        self.peers, self.held, self.got, self.send, self.recv = peers, held, got, send, recv

    def copy(self, i, kind, level):
        return pltpu.make_async_remote_copy(
            src_ref=self.held.at[level], dst_ref=self.got.at[i], send_sem=self.send.at[i], recv_sem=self.recv.at[i],
            device_id=self.peers[kind], device_id_type=MESH,
        )

    STAGES = ((("z1", 0), ("z2", 1), ("z3", 2)), (("x", 3),), (("y", 4),), (("core", 5),))

    def start(self, level):
        for kind, i in self.STAGES[level]:
            self.copy(i, kind, level).start()

    def finish(self, level):
        total = self.held[level].astype(F32)
        for kind, i in self.STAGES[level]:
            self.copy(i, kind, level).wait_recv()
            total = total + self.got[i].astype(F32)
        self.held[level + 1] = total.astype(self.held.dtype)

    def drain(self):
        for level, stage in enumerate(self.STAGES):
            for kind, i in stage:
                self.copy(i, kind, level).wait_send()


class Gather:
    def __init__(self, peers, direct, shard, zbuf, group, full, local, send, recv):
        self.peers, self.shard, self.zbuf, self.group, self.full = peers, shard, zbuf, group, full
        self.local, self.send, self.recv = local, send, recv
        self.direct = direct
        self.rows, self.cols = group.shape
        z = lax.axis_index("seq")
        self.inner = (z == 1) | (z == 2)

    def place(self, which, half):
        y, x, c, _ = position()
        y, x = {"own": (y, x), "x": (y, 1 - x), "y": (1 - y, x), "xy": (1 - y, 1 - x)}[which]
        rows = pl.ds(pl.multiple_of((4 * y + 2 * x + c) * self.rows, self.rows), self.rows)
        n = self.cols // 2
        return (rows, pl.ds(0, self.cols)) if half is None else (rows, pl.ds(half * n, n))

    PLAN = {
        5: ("own", 0, "x"), 6: ("own", 1, "y"), 7: ("own", 0, "y"), 8: ("x", 0, "y"), 9: ("own", 1, "x"), 10: ("y", 1, "x"),
        11: ("own", None, "core"), 12: ("x", 0, "core"), 13: ("y", 1, "core"), 14: ("y", 0, "core"), 15: ("xy", 0, "core"),
        16: ("x", 1, "core"), 17: ("xy", 1, "core"),
    }

    def copy(self, i):
        if i < 5:
            z = lax.axis_index("seq")
            if self.direct:
                return self.remote(self.shard, self.zbuf.at[z], i, ("z1", "z2", "z3")[i])
            whose = (z, z, partner(z), 3 - z, partner(3 - z))[i]
            dst = self.zbuf.at[whose]
            src = self.shard if i < 2 else dst
            kind = ("pair", "across", "across", "pair", "pair")[i]
        else:
            which, half, kind = self.PLAN[i]
            at = self.place(which, half)
            src = dst = self.full.at[at]
            if which == "own":
                src = self.group if half is None else self.group.at[:, pl.ds(half * (self.cols // 2), self.cols // 2)]
        return self.remote(src, dst, i, kind)

    def remote(self, src, dst, i, kind):
        return pltpu.make_async_remote_copy(
            src_ref=src, dst_ref=dst, send_sem=self.send.at[i], recv_sem=self.recv.at[i], device_id=self.peers[kind],
            device_id_type=MESH,
        )

    def own_in(self):
        return pltpu.make_async_copy(self.shard, self.zbuf.at[lax.axis_index("seq")], self.local.at[0])

    def own_out(self):
        return pltpu.make_async_copy(self.group, self.full.at[self.place("own", None)], self.local.at[1])

    def start(self, items):
        for i in items:
            self.copy(i).start()

    def arrive(self, items):
        for i in items:
            self.copy(i).wait_recv()

    def step0(self):
        self.own_in().start()
        if self.direct:
            self.start((0, 1, 2))
            return
        self.start((0,))

        @pl.when(self.inner)
        def _():
            self.start((1,))

    def stepa(self):
        self.arrive((0,))

        @pl.when(self.inner)
        def _():
            self.start((2,))

    def stepb(self):
        @pl.when(self.inner)
        def _():
            self.arrive((1,))
            self.start((3,))
            self.arrive((2,))
            self.start((4,))

    def step1(self):
        if self.direct:
            self.arrive((0, 1, 2))
        else:

            @pl.when(jnp.logical_not(self.inner))
            def _():
                self.arrive((3, 4))

        self.own_in().wait()
        self.group[...] = jnp.concatenate([self.zbuf[i].astype(F32) for i in range(4)], axis=0).astype(BF16)
        self.own_out().start()
        self.start((5, 6, 7, 9, 11))

    def step2(self):
        self.arrive((5, 6))
        self.start((8, 10, 12, 13))

    def step3(self):
        self.arrive((7, 9, 8, 10))
        self.start((14, 16, 15, 17))

    def step4(self):
        self.arrive((11, 12, 13, 14, 16, 15, 17))
        self.own_out().wait()

    def drain(self):
        for i in (*range(3 if self.direct else 1), *range(5, 18)):
            self.copy(i).wait_send()
        if self.direct:
            return

        @pl.when(self.inner)
        def _():
            for i in range(1, 5):
                self.copy(i).wait_send()


class Swap:
    def __init__(self, peers, pick, land, local, send, recv):
        self.peers, self.pick, self.land, self.local, self.send, self.recv = peers, pick, land, local, send, recv

    def copies(self):
        z = lax.axis_index("seq")
        for j in range(3):
            yield pltpu.make_async_remote_copy(
                src_ref=self.pick(lax.rem(z + j + 1, 4)), dst_ref=self.land, send_sem=self.send.at[j], recv_sem=self.recv.at[j],
                device_id=self.peers[f"z{j + 1}"], device_id_type=MESH,
            )

    def own(self):
        return pltpu.make_async_copy(self.pick(lax.axis_index("seq")), self.land, self.local)

    def start(self):
        for copy in self.copies():
            copy.start()
        self.own().start()

    def arrive(self):
        for copy in self.copies():
            copy.wait_recv()
        self.own().wait()

    def drain(self):
        for copy in self.copies():
            copy.wait_send()


def rows_at(start, size):
    return pl.ds(pl.multiple_of(start, size), size)


GATHERED = ((0, 0), (0, 1), (0, 2), (1, 0), (2, 0), (2, 1), (2, 2), (3, 0), (4, 0), (4, 1), (4, 2), (4, 3), (5, 0))
BEFORE = {
    0: ("0 0", "0 1", "0 2", "0 3", "1 0", "1 1", "0 4", "0 5", "2 0", "0 6", "1 2", "0 7", "0 8", "0 9", "2 1", "a 4", "1 3", "a 5", "a 6", "a 7", "3 0", "a 8", "2 2", "a 9", "0 10", "4 0", "0 11", "0 12", "3 1", "b 4", "2 3", "b 5", "b 6", "a 10", "4 1", "b 7", "a 11", "3 2", "b 8", "a 12", "3 3", "1 4", "b 9", "4 2", "4 3"),
    1: ("2 4", "1 5", "b 10", "b 11", "b 12"),
    2: ("3 4", "1 6", "2 5"),
    3: ("4 4", "2 6", "1 7"),
    4: ("3 5", "3 6", "1 8"),
    5: ("4 5", "4 6", "2 7", "2 8"),
    6: ("3 7", "1 9"),
    7: ("4 7", "3 8", "2 9", "1 10"),
}
AFTER = ("1 11", "1 12", "4 8", "3 9", "2 10", "2 11", "4 9", "2 12", "3 10", "3 11", "4 10", "4 11", "3 12", "4 12")
VEC_AT = ("1 0", "1 2", "2 1", "3 1")


def first_kernel(x_ref, vec_ref, *refs):
    shards = refs[:6]
    a_ref, qkv_ref, pt_ref, o_ref, land_ref = refs[6:11]
    fulls, vec_out = refs[11:17], refs[17]
    wqkv_ref, wo_ref, x1_ref = refs[18:21]
    count = len(GATHERED)
    zbufs, groups = refs[21 : 21 + count], refs[21 + count : 21 + 2 * count]
    held, got, local, send, recv, vsend, vrecv, keep, xlocal, xsend, xrecv = refs[21 + 2 * count :]
    step = pl.program_id(0)
    blocks, rows, width = x1_ref.shape
    per = land_ref.shape[1] // 4
    part = rows // 4
    z = lax.axis_index("seq")
    peers = partners()
    vec = Sum(peers, held, got, vsend, vrecv)
    homes = (wqkv_ref, wo_ref) + tuple(fulls[2:])

    def piece(u):
        w, at = GATHERED[u]
        return (ref.at[:, pl.ds(at * width, width)] for ref in (shards[w], homes[w]))

    work = []
    for u in range(count):
        shard, full = piece(u)
        work.append(Gather(peers, u < 4, shard, zbufs[u], groups[u], full, local.at[u], send.at[u], recv.at[u]))

    def swap(b):
        return Swap(
            peers, lambda to: x1_ref.at[b, rows_at(to * part, part)], land_ref.at[b // per, z * per + lax.rem(b, per)],
            xlocal.at[b], xsend.at[b], xrecv.at[b],
        )

    def kept(i):
        return pltpu.make_async_copy(homes[i], fulls[i], keep.at[i])

    def event(name):
        stage, i = name.split()
        getattr(work[int(i)], "step" + stage)()

    @pl.when(step == 0)
    def _():
        held[0] = vec_ref[...]
        enter(peers)
        vec.start(0)
        for k, name in enumerate(BEFORE[0]):
            event(name)
            if name in VEC_AT:
                level = VEC_AT.index(name)
                vec.finish(level)
                if level < 3:
                    vec.start(level + 1)
        vec_out[...] = held[4].astype(F32)
        kept(0).start()
        kept(1).start()

    for k in range(1, 8):

        @pl.when(step == k)
        def _(k=k):
            for name in BEFORE[k]:
                event(name)

    x1_ref[step] = space_rows(
        x_ref[0].astype(F32), vec_out, wqkv_ref, wo_ref, a_ref, qkv_ref, pt_ref.at[0], o_ref
    )
    swap(step).start()

    @pl.when(step == blocks - 1)
    def _():
        for name in AFTER:
            event(name)
        kept(0).wait()
        kept(1).wait()
        vec.drain()
        for w in work:
            w.drain()

        def finish(b, _):
            swap(b).arrive()
            swap(b).drain()
            return 0

        lax.fori_loop(0, blocks, finish, 0)


def first(x, vec, shards, clips):
    blocks, rows, width = x.shape
    tok = blocks * rows
    frames = blocks // clips
    count = len(GATHERED)
    dma = pltpu.SemaphoreType.DMA
    seq = pl.BlockSpec((1, rows, width), lambda b: (b, 0, 0))
    fixed = pl.BlockSpec((VEC_ROWS, width), lambda b: (0, 0))
    out = pl.pallas_call(
        first_kernel,
        grid=(blocks,),
        in_specs=[seq, whole(vec.shape)] + [ANYWHERE] * 6,
        out_specs=[rows_spec(rows, width), rows_spec(rows, 3 * width), probs_spec(rows), rows_spec(rows, width), ANYWHERE]
        + [ANYWHERE] * 6 + [fixed],
        out_shape=[
            sds(tok, width), sds(tok, 3 * width), sds(blocks, HEADS // 2, 2 * rows, rows), sds(tok, width),
            sds(clips, 4 * frames, rows // 4, width),
        ] + [sds(32 * s.shape[0], s.shape[1]) for s in shards] + [sds(VEC_ROWS, width, dtype=F32)],
        scratch_shapes=[
            pltpu.VMEM((width, 3 * width), BF16), pltpu.VMEM((width, width), BF16), pltpu.VMEM((blocks, rows, width), BF16)
        ]
        + [pltpu.VMEM((4, shards[w].shape[0], width), BF16) for w, _ in GATHERED]
        + [pltpu.VMEM((4 * shards[w].shape[0], width), BF16) for w, _ in GATHERED]
        + [
            pltpu.VMEM((5, *vec.shape), BF16), pltpu.VMEM((6, *vec.shape), BF16), dma((count, 2)), dma((count, 18)),
            dma((count, 18)),
            dma((6,)), dma((6,)), dma((2,)), dma((blocks,)), dma((blocks, 3)), dma((blocks, 3)),
        ],
        compiler_params=params(0),
        name="first",
    )(x, vec.astype(BF16), *shards)
    return out[:4], out[4], out[5:11], out[11]


def middle_kernel(x1_ref, cot_ref, vec_ref, wqkv_ref, wo_ref, win_ref, wout_ref, *refs):
    out_ref, home_ref, rest_ref, g_ref = refs[:4]
    rest = refs[4:12]
    sum_ref = rest[7]
    qkv_ref, pt_ref, gland, dx1_ref, glocal, gsend, grecv, xlocal, xsend, xrecv = refs[12:]
    step = pl.program_id(0)
    blocks, frames, part, width = gland.shape
    rows = frames * part
    clips, per, places, _ = cot_ref.shape
    chunks = blocks // clips
    mine = places // 4
    z = lax.axis_index("seq")
    peers = partners()

    def swap_in(b):
        clip, chunk = b // chunks, b % chunks
        return Swap(
            peers, lambda to: cot_ref.at[clip, :, rows_at(to * mine + chunk * part, part)],
            gland.at[b, pl.ds(z * per, per)], glocal.at[b], gsend.at[b], grecv.at[b],
        )

    def swap_out(b):
        clip, chunk = b // chunks, b % chunks
        return Swap(
            peers, lambda to: dx1_ref.at[b, pl.ds(to * per, per)],
            home_ref.at[clip, :, rows_at(z * mine + chunk * part, part)], xlocal.at[b], xsend.at[b], xrecv.at[b],
        )

    @pl.when(step == 0)
    def _():
        sum_ref[...] = jnp.zeros_like(sum_ref)
        enter({k: v for k, v in peers.items() if k[0] == "z"})

        def begin(b, _):
            swap_in(b).start()
            return 0

        lax.fori_loop(0, blocks, begin, 0)

    def take_g():
        swap_in(step).arrive()
        g16 = gland[step].reshape(rows, width)
        g_ref[...] = g16
        return g16

    x1 = x1_ref[0].reshape(rows, width).astype(F32)
    out, dx1 = place_rows(x1, take_g, part, vec_ref, wqkv_ref, wo_ref, win_ref, wout_ref, *rest, qkv_ref, pt_ref)
    out_ref[0] = out.reshape(frames, part, width)
    dx1_ref[step] = dx1.reshape(frames, part, width)

    @pl.when(step < blocks - 1)
    def _():
        swap_out(step).start()

    @pl.when(step == blocks - 1)
    def _():
        rest_out = pltpu.make_async_copy(dx1_ref.at[blocks - 1], rest_ref, xlocal.at[blocks - 1])
        rest_out.start()

        def finish(b, _):
            swap_in(b).drain()
            swap_out(b).arrive()
            swap_out(b).drain()
            return 0

        lax.fori_loop(0, blocks - 1, finish, 0)
        swap_in(blocks - 1).drain()
        rest_out.wait()


def middle(x1, cot, vec, wqkv, wo, win, wout):
    clips, frames, mine, width = x1.shape
    rows = 256
    part = rows // frames
    per = mine // part
    blocks = clips * per
    tok = blocks * rows
    ff = win.shape[1]
    dma = pltpu.SemaphoreType.DMA
    n = rows_spec(rows, width)
    return pl.pallas_call(
        middle_kernel,
        grid=(blocks,),
        in_specs=[pl.BlockSpec((1, frames, part, width), lambda b: (b // per, 0, b % per, 0)), ANYWHERE]
        + [whole(w.shape) for w in (vec, wqkv, wo, win, wout)],
        out_specs=[
            pl.BlockSpec((1, frames, part, width), lambda b: (b, 0, 0, 0)), ANYWHERE, ANYWHERE, n, n,
            rows_spec(rows, 3 * width), n, n, n, rows_spec(rows, ff), rows_spec(rows, ff), pl.BlockSpec((SUM_ROWS, 8, width), lambda b: (0, 0, 0)),
        ],
        out_shape=[
            sds(blocks, frames, part, width), sds(*cot.shape), sds(frames, part, width), sds(tok, width), sds(tok, width), sds(tok, 3 * width),
            sds(tok, width), sds(tok, width), sds(tok, width), sds(tok, ff), sds(tok, ff),
            sds(SUM_ROWS, 8, width, dtype=F32),
        ],
        scratch_shapes=[
            pltpu.VMEM((rows, 3 * width), BF16), pltpu.VMEM((HEADS // 2, 2 * rows, rows), BF16),
            pltpu.VMEM((blocks, frames, part, width), BF16), pltpu.VMEM((blocks, frames, part, width), BF16),
            dma((blocks,)), dma((blocks, 3)), dma((blocks, 3)), dma((blocks,)), dma((blocks, 3)), dma((blocks, 3)),
        ],
        compiler_params=params(1),
        name="middle",
    )(x1, cot, vec, wqkv, wo, win, wout)


class Scatter:
    def __init__(self, peers, direct, piece, core, first, second, zsend, zgot, out, send, recv):
        self.peers, self.piece, self.core = peers, piece, core
        self.first, self.second, self.zsend, self.zgot, self.out = first, second, zsend, zgot, out
        self.send, self.recv = send, recv
        self.direct = direct
        z = lax.axis_index("seq")
        self.inner = (z == 1) | (z == 2)
        self.rows, self.half = core.shape[1], core.shape[2] // 2

    def block(self, i, c):
        return rows_at((2 * i + c) * self.rows, self.rows)

    def copy(self, i):
        y, x, c, z = position()
        if i < 4:
            src, dst, kind = self.piece.at[self.block(i, 1 - c)], self.core.at[i], "core"
        elif i < 6:
            src, dst, kind = self.core.at[2 * (i - 4) + 1 - x, :, pl.ds(0, self.half)], self.first.at[0, i - 4], "x"
        elif i < 8:
            src, dst, kind = self.core.at[2 * (1 - y) + i - 6, :, pl.ds(self.half, self.half)], self.first.at[1, i - 6], "y"
        elif i == 8:
            src, dst, kind = self.first.at[0, 1 - y], self.second.at[0], "y"
        elif i == 9:
            src, dst, kind = self.first.at[1, 1 - x], self.second.at[1], "x"
        elif self.direct:
            j = i - 9
            src, dst, kind = self.zsend.at[lax.rem(z + j, 4)], self.zgot.at[j - 1], f"z{j}"
        else:
            near, far = partner(z), 3 - partner(z)
            whose = (near, far, partner(far), 3 - z, partner(3 - z), near)[i - 10]
            src, dst = self.zsend.at[whose], self.zgot.at[(0, 1, 2, 3, 4, 0)[i - 10]]
            kind = "across" if i in (13, 14) else "pair"
        return pltpu.make_async_remote_copy(
            src_ref=src, dst_ref=dst, send_sem=self.send.at[i], recv_sem=self.recv.at[i], device_id=self.peers[kind],
            device_id_type=MESH,
        )

    def start(self, items):
        for i in items:
            self.copy(i).start()

    def arrive(self, items):
        for i in items:
            self.copy(i).wait_recv()

    def sent(self, items):
        for i in items:
            self.copy(i).wait_send()

    def step0(self):
        self.start(range(4))

    def step1(self):
        _, _, c, _ = position()
        self.arrive(range(4))

        def add(i, _):
            self.core[i] = self.piece[self.block(i, c)] + self.core[i]
            return 0

        lax.fori_loop(0, 4, add, 0)
        self.start(range(4, 8))
        self.sent(range(4))

    def step2(self):
        y, x, _, _ = position()
        n = self.half
        self.arrive(range(4, 8))
        for i in range(2):
            self.first[0, i] = self.first[0, i] + self.core[2 * i + x, :, :n]
            self.first[1, i] = self.first[1, i] + self.core[2 * y + i, :, n:]
        self.start((8, 9))

    def step3(self):
        y, x, _, _ = position()
        self.arrive((8, 9))
        r = self.zsend.shape[1]
        for k, at in ((0, y), (1, x)):
            total = self.first[k, at].astype(F32) + self.second[k].astype(F32)
            for i in range(4):
                self.zsend[i, :, k * self.half : (k + 1) * self.half] = total[i * r : (i + 1) * r].astype(BF16)
        if self.direct:
            self.start((10, 11, 12))
            return

        @pl.when(jnp.logical_not(self.inner))
        def _():
            self.start((10, 11, 12))

    def stepb(self):
        @pl.when(self.inner)
        def _():
            z = lax.axis_index("seq")
            self.arrive((10, 11, 12))
            for whose, i in ((3 - z, 1), (partner(3 - z), 2)):
                self.zsend[whose] = self.zsend[whose] + self.zgot[i]
            self.start((13, 14))

    def stepc(self):
        @pl.when(self.inner)
        def _():
            z = lax.axis_index("seq")
            self.arrive((13, 14))
            near = partner(z)
            self.zsend[near] = self.zsend[near] + self.zgot[4]
            self.start((15,))

    def step4(self):
        z = lax.axis_index("seq")
        if self.direct:
            self.arrive((10, 11, 12))
            total = self.zsend[z].astype(F32)
            for i in range(3):
                total = total + self.zgot[i].astype(F32)
            self.out[...] = total
            self.sent((10, 11, 12))
            return

        @pl.when(self.inner)
        def _():
            self.out[...] = self.zsend[z].astype(F32) + self.zgot[0].astype(F32) + self.zgot[3].astype(F32)
            self.sent((13, 14, 15))

        @pl.when(jnp.logical_not(self.inner))
        def _():
            self.arrive((15,))
            self.out[...] = self.zsend[z].astype(F32) + self.zgot[0].astype(F32)
            self.sent((10, 11, 12))

    def drain(self):
        self.sent(range(4, 10))


PANELS, BLOCKS, UNITS, SLOTS = 11, 8, 16, 6
CHAINED = 12
STEPS = PANELS + BLOCKS + UNITS - PANELS
AFTER_STEP = {
    3: ("0 0", "0 1", "0 2", "0 3"),
    4: ("0 4",),
    5: ("0 5", "1 0", "1 1"),
    6: ("0 6", "1 2"),
    7: ("0 7", "1 3", "1 4", "2 0"),
    8: ("0 8", "2 1"),
    9: ("0 9", "2 2", "1 5"),
    10: ("0 10", "2 3", "2 4"),
    11: ("1 6", "1 7", "3 0", "3 1", "3 2"),
    12: ("2 5", "1 8", "1 9", "3 3", "3 4", "2 6", "b 0"),
    13: ("2 7", "1 10", "b 1", "b 2", "3 5"),
    14: ("2 8", "2 9", "c 0", "3 6"),
    15: ("2 10", "b 3", "b 4", "c 1", "3 7"),
    16: ("c 2",),
    17: ("b 5",),
    18: ("b 6", "4 0", "3 8"),
    19: ("0 11", "c 3", "c 4"),
    20: ("0 12", "b 7", "c 5", "c 6", "4 1", "1 11", "3 9"),
    21: ("0 13", "1 12", "b 8", "c 7", "4 2", "3 10"),
    22: ("0 14", "2 11", "1 13", "b 9", "c 8", "4 3", "4 4", "4 5", "4 6", "2 12", "b 10"),
    23: ("0 15", "1 14", "c 9", "3 11", "4 7", "c 10"),
}
TAIL = ("4 8", "2 13", "3 12", "1 15", "4 9", "b 11", "2 14", "4 10", "3 13", "4 12", "c 11", "2 15", "3 14", "4 11", "4 13", "3 15", "4 14", "4 15")
OUT_AT = (0, 3, 6, 9, 12, 13, 14, 15)


def last_kernel(
    x_ref, g1_ref, qkv_ref, pt_ref, vec_ref, sums_ref, wqkv_ref, wo_ref, z_ref, g_ref, a3_ref, dh_ref, ot_ref, gt_ref, a2_ref,
    dp_ref, a1_ref, o_ref, rest_ref, out_ref, dx_ref, sqkv_out, so_out, tqkv_out, to_out, win_out, wout_out, vec_out, home_ref,
    dps_ref, g1_all, lbuf, rbuf, pieces, core, one, two, zsend, zgot, dpbuf, gbuf, gland, ssum, held, got, lsem, rsem, send, recv, vsend, vrecv,
    dpsem, gsem, olocal, osend, orecv, rlocal, rsend, rrecv,
):
    step = pl.program_id(0)
    z = lax.axis_index("seq")
    peers = partners()
    width = x_ref.shape[2]
    rows = core.shape[2]
    small = zsend.shape[2]
    blocks, frames, part, _ = out_ref.shape
    clips, per, places, _ = home_ref.shape
    chunks, mine = blocks // clips, places // 4
    vec = Sum(peers, held, got, vsend, vrecv)

    def columns(i):
        return pl.ds(pl.multiple_of(i * width, width), width)

    def out_of(u):
        if u < 4:
            return wout_out.at[pl.ds(u * small, small)]
        if u == 8:
            return to_out
        if u == 12:
            return so_out
        ref, i = (win_out, u - 4) if u < 8 else (tqkv_out, u - 9) if u < 12 else (sqkv_out, u - 13)
        return ref.at[:, pl.ds(i * width, width)]

    work = [
        Scatter(
            peers, u >= CHAINED, pieces.at[u % SLOTS], core.at[u], one.at[u], two.at[u], zsend.at[u % 8], zgot.at[u], out_of(u), send.at[u],
            recv.at[u],
        )
        for u in range(UNITS)
    ]

    def event(name):
        stage, u = name.split()
        getattr(work[int(u)], "step" + stage)()

    def swap(b):
        return Swap(
            peers, lambda to: out_ref.at[b, pl.ds(to * per, per)],
            home_ref.at[b // chunks, :, rows_at(z * mine + (b % chunks) * part, part)], olocal.at[b], osend.at[b], orecv.at[b],
        )

    rest = Swap(
        peers, lambda to: rest_ref.at[pl.ds(to * per, per)], gland.at[:, z], rlocal, rsend, rrecv,
    )

    def load(ref, at, buf, sem, slot):
        src = ref if at is None else ref.at[:, columns(at)]
        return pltpu.make_async_copy(src, buf.at[slot], sem.at[slot])

    def fetch(p, left, l_at, right, r_at):
        slot = lax.rem(p, 2)
        load(left, l_at, lbuf, lsem, slot).start()
        load(right, r_at, rbuf, rsem, slot).start()

    def fetch_panel(p):
        for least, most, left, right, which in (
            (0, 4, z_ref, g_ref, "l"), (4, 8, a3_ref, dh_ref, "r"), (8, 9, ot_ref, gt_ref, ""), (9, 12, a2_ref, dp_ref, "r"),
            (12, 13, o_ref, g1_all, ""), (13, 16, a1_ref, dps_ref, "r"),
        ):

            @pl.when((p >= least) & (p < most))
            def _():
                at = p - least
                fetch(p, left, at if which == "l" else None, right, at if which == "r" else None)

    def dp_out(b):
        return pltpu.make_async_copy(dpbuf.at[b % 2], dps_ref.at[rows_at(b * x_ref.shape[1], x_ref.shape[1])], dpsem.at[b % 2])

    def g1_out(b):
        return pltpu.make_async_copy(gbuf.at[b % 2], g1_all.at[rows_at(b * x_ref.shape[1], x_ref.shape[1])], gsem.at[b % 2])

    is_block = (step >= PANELS) & (step < PANELS + BLOCKS)
    panel = jnp.where(step < PANELS, step, step - BLOCKS)

    @pl.when(step == 0)
    def _():
        ssum[...] = sums_ref[...]
        fetch_panel(step)
        enter(peers)
        rest.start()

    for b, at in enumerate(OUT_AT):

        @pl.when(step == at)
        def _(b=b):
            swap(b).start()

    @pl.when((step < PANELS - 1) | (step >= PANELS + BLOCKS - 1) & (step < STEPS - 1))
    def _():
        fetch_panel(jnp.where(step < PANELS, step + 1, step + 1 - BLOCKS))

    @pl.when(jnp.logical_not(is_block))
    def _():
        slot = lax.rem(panel, 2)
        load(z_ref, 0, lbuf, lsem, slot).wait()
        load(z_ref, 0, rbuf, rsem, slot).wait()
        total = outer_sum(lbuf[slot], rbuf[slot])

        @pl.when(panel >= 4)
        def _():
            pieces[lax.rem(panel, SLOTS)] = total.astype(BF16)

        @pl.when(panel < 4)
        def _():
            cut = total.reshape(2, 4, 4, small, width)
            for d in range(2):
                for i in range(4):
                    both = jnp.concatenate([cut[d, k, i] for k in range(4)], axis=0)
                    pieces[i, rows_at((2 * panel + d) * rows, rows)] = both.astype(BF16)

    @pl.when(is_block)
    def _():
        b = step - PANELS

        @pl.when(b >= 2)
        def _():
            dp_out(b - 2).wait()
            g1_out(b - 2).wait()

        slot = lax.rem(b, 2)
        gbuf[slot] = g1_ref[0]

        @pl.when(b == BLOCKS - per)
        def _():
            rest.arrive()

        @pl.when(b >= BLOCKS - per)
        def _():
            for k in range(4):
                gbuf[slot, pl.ds(k * mine + mine - part, part)] = gland[b - (BLOCKS - per), k]

        g1_out(b).start()
        dx_ref[0] = space_back_rows(
            x_ref[0].astype(F32), gbuf[slot], qkv_ref, pt_ref.at[0], vec_ref, wqkv_ref, wo_ref, dpbuf.at[lax.rem(b, 2)], ssum
        )
        dp_out(b).start()

    @pl.when(step == PANELS + BLOCKS - 1)
    def _():
        dp_out(step - PANELS - 1).wait()
        dp_out(step - PANELS).wait()
        g1_out(step - PANELS - 1).wait()
        g1_out(step - PANELS).wait()
        held[0] = jnp.concatenate([jnp.sum(ssum[i], axis=0, keepdims=True) for i in range(SUM_ROWS)], axis=0)
        vec.start(0)

    for k, names in AFTER_STEP.items():

        @pl.when(step == k)
        def _(k=k, names=names):
            for name in names:
                event(name)
            if k >= PANELS + BLOCKS:
                level = k - PANELS - BLOCKS
                if level < 4:
                    vec.finish(level)
                if level < 3:
                    vec.start(level + 1)

    @pl.when(step == STEPS - 1)
    def _():
        for name in TAIL:
            event(name)
        vec_out[...] = held[4]
        vec.drain()
        rest.drain()
        for w in work:
            w.drain()

        def finish(b, _):
            swap(b).arrive()
            swap(b).drain()
            return 0

        lax.fori_loop(0, blocks, finish, 0)


def last(x, g1, rest, home, saved, vec, wqkv, wo, out, shapes):
    z, g, a3, dh, ot, gt, a2, dp, a1, o, qkv, pt, sums = saved
    blocks, rows, width = x.shape
    tok = blocks * rows
    dma = pltpu.SemaphoreType.DMA
    in_vmem = pl.BlockSpec(memory_space=pltpu.VMEM)

    def at(s):
        return jnp.minimum(jnp.maximum(s - PANELS, 0), BLOCKS - 1)

    seq = pl.BlockSpec((1, rows, width), lambda s: (at(s), 0, 0))
    small = width // 32
    result = pl.pallas_call(
        last_kernel,
        grid=(STEPS,),
        in_specs=[
            seq, seq, pl.BlockSpec((rows, 3 * width), lambda s: (at(s), 0)),
            pl.BlockSpec((1, HEADS // 2, 2 * rows, rows), lambda s: (at(s), 0, 0, 0)),
        ] + [whole(v.shape) for v in (vec, sums, wqkv, wo)] + [ANYWHERE] * 12,
        out_specs=[seq] + [in_vmem] * 7 + [ANYWHERE] * 3,
        out_shape=[sds(*x.shape)] + [sds(*s, dtype=F32) for s in shapes]
        + [sds(SUM_ROWS, width, dtype=F32), sds(*home), sds(tok, 3 * width), sds(tok, width)],
        scratch_shapes=[
            pltpu.VMEM((2, tok, width), BF16), pltpu.VMEM((2, tok, width), BF16), pltpu.VMEM((SLOTS, width, width), BF16),
            pltpu.VMEM((UNITS, 4, 4 * small, width), BF16),
            pltpu.VMEM((UNITS, 2, 2, 4 * small, width // 2), BF16), pltpu.VMEM((UNITS, 2, 4 * small, width // 2), BF16),
            pltpu.VMEM((8, 4, small, width), BF16),
            pltpu.VMEM((UNITS, 5, small, width), BF16), pltpu.VMEM((2, rows, 3 * width), BF16),
            pltpu.VMEM((2, rows, width), BF16), pltpu.VMEM((rest.shape[0] // 4, 4, *rest.shape[1:]), BF16),
            pltpu.VMEM((SUM_ROWS, 8, width), F32), pltpu.VMEM((5, SUM_ROWS, width), F32), pltpu.VMEM((6, SUM_ROWS, width), F32),
            dma((2,)), dma((2,)), dma((UNITS, 16)), dma((UNITS, 16)), dma((6,)), dma((6,)), dma((2,)), dma((2,)), dma((blocks,)),
            dma((blocks, 3)), dma((blocks, 3)), dma(()), dma((3,)), dma((3,)),
        ],
        compiler_params=params(2),
        name="last",
    )(x, g1, qkv, pt, vec, sums, wqkv, wo, z, g, a3, dh, ot, gt, a2, dp, a1, o, rest, out)
    return result[0], result[1:7], result[7], result[8]


def ring_layer(inputs, cotangent, shards, vec):
    clips, frames, places, width = inputs.shape
    x = inputs.reshape(clips * frames, places, width)
    (a1, qkv, pt, o), x1, (wqkv, wo, tqkv, to, win, wout), vec = first(x, vec, shards, clips)
    out, g1, rest, g, a2, dp, ot, gt, a3, z, dh, sums = middle(x1, cotangent, vec, tqkv, to, win, wout)
    saved = (z, g, a3, dh, ot, gt, a2, dp, a1, o, qkv, pt, sums)
    dx, grads, rows, output = last(
        x, g1.reshape(x.shape), rest, inputs.shape, saved, vec, wqkv, wo, out, [s.shape for s in shards]
    )
    return output, dx.reshape(inputs.shape), grads, rows


def my_index():
    return lax.axis_index("dp") * lax.axis_size("seq") + lax.axis_index("seq")


def spread_vectors(shards, width):
    devices = lax.axis_size("dp") * lax.axis_size("seq")
    me = my_index()
    rows = []
    for items in (NARROW, WIDE, (LONG,)):
        part = jnp.stack([shards[i] for i in items]).astype(F32)
        size = part.shape[1]
        zero = jnp.zeros((len(items), devices * size), F32)
        rows.append(lax.dynamic_update_slice(zero, part, (0, me * size)).reshape(-1, width))
    rows = jnp.concatenate(rows)
    return jnp.pad(rows, ((0, VEC_ROWS - rows.shape[0]), (0, 0)))


def own_vectors(rows):
    devices = lax.axis_size("dp") * lax.axis_size("seq")
    me = my_index()
    out, at = {}, 0
    width = rows.shape[1]
    for items, height in ((NARROW, 1), (WIDE, 2), ((LONG,), 4)):
        block = rows[at : at + height * len(items)].reshape(len(items), height * width)
        size = height * width // devices
        part = lax.dynamic_slice(block, (0, me * size), (len(items), size))
        for k, item in enumerate(items):
            out[item] = part[k]
        at += height * len(items)
    return [out[i] for i in range(12)]


def on_device(
    ring, inputs, norm_one_gain, norm_one_shift, space_qkv, space_qv_bias, space_out, space_out_bias,
    norm_two_gain, norm_two_shift, time_qkv, time_qv_bias, time_out, time_out_bias,
    norm_three_gain, norm_three_shift, mlp_in, mlp_in_bias, mlp_out, mlp_out_bias, cotangent,
):
    width = inputs.shape[-1]
    vec = spread_vectors(
        (norm_one_gain, norm_one_shift, space_qv_bias, space_out_bias, norm_two_gain, norm_two_shift,
         time_qv_bias, time_out_bias, norm_three_gain, norm_three_shift, mlp_in_bias, mlp_out_bias), width
    )
    shards = (space_qkv, space_out, time_qkv, time_out, mlp_in, mlp_out)
    layer = ring_layer if ring else plain_layer
    output, dx, grads, rows = layer(inputs, cotangent, shards, vec)
    gsqkv, gso, gtqkv, gto, gin, gout = grads
    vecs = own_vectors(rows)
    return (
        output, dx, vecs[0], vecs[1], gsqkv, vecs[2], gso, vecs[3], vecs[4], vecs[5], gtqkv,
        vecs[6], gto, vecs[7], vecs[8], vecs[9], gin, vecs[10], gout, vecs[11],
    )


def solution(mesh):
    tokens = P("dp", "seq", None, None)
    vector, matrix = P(("dp", "seq")), P(("dp", "seq"), None)
    weights = (vector, vector, matrix, vector, matrix, vector) * 3
    ring = mesh.shape["dp"] == 8 and mesh.shape["seq"] == 4
    return jax.shard_map(
        functools.partial(on_device, ring),
        mesh=mesh,
        in_specs=(tokens,) + weights + (tokens,),
        out_specs=(tokens, tokens) + weights,
        check_vma=False,
    )
```

```python
import functools
import jax
import jax.numpy as jnp
from jax import lax
from jax.experimental import pallas as pl
from jax.experimental.pallas import tpu as pltpu
from jax.sharding import PartitionSpec as P

HEADS = 12
HD = 64
EPS = 1e-06
SCALE = 0.125
F32 = jnp.float32
BF16 = jnp.bfloat16
RSQRT2 = 0.7071067811865476
RSQRT2PI = 0.3989422804014327


def dot(a, b):
    return jnp.dot(a, b, preferred_element_type=F32)


def dot_nt(a, b):
    return lax.dot_general(a, b, (((1,), (1,)), ((), ())), preferred_element_type=F32)


def fold(rows):
    return jnp.sum(rows.reshape(rows.shape[0] // 8, 8, rows.shape[1]), axis=0)


def norm(rows):
    center = rows - jnp.mean(rows, axis=-1, keepdims=True)
    rstd = lax.rsqrt(jnp.mean(center * center, axis=-1, keepdims=True) + EPS)
    return center * rstd, rstd


def norm_back(du, hat, rstd, gain):
    e = du * gain
    return rstd * (
        e - jnp.mean(e, axis=-1, keepdims=True) - hat * jnp.mean(e * hat, axis=-1, keepdims=True)
    )


def split_heads(pair):
    low = lax.broadcasted_iota(jnp.int32, (1, 2 * HD), 1) < HD
    zero = jnp.zeros_like(pair)
    return jnp.concatenate([jnp.where(low, pair, zero), jnp.where(low, zero, pair)], axis=0)


def join_heads(both):
    n = both.shape[0] // 2
    low = lax.broadcasted_iota(jnp.int32, (1, 2 * HD), 1) < HD
    return jnp.where(low, both[:n], both[n:])


def by_head(left, right):
    n = right.shape[0] // 2
    top = dot(left[:HD], right[:n])
    bottom = dot(left[HD:], right[n:])
    return jnp.concatenate([top, bottom], axis=0)


def attend(qkv_ref, pt_ref, o_ref, period):
    width = HEADS * HD
    n = qkv_ref.shape[0]
    for pair in range(HEADS // 2):
        at = pair * 2 * HD
        q = qkv_ref[:, at : at + 2 * HD] * jnp.asarray(SCALE, BF16)
        k = qkv_ref[:, width + at : width + at + 2 * HD]
        v = qkv_ref[:, 2 * width + at : 2 * width + at + 2 * HD]
        s = dot_nt(split_heads(k), q)
        if period:
            keys = lax.broadcasted_iota(jnp.int32, s.shape, 0) % period
            queries = lax.broadcasted_iota(jnp.int32, s.shape, 1) % period
            s = jnp.where(keys == queries, s, -1e30)
        probs = []
        for half in (s[:n], s[n:]):
            e = jnp.exp(half - jnp.max(half, axis=0, keepdims=True))
            probs.append((e * (1.0 / jnp.sum(e, axis=0, keepdims=True))).astype(BF16))
        p = jnp.concatenate(probs, axis=0)
        pt_ref[pair] = p
        o_ref[:, at : at + 2 * HD] = by_head(v.T, p).astype(BF16).T


def attend_back(qkv_ref, pt_ref, do, dp_ref):
    width = HEADS * HD
    n = qkv_ref.shape[0]
    for pair in range(HEADS // 2):
        at = pair * 2 * HD
        q = qkv_ref[:, at : at + 2 * HD] * jnp.asarray(SCALE, BF16)
        k = qkv_ref[:, width + at : width + at + 2 * HD]
        v = qkv_ref[:, 2 * width + at : 2 * width + at + 2 * HD]
        g = do[:, at : at + 2 * HD]
        p = pt_ref[pair]
        dp = dot_nt(split_heads(v), g)
        wide = p.astype(F32)
        ds = []
        for sl in (slice(0, n), slice(n, 2 * n)):
            t = wide[sl] * dp[sl]
            ds.append((t - wide[sl] * jnp.sum(t, axis=0, keepdims=True)).astype(BF16))
        ds = jnp.concatenate(ds, axis=0)
        dp_ref[:, 2 * width + at : 2 * width + at + 2 * HD] = join_heads(dot(p, g)).astype(BF16)
        dp_ref[:, width + at : width + at + 2 * HD] = join_heads(dot(ds, q)).astype(BF16)
        dp_ref[:, at : at + 2 * HD] = (by_head(k.T, ds) * SCALE).astype(BF16).T


GAIN1, SHIFT1, BO1, GAIN2, SHIFT2, BO2, GAIN3, SHIFT3, BOUT, BQ1, BV1, BQ2, BV2, BIN = range(14)
NARROW = (0, 1, 3, 4, 5, 7, 8, 9, 11)
WIDE = (2, 6)
LONG = 10
VEC_ROWS = 32
SUM_ROWS = 24
VMEM_LIMIT = 62 * 2**20


def row(vec_ref, i):
    return vec_ref[i : i + 1]


def project(a, wqkv_ref, bq, bv, qkv_ref):
    width = a.shape[1]
    for i, bias in enumerate((bq, None, bv)):
        sl = slice(i * width, (i + 1) * width)
        part = dot(a, wqkv_ref[:, sl])
        qkv_ref[:, sl] = (part if bias is None else part + bias).astype(BF16)


def space_rows(x, vec_ref, wqkv_ref, wo_ref, a_ref, qkv_ref, pt_ref, o_ref):
    hat, _ = norm(x)
    a = (hat * row(vec_ref, GAIN1) + row(vec_ref, SHIFT1)).astype(BF16)
    a_ref[...] = a
    project(a, wqkv_ref, row(vec_ref, BQ1), row(vec_ref, BV1), qkv_ref)
    attend(qkv_ref, pt_ref, o_ref, 0)
    return (x + dot(o_ref[...], wo_ref[...]) + row(vec_ref, BO1)).astype(BF16)


def place_rows(
    x1, take_g, midway, period, vec_ref, wqkv_ref, wo_ref, win_ref, wout_ref, a2_ref, dp_ref, o_ref, gt_ref, a3_ref, z_ref, dh_ref,
    sum_ref, qkv_ref, pt_ref,
):
    rows, width = x1.shape
    hat2, rstd2 = norm(x1)
    a2 = (hat2 * row(vec_ref, GAIN2) + row(vec_ref, SHIFT2)).astype(BF16)
    a2_ref[...] = a2
    project(a2, wqkv_ref, row(vec_ref, BQ2), row(vec_ref, BV2), qkv_ref)
    attend(qkv_ref, pt_ref, o_ref, period)
    t = (dot(o_ref[...], wo_ref[...]) + row(vec_ref, BO2)).astype(BF16).astype(F32)
    x2 = x1 + t
    hat3, rstd3 = norm(x2)
    a3 = (hat3 * row(vec_ref, GAIN3) + row(vec_ref, SHIFT3)).astype(BF16)
    a3_ref[...] = a3
    g16 = take_g()
    g = g16.astype(F32)
    sum_ref[BOUT] += fold(g)
    y = x2 + row(vec_ref, BOUT)
    da3 = jnp.zeros((rows, width), F32)
    for i in range(win_ref.shape[1] // width):
        sl = slice(i * width, (i + 1) * width)
        h = dot(a3, win_ref[:, sl]) + row(vec_ref, BIN + i)
        cdf = 0.5 + 0.5 * lax.erf(h * RSQRT2)
        z = (h * cdf).astype(BF16)
        z_ref[:, sl] = z
        y = y + dot(z, wout_ref[sl, :])
        dz = dot_nt(g16, wout_ref[sl, :])
        dh = (dz * (cdf + h * (RSQRT2PI * jnp.exp(-0.5 * h * h)))).astype(BF16)
        dh_ref[:, sl] = dh
        sum_ref[BIN + i] += fold(dh.astype(F32))
        da3 = da3 + dot_nt(dh, win_ref[:, sl])
        if i == 1:
            midway()
    sum_ref[GAIN3] += fold(da3 * hat3)
    sum_ref[SHIFT3] += fold(da3)
    dx2 = g + norm_back(da3, hat3, rstd3, row(vec_ref, GAIN3))
    gt = dx2.astype(BF16)
    gt_ref[...] = gt
    sum_ref[BO2] += fold(gt.astype(F32))
    do = dot_nt(gt, wo_ref[...]).astype(BF16)
    attend_back(qkv_ref, pt_ref, do, dp_ref)
    sum_ref[BQ2] += fold(dp_ref[:, :width].astype(F32))
    sum_ref[BV2] += fold(dp_ref[:, 2 * width :].astype(F32))
    da2 = dot_nt(dp_ref[...], wqkv_ref[...]).astype(BF16).astype(F32)
    sum_ref[GAIN2] += fold(da2 * hat2)
    sum_ref[SHIFT2] += fold(da2)
    dx1 = dx2 + norm_back(da2, hat2, rstd2, row(vec_ref, GAIN2))
    return y.astype(BF16), dx1.astype(BF16)


def space_back_rows(x, g, qkv_ref, pt_ref, vec_ref, wqkv_ref, wo_ref, dp_ref, sum_ref):
    width = x.shape[1]
    sum_ref[BO1] += fold(g.astype(F32))
    do = dot_nt(g, wo_ref[...]).astype(BF16)
    attend_back(qkv_ref, pt_ref, do, dp_ref)
    sum_ref[BQ1] += fold(dp_ref[:, :width].astype(F32))
    sum_ref[BV1] += fold(dp_ref[:, 2 * width :].astype(F32))
    da = dot_nt(dp_ref[...], wqkv_ref[...])
    hat, rstd = norm(x)
    sum_ref[GAIN1] += fold(da * hat)
    sum_ref[SHIFT1] += fold(da)
    return (g.astype(F32) + norm_back(da, hat, rstd, row(vec_ref, GAIN1))).astype(BF16)


def params(collective=None):
    extra = {} if collective is None else {"collective_id": collective, "has_side_effects": True}
    return pltpu.CompilerParams(vmem_limit_bytes=VMEM_LIMIT, dimension_semantics=("arbitrary",), **extra)


def whole(shape):
    return pl.BlockSpec(shape, lambda b: (0,) * len(shape), pipeline_mode=pl.Buffered(1))


def rows_spec(rows, cols):
    return pl.BlockSpec((rows, cols), lambda b: (b, 0))


def sds(*shape, dtype=BF16):
    return jax.ShapeDtypeStruct(shape, dtype)


ANYWHERE = pl.BlockSpec(memory_space=pl.ANY)


def space_kernel(x_ref, vec_ref, wqkv_ref, wo_ref, x1_ref, a_ref, qkv_ref, pt_ref, o_ref):
    x1_ref[0] = space_rows(x_ref[0].astype(F32), vec_ref, wqkv_ref, wo_ref, a_ref, qkv_ref, pt_ref.at[0], o_ref)


def place_kernel(x1_ref, g_ref, vec_ref, wqkv_ref, wo_ref, win_ref, wout_ref, out_ref, dx1_ref, *rest):
    _, frames, places, width = x1_ref.shape
    rows = frames * places
    sum_ref = rest[7]

    @pl.when(pl.program_id(0) == 0)
    def _():
        sum_ref[...] = jnp.zeros_like(sum_ref)

    x1 = x1_ref[0].reshape(rows, width).astype(F32)

    def take_g():
        return g_ref[0].reshape(rows, width)

    out, dx1 = place_rows(x1, take_g, lambda: None, places, vec_ref, wqkv_ref, wo_ref, win_ref, wout_ref, *rest)
    out_ref[0] = out.reshape(frames, places, width)
    dx1_ref[0] = dx1.reshape(frames, places, width)


def space_back_kernel(x_ref, g_ref, qkv_ref, pt_ref, vec_ref, wqkv_ref, wo_ref, dx_ref, dp_ref, sum_ref):
    @pl.when(pl.program_id(0) == 0)
    def _():
        sum_ref[...] = jnp.zeros_like(sum_ref)

    dx_ref[0] = space_back_rows(
        x_ref[0].astype(F32), g_ref[0], qkv_ref, pt_ref.at[0], vec_ref, wqkv_ref, wo_ref, dp_ref, sum_ref
    )


def probs_spec(rows):
    return pl.BlockSpec((1, HEADS // 2, 2 * rows, rows), lambda b: (b, 0, 0, 0))


def space_fwd(x, vec, wqkv, wo):
    blocks, rows, width = x.shape
    tok = blocks * rows
    seq = pl.BlockSpec((1, rows, width), lambda b: (b, 0, 0))
    return pl.pallas_call(
        space_kernel,
        grid=(blocks,),
        in_specs=[seq, whole(vec.shape), whole(wqkv.shape), whole(wo.shape)],
        out_specs=[seq, rows_spec(rows, width), rows_spec(rows, 3 * width), probs_spec(rows), rows_spec(rows, width)],
        out_shape=[
            sds(*x.shape), sds(tok, width), sds(tok, 3 * width), sds(blocks, HEADS // 2, 2 * rows, rows), sds(tok, width)
        ],
        compiler_params=params(),
        name="space_fwd",
    )(x, vec, wqkv, wo)


def place_all(x1, g, vec, wqkv, wo, win, wout):
    clips, frames, places, width = x1.shape
    rows = 256
    part = rows // frames
    per = places // part
    blocks = clips * per
    tok = blocks * rows
    ff = win.shape[1]
    spec = pl.BlockSpec((1, frames, part, width), lambda b: (b // per, 0, b % per, 0))
    n = rows_spec(rows, width)
    return pl.pallas_call(
        place_kernel,
        grid=(blocks,),
        in_specs=[spec, spec] + [whole(w.shape) for w in (vec, wqkv, wo, win, wout)],
        out_specs=[
            spec, spec, n, rows_spec(rows, 3 * width), n, n, n, rows_spec(rows, ff), rows_spec(rows, ff),
            pl.BlockSpec((SUM_ROWS, 8, width), lambda b: (0, 0, 0)),
        ],
        out_shape=[
            sds(*x1.shape), sds(*x1.shape), sds(tok, width), sds(tok, 3 * width), sds(tok, width), sds(tok, width),
            sds(tok, width), sds(tok, ff), sds(tok, ff), sds(SUM_ROWS, 8, width, dtype=F32),
        ],
        scratch_shapes=[pltpu.VMEM((rows, 3 * width), BF16), pltpu.VMEM((HEADS // 2, 2 * rows, rows), BF16)],
        compiler_params=params(),
        name="place_all",
    )(x1, g, vec, wqkv, wo, win, wout)


def space_bwd(x, g, qkv, pt, vec, wqkv, wo):
    blocks, rows, width = x.shape
    tok = blocks * rows
    seq = pl.BlockSpec((1, rows, width), lambda b: (b, 0, 0))
    return pl.pallas_call(
        space_back_kernel,
        grid=(blocks,),
        in_specs=[
            seq, seq, rows_spec(rows, 3 * width), probs_spec(rows), whole(vec.shape), whole(wqkv.shape), whole(wo.shape)
        ],
        out_specs=[seq, rows_spec(rows, 3 * width), pl.BlockSpec((SUM_ROWS, 8, width), lambda b: (0, 0, 0))],
        out_shape=[sds(*x.shape), sds(tok, 3 * width), sds(SUM_ROWS, 8, width, dtype=F32)],
        compiler_params=params(),
        name="space_bwd",
    )(x, g, qkv, pt, vec, wqkv, wo)


def outer_sum(left, right):
    return lax.dot_general(left, right, (((0,), (0,)), ((), ())), preferred_element_type=F32)


def plain_layer(inputs, cotangent, shards, vec):
    clips, frames, places, width = inputs.shape

    def out_there(rows):
        return lax.all_to_all(rows, "seq", split_axis=2, concat_axis=1, tiled=True)

    def back_home(rows):
        return lax.all_to_all(rows, "seq", split_axis=1, concat_axis=2, tiled=True)

    wqkv, wo, tqkv, to, win, wout = [lax.all_gather(s, ("dp", "seq"), axis=0, tiled=True) for s in shards]
    vec = lax.psum(vec, ("dp", "seq"))
    x = inputs.reshape(clips * frames, places, width)
    cot = out_there(cotangent)
    x1, a1, qkv, pt, o = space_fwd(x, vec, wqkv, wo)
    x1 = out_there(x1.reshape(inputs.shape))
    out, dx1, a2, dp, ot, gt, a3, z, dh, sums = place_all(x1, cot, vec, tqkv, to, win, wout)
    output = back_home(out)
    g1 = back_home(dx1).reshape(x.shape)
    dx, dps, space_sums = space_bwd(x, g1, qkv, pt, vec, wqkv, wo)
    part = 256 // cot.shape[1]
    g = cot.reshape(clips, cot.shape[1], -1, part, width).transpose(0, 2, 1, 3, 4).reshape(-1, width)
    pairs = ((a1, dps), (o, g1.reshape(-1, width)), (a2, dp), (ot, gt), (a3, dh), (z, g))
    grads = []
    for left, right in pairs:
        part = lax.psum_scatter(outer_sum(left, right).astype(BF16), "dp", scatter_dimension=0, tiled=True)
        grads.append(lax.psum_scatter(part, "seq", scatter_dimension=0, tiled=True).astype(F32))
    return output, dx.reshape(inputs.shape), grads, lax.psum((sums + space_sums).sum(1), ("dp", "seq"))


MESH = pl.DeviceIdType.MESH


def position():
    d, z = lax.axis_index("dp"), lax.axis_index("seq")
    return d // 4, lax.rem(d // 2, 2), lax.rem(d, 2), z


def partner(z):
    return z + 1 - 2 * lax.rem(z, 2)


def partners():
    y, x, c, z = position()
    return {
        "x": (4 * y + 2 * (1 - x) + c, z),
        "y": (4 * (1 - y) + 2 * x + c, z),
        "core": (4 * y + 2 * x + 1 - c, z),
        "pair": (4 * y + 2 * x + c, partner(z)),
        "across": (4 * y + 2 * x + c, 3 - z),
        "z1": (4 * y + 2 * x + c, lax.rem(z + 1, 4)),
        "z2": (4 * y + 2 * x + c, lax.rem(z + 2, 4)),
        "z3": (4 * y + 2 * x + c, lax.rem(z + 3, 4)),
    }


def enter(peers):
    barrier = pltpu.get_barrier_semaphore()
    greeted = [peer for kind, peer in peers.items() if kind not in ("pair", "across")]
    for peer in greeted:
        pl.semaphore_signal(barrier, inc=1, device_id=peer, device_id_type=MESH)
    pl.semaphore_wait(barrier, len(greeted))


class Sum:
    def __init__(self, peers, held, got, send, recv):
        self.peers, self.held, self.got, self.send, self.recv = peers, held, got, send, recv

    def copy(self, i, kind, level):
        return pltpu.make_async_remote_copy(
            src_ref=self.held.at[level], dst_ref=self.got.at[i], send_sem=self.send.at[i], recv_sem=self.recv.at[i],
            device_id=self.peers[kind], device_id_type=MESH,
        )

    STAGES = ((("z1", 0), ("z2", 1), ("z3", 2)), (("x", 3),), (("y", 4),), (("core", 5),))

    def start(self, level):
        for kind, i in self.STAGES[level]:
            self.copy(i, kind, level).start()

    def finish(self, level):
        total = self.held[level].astype(F32)
        for kind, i in self.STAGES[level]:
            self.copy(i, kind, level).wait_recv()
            total = total + self.got[i].astype(F32)
        self.held[level + 1] = total.astype(self.held.dtype)

    def drain(self):
        for level, stage in enumerate(self.STAGES):
            for kind, i in stage:
                self.copy(i, kind, level).wait_send()


class Gather:
    def __init__(self, peers, direct, shard, zbuf, group, full, local, send, recv):
        self.peers, self.shard, self.zbuf, self.group, self.full = peers, shard, zbuf, group, full
        self.local, self.send, self.recv = local, send, recv
        self.direct = direct
        self.rows, self.cols = group.shape
        z = lax.axis_index("seq")
        self.inner = (z == 1) | (z == 2)

    def place(self, which, half):
        y, x, c, _ = position()
        y, x = {"own": (y, x), "x": (y, 1 - x), "y": (1 - y, x), "xy": (1 - y, 1 - x)}[which]
        rows = pl.ds(pl.multiple_of((4 * y + 2 * x + c) * self.rows, self.rows), self.rows)
        n = self.cols // 2
        return (rows, pl.ds(0, self.cols)) if half is None else (rows, pl.ds(half * n, n))

    PLAN = {
        5: ("own", 0, "x"), 6: ("own", 1, "y"), 7: ("own", 0, "y"), 8: ("x", 0, "y"), 9: ("own", 1, "x"), 10: ("y", 1, "x"),
        11: ("own", None, "core"), 12: ("x", 0, "core"), 13: ("y", 1, "core"), 14: ("y", 0, "core"), 15: ("xy", 0, "core"),
        16: ("x", 1, "core"), 17: ("xy", 1, "core"),
    }

    def copy(self, i):
        if i < 5:
            z = lax.axis_index("seq")
            if self.direct:
                return self.remote(self.shard, self.zbuf.at[z], i, ("z1", "z2", "z3")[i])
            whose = (z, z, partner(z), 3 - z, partner(3 - z))[i]
            dst = self.zbuf.at[whose]
            src = self.shard if i < 2 else dst
            kind = ("pair", "across", "across", "pair", "pair")[i]
        else:
            which, half, kind = self.PLAN[i]
            at = self.place(which, half)
            src = dst = self.full.at[at]
            if which == "own":
                src = self.group if half is None else self.group.at[:, pl.ds(half * (self.cols // 2), self.cols // 2)]
        return self.remote(src, dst, i, kind)

    def remote(self, src, dst, i, kind):
        return pltpu.make_async_remote_copy(
            src_ref=src, dst_ref=dst, send_sem=self.send.at[i], recv_sem=self.recv.at[i], device_id=self.peers[kind],
            device_id_type=MESH,
        )

    def own_in(self):
        return pltpu.make_async_copy(self.shard, self.zbuf.at[lax.axis_index("seq")], self.local.at[0])

    def own_out(self):
        return pltpu.make_async_copy(self.group, self.full.at[self.place("own", None)], self.local.at[1])

    def start(self, items):
        for i in items:
            self.copy(i).start()

    def arrive(self, items):
        for i in items:
            self.copy(i).wait_recv()

    def step0(self):
        self.own_in().start()
        if self.direct:
            self.start((0, 1, 2))
            return
        self.start((0,))

        @pl.when(self.inner)
        def _():
            self.start((1,))

    def stepa(self):
        self.arrive((0,))

        @pl.when(self.inner)
        def _():
            self.start((2,))

    def stepb(self):
        @pl.when(self.inner)
        def _():
            self.arrive((1,))
            self.start((3,))
            self.arrive((2,))
            self.start((4,))

    def step1(self):
        if self.direct:
            self.arrive((0, 1, 2))
        else:

            @pl.when(jnp.logical_not(self.inner))
            def _():
                self.arrive((3, 4))

        self.own_in().wait()
        self.group[...] = jnp.concatenate([self.zbuf[i].astype(F32) for i in range(4)], axis=0).astype(BF16)
        self.own_out().start()
        self.start((5, 6, 7, 9, 11))

    def step2(self):
        self.arrive((5, 6))
        self.start((8, 10, 12, 13))

    def step3(self):
        self.arrive((7, 9, 8, 10))
        self.start((14, 16, 15, 17))

    def step4(self):
        self.arrive((11, 12, 13, 14, 16, 15, 17))
        self.own_out().wait()

    def drain(self):
        for i in (*range(3 if self.direct else 1), *range(5, 18)):
            self.copy(i).wait_send()
        if self.direct:
            return

        @pl.when(self.inner)
        def _():
            for i in range(1, 5):
                self.copy(i).wait_send()


class Swap:
    def __init__(self, peers, pick, land, local, send, recv):
        self.peers, self.pick, self.land, self.local, self.send, self.recv = peers, pick, land, local, send, recv

    def copies(self):
        z = lax.axis_index("seq")
        for j in range(3):
            yield pltpu.make_async_remote_copy(
                src_ref=self.pick(lax.rem(z + j + 1, 4)), dst_ref=self.land, send_sem=self.send.at[j], recv_sem=self.recv.at[j],
                device_id=self.peers[f"z{j + 1}"], device_id_type=MESH,
            )

    def own(self):
        return pltpu.make_async_copy(self.pick(lax.axis_index("seq")), self.land, self.local)

    def start(self):
        for copy in self.copies():
            copy.start()
        if self.local is not None:
            self.own().start()

    def arrive(self):
        for copy in self.copies():
            copy.wait_recv()
        if self.local is not None:
            self.own().wait()

    def drain(self):
        for copy in self.copies():
            copy.wait_send()


def rows_at(start, size):
    return pl.ds(pl.multiple_of(start, size), size)


GATHERED = ((0, 0), (0, 1), (0, 2), (1, 0), (2, 0), (2, 1), (2, 2), (3, 0), (5, 0), (4, 0), (4, 1), (4, 2), (4, 3))
BEFORE = {
    0: (0, 1, 2, 3, 300, 301, 4, 5, 400, 6, 302, 7, 8, 401, 303, 104, 105, 500, 106, 402, 107, 9, 600, 108, 501, 403, 204, 109, 10, 601, 205, 206, 11, 502, 207, 503, 304, 110, 12, 602, 208, 603),
    1: (404, 305, 306, 209, 210, 111, 112),
    2: (504, 405, 307),
    3: (604, 406, 308, 211, 212, 505, 407),
    4: (605, 506),
    5: (606,),
    6: (408,),
    7: (507, 309),
}
EARLY = (310, 311, 312, 607)
LATE = (508, 409, 410, 608, 411, 412, 509, 510, 609, 511, 610, 512, 611, 612)
VEC_AT = (300, 302, 401, 501)
AFTER_SPACE = {0: (0,), 1: (1,), 2: (2,), 3: (3,), 7: (100,)}
AT_PLACE = {
    (0, 0): (101,), (0, 1): (4,), (0, 2): (102,), (1, 0): (5,), (1, 2): (103,),
    (2, 0): (6,), (2, 2): (7,), (3, 0): (104,), (3, 2): (105,), (4, 0): (106,),
    (4, 2): (107,), (5, 2): (200,), (6, 0): (201,), (6, 2): (202,), (7, 0): (203,), (7, 2): (204,),
}
KEPT = 5


def front_kernel(x_ref, vec_ref, cot_ref, *refs):
    shards = refs[:6]
    a_ref, qkv_ref, pt_ref, o_ref = refs[6:10]
    land_ref, home_ref, wqkv_out, wo_out, vec_out = refs[10:15]
    out_all, out_home, rest_all, g_ref = refs[15:19]
    kept_refs = refs[19:27]
    sum_ref = kept_refs[7]
    weights = refs[27:33]
    x1_ref, tqkv_ref, tpt_ref, gland, dx1_ref, xin, out_ref = refs[33:40]
    count = len(GATHERED)
    refs = refs[40:]
    zbufs, groups = refs[:count], refs[count : 2 * count]
    held, got, local, send, recv, vsend, vrecv, keep, xlocal, xsend, xrecv = refs[2 * count : 2 * count + 11]
    glocal, gsend, grecv, dlocal, dsend, drecv, xload, gkeep, okeep, dkeep = refs[2 * count + 11 :]
    step = pl.program_id(0)
    blocks, rows, width = x1_ref.shape
    _, frames, part, _ = gland.shape
    clips, per, places, _ = cot_ref.shape
    chunks, mine = blocks // clips, places // 4
    z = lax.axis_index("seq")
    peers = partners()
    vec = Sum(peers, held, got, vsend, vrecv)

    def piece(u):
        w, at = GATHERED[u]
        return (ref.at[:, pl.ds(at * width, width)] for ref in (shards[w], weights[w]))

    work = []
    for u in range(count):
        shard, full = piece(u)
        work.append(Gather(peers, u < 4, shard, zbufs[u], groups[u], full, local.at[u], send.at[u], recv.at[u]))

    def swap_x1(b):
        return Swap(
            peers, lambda to: x1_ref.at[b, rows_at(to * mine, mine)], land_ref.at[b // per, z * per + lax.rem(b, per)],
            xlocal.at[b], xsend.at[b], xrecv.at[b],
        )

    def swap_cot(b):
        return Swap(
            peers, lambda to: cot_ref.at[b // chunks, :, rows_at(to * mine + (b % chunks) * part, part)],
            gland.at[b, pl.ds(z * per, per)], glocal.at[b], gsend.at[b], grecv.at[b],
        )

    def swap_dx1(b):
        return Swap(
            peers, lambda to: dx1_ref.at[b, pl.ds(to * per, per)],
            home_ref.at[b // chunks, :, rows_at(z * mine + (b % chunks) * part, part)], dlocal.at[b], dsend.at[b], drecv.at[b],
        )

    def out_copies(b):
        own = out_home.at[b // chunks, :, rows_at(z * mine + (b % chunks) * part, part)]
        return (
            pltpu.make_async_copy(out_ref.at[b % 2], out_all.at[b], okeep.at[b % 2, 0]),
            pltpu.make_async_copy(out_ref.at[b % 2, pl.ds(z * per, per)], own, okeep.at[b % 2, 1]),
        )

    def dx1_copies(b):
        own = home_ref.at[b // chunks, :, rows_at(z * mine + (b % chunks) * part, part)]
        return (
            pltpu.make_async_copy(dx1_ref.at[KEPT + b % 2], rest_all.at[b - KEPT], dkeep.at[b % 2, 0]),
            pltpu.make_async_copy(dx1_ref.at[KEPT + b % 2, pl.ds(z * per, per)], own, dkeep.at[b % 2, 1]),
        )

    def load_x1(b):
        src = land_ref.at[b // chunks, :, rows_at((b % chunks) * part, part)]
        return pltpu.make_async_copy(src, xin.at[b % 2], xload.at[b % 2])

    def g_out(b):
        return pltpu.make_async_copy(gland.at[b], g_ref.at[b], gkeep.at[b])

    def kept(i):
        return pltpu.make_async_copy(weights[i], (wqkv_out, wo_out)[i], keep.at[i])

    def event(code):
        w = work[code % 100]
        (w.step0, w.stepa, w.stepb, w.step1, w.step2, w.step3, w.step4)[code // 100]()

    @pl.when(step == 0)
    def _():
        sum_ref[...] = jnp.zeros_like(sum_ref)
        held[0] = vec_ref[...]
        enter(peers)
        vec.start(0)
        for name in BEFORE[0]:
            event(name)
            if name in VEC_AT:
                level = VEC_AT.index(name)
                vec.finish(level)
                if level < 3:
                    vec.start(level + 1)
        vec_out[...] = held[4].astype(F32)
        kept(0).start()
        kept(1).start()

    for k in range(1, 8):

        @pl.when(step == k)
        def _(k=k):
            for name in BEFORE[k]:
                event(name)

    def exchange(code):
        (swap_x1, swap_cot, swap_dx1)[code // 100](code % 100).start()

    def at(point):
        for (b, where), names in AT_PLACE.items():
            if where == point:

                @pl.when(step == blocks + b)
                def _(names=names):
                    for name in names:
                        exchange(name)

    @pl.when(step < blocks)
    def _():
        x1_ref[step] = space_rows(
            x_ref[0].astype(F32), vec_out, weights[0], weights[1], a_ref, qkv_ref, pt_ref.at[0], o_ref
        )

        for k, names in AFTER_SPACE.items():

            @pl.when(step == k)
            def _(names=names):
                for name in names:
                    exchange(name)

    @pl.when(step >= blocks)
    def _():
        b = step - blocks
        slot = lax.rem(b, 2)
        at(0)

        @pl.when(b == 0)
        def _():
            for name in EARLY:
                event(name)

        @pl.when(lax.rem(b, chunks) == 0)
        def _():
            def arrived(k, _):
                swap_x1((b // chunks) * per + k).arrive()
                return 0

            lax.fori_loop(0, per, arrived, 0)
            load_x1(b).start()

        load_x1(b).wait()

        @pl.when(lax.rem(b, chunks) < chunks - 1)
        def _():
            load_x1(b + 1).start()

        def take_g():
            at(1)

            @pl.when(b == 0)
            def _():
                for name in LATE:
                    event(name)

            swap_cot(b).arrive()
            g_out(b).start()
            return gland[b].reshape(rows, width)

        x1 = xin[slot].reshape(rows, width).astype(F32)
        out, dx1 = place_rows(x1, take_g, lambda: at(2), part, vec_out, *weights[2:], *kept_refs, tqkv_ref, tpt_ref)

        @pl.when(b >= 2)
        def _():
            for copy in out_copies(b - 2):
                copy.wait()

        out_ref[slot] = out.reshape(frames, part, width)
        for copy in out_copies(b):
            copy.start()

        @pl.when(b >= KEPT + 2)
        def _():
            for copy in dx1_copies(b - 2):
                copy.wait()

        dx1_ref[jnp.where(b < KEPT, b, KEPT + slot)] = dx1.reshape(frames, part, width)

        @pl.when(b >= KEPT)
        def _():
            for copy in dx1_copies(b):
                copy.start()

    @pl.when(step == 2 * blocks - 1)
    def _():
        kept(0).wait()
        kept(1).wait()
        vec.drain()
        for w in work:
            w.drain()

        def finish(b, _):
            swap_x1(b).drain()
            swap_cot(b).drain()
            g_out(b).wait()
            return 0

        lax.fori_loop(0, blocks, finish, 0)

        for b in (blocks - 2, blocks - 1):
            for copy in out_copies(b) + dx1_copies(b):
                copy.wait()

        def finish_dx1(b, _):
            swap_dx1(b).arrive()
            swap_dx1(b).drain()
            return 0

        lax.fori_loop(0, KEPT, finish_dx1, 0)


def front(x, cot, vec, shards):
    blocks, rows, width = x.shape
    clips, per, places, _ = cot.shape
    frames = 4 * per
    part = rows // frames
    tok = blocks * rows
    count = len(GATHERED)
    dma = pltpu.SemaphoreType.DMA

    def one(s):
        return jnp.minimum(s, blocks - 1)

    def two(s):
        return jnp.maximum(s - blocks, 0)

    def early(*shape):
        return pl.BlockSpec(shape, lambda s: (one(s),) + (0,) * (len(shape) - 1))

    def late(*shape):
        return pl.BlockSpec(shape, lambda s: (two(s),) + (0,) * (len(shape) - 1))

    fixed = pl.BlockSpec((VEC_ROWS, width), lambda s: (0, 0))
    full = [(32 * s.shape[0], s.shape[1]) for s in shards]
    ff = full[4][1]
    place = (blocks, frames, part, width)
    token_widths = (width, 3 * width, width, width, width, ff, ff)
    out = pl.pallas_call(
        front_kernel,
        grid=(2 * blocks,),
        in_specs=[early(1, rows, width), whole(vec.shape)] + [ANYWHERE] * 7,
        out_specs=[
            early(rows, width), early(rows, 3 * width), early(1, HEADS // 2, 2 * rows, rows), early(rows, width),
            ANYWHERE, ANYWHERE, ANYWHERE, ANYWHERE, fixed, ANYWHERE, ANYWHERE, ANYWHERE, ANYWHERE,
        ] + [late(rows, w) for w in token_widths] + [pl.BlockSpec((SUM_ROWS, 8, width), lambda s: (0, 0, 0))],
        out_shape=[
            sds(tok, width), sds(tok, 3 * width), sds(blocks, HEADS // 2, 2 * rows, rows), sds(tok, width),
            sds(clips, frames, places // 4, width), sds(*cot.shape), sds(*full[0]), sds(*full[1]),
            sds(VEC_ROWS, width, dtype=F32), sds(*place), sds(*cot.shape), sds(blocks - KEPT, *place[1:]),
            sds(*place),
        ] + [sds(tok, w) for w in token_widths] + [sds(SUM_ROWS, 8, width, dtype=F32)],
        scratch_shapes=[pltpu.VMEM(s, BF16) for s in full]
        + [
            pltpu.VMEM((blocks, rows, width), BF16), pltpu.VMEM((rows, 3 * width), BF16),
            pltpu.VMEM((HEADS // 2, 2 * rows, rows), BF16), pltpu.VMEM(place, BF16),
            pltpu.VMEM((KEPT + 2, *place[1:]), BF16), pltpu.VMEM((2, *place[1:]), BF16), pltpu.VMEM((2, *place[1:]), BF16),
        ]
        + [pltpu.VMEM((4, shards[w].shape[0], width), BF16) for w, _ in GATHERED]
        + [pltpu.VMEM((4 * shards[w].shape[0], width), BF16) for w, _ in GATHERED]
        + [
            pltpu.VMEM((5, *vec.shape), BF16), pltpu.VMEM((6, *vec.shape), BF16), dma((count, 2)), dma((count, 18)),
            dma((count, 18)), dma((6,)), dma((6,)), dma((2,)), dma((blocks,)), dma((blocks, 3)), dma((blocks, 3)),
            dma((blocks,)), dma((blocks, 3)), dma((blocks, 3)), dma((KEPT,)), dma((KEPT, 3)), dma((KEPT, 3)), dma((2,)), dma((blocks,)),
            dma((2, 2)), dma((2, 2)),
        ],
        compiler_params=params(0),
        name="front",
    )(x, vec.astype(BF16), cot, *shards)
    return out[:4], out[5], out[6:8], out[8], out[9:12], out[12:]


class Scatter:
    def __init__(self, peers, direct, piece, core, first, second, zsend, zgot, out, send, recv):
        self.peers, self.piece, self.core = peers, piece, core
        self.first, self.second, self.zsend, self.zgot, self.out = first, second, zsend, zgot, out
        self.send, self.recv = send, recv
        self.direct = direct
        z = lax.axis_index("seq")
        self.inner = (z == 1) | (z == 2)
        self.rows, self.half = core.shape[1], core.shape[2] // 2

    def block(self, i, c):
        return rows_at((2 * i + c) * self.rows, self.rows)

    def copy(self, i):
        y, x, c, z = position()
        if i < 4:
            src, dst, kind = self.piece.at[self.block(i, 1 - c)], self.core.at[i], "core"
        elif i < 6:
            src, dst, kind = self.core.at[2 * (i - 4) + 1 - x, :, pl.ds(0, self.half)], self.first.at[0, i - 4], "x"
        elif i < 8:
            src, dst, kind = self.core.at[2 * (1 - y) + i - 6, :, pl.ds(self.half, self.half)], self.first.at[1, i - 6], "y"
        elif i == 8:
            src, dst, kind = self.first.at[0, 1 - y], self.second.at[0], "y"
        elif i == 9:
            src, dst, kind = self.first.at[1, 1 - x], self.second.at[1], "x"
        elif self.direct:
            j = i - 9
            src, dst, kind = self.zsend.at[lax.rem(z + j, 4)], self.zgot.at[j - 1], f"z{j}"
        else:
            near, far = partner(z), 3 - partner(z)
            whose = (near, far, partner(far), 3 - z, partner(3 - z), near)[i - 10]
            src, dst = self.zsend.at[whose], self.zgot.at[(0, 1, 2, 3, 4, 0)[i - 10]]
            kind = "across" if i in (13, 14) else "pair"
        return pltpu.make_async_remote_copy(
            src_ref=src, dst_ref=dst, send_sem=self.send.at[i], recv_sem=self.recv.at[i], device_id=self.peers[kind],
            device_id_type=MESH,
        )

    def start(self, items):
        for i in items:
            self.copy(i).start()

    def arrive(self, items):
        for i in items:
            self.copy(i).wait_recv()

    def sent(self, items):
        for i in items:
            self.copy(i).wait_send()

    def step0(self):
        self.start(range(4))

    def step1(self):
        _, _, c, _ = position()
        self.arrive(range(4))

        def add(i, _):
            self.core[i] = self.piece[self.block(i, c)] + self.core[i]
            return 0

        lax.fori_loop(0, 4, add, 0)
        self.start(range(4, 8))
        self.sent(range(4))

    def step2(self):
        y, x, _, _ = position()
        n = self.half
        self.arrive(range(4, 8))
        for i in range(2):
            self.first[0, i] = self.first[0, i] + self.core[2 * i + x, :, :n]
            self.first[1, i] = self.first[1, i] + self.core[2 * y + i, :, n:]
        self.start((8, 9))

    def step3(self):
        y, x, _, _ = position()
        self.arrive((8, 9))
        r = self.zsend.shape[1]
        for k, at in ((0, y), (1, x)):
            total = self.first[k, at].astype(F32) + self.second[k].astype(F32)
            for i in range(4):
                self.zsend[i, :, k * self.half : (k + 1) * self.half] = total[i * r : (i + 1) * r].astype(BF16)
        if self.direct:
            self.start((10, 11, 12))
            return

        @pl.when(jnp.logical_not(self.inner))
        def _():
            self.start((10, 11, 12))

    def stepb(self):
        @pl.when(self.inner)
        def _():
            z = lax.axis_index("seq")
            self.arrive((10, 11, 12))
            for whose, i in ((3 - z, 1), (partner(3 - z), 2)):
                self.zsend[whose] = self.zsend[whose] + self.zgot[i]
            self.start((13, 14))

    def stepc(self):
        @pl.when(self.inner)
        def _():
            z = lax.axis_index("seq")
            self.arrive((13, 14))
            near = partner(z)
            self.zsend[near] = self.zsend[near] + self.zgot[4]
            self.start((15,))

    def step4(self):
        z = lax.axis_index("seq")
        if self.direct:
            self.arrive((10, 11, 12))
            total = self.zsend[z].astype(F32)
            for i in range(3):
                total = total + self.zgot[i].astype(F32)
            self.out[...] = total
            self.sent((10, 11, 12))
            return

        @pl.when(self.inner)
        def _():
            self.out[...] = self.zsend[z].astype(F32) + self.zgot[0].astype(F32) + self.zgot[3].astype(F32)
            self.sent((13, 14, 15))

        @pl.when(jnp.logical_not(self.inner))
        def _():
            self.arrive((15,))
            self.out[...] = self.zsend[z].astype(F32) + self.zgot[0].astype(F32)
            self.sent((10, 11, 12))

    def drain(self):
        self.sent(range(4, 10))


PANELS, BLOCKS, UNITS, SLOTS = 11, 8, 16, 6
CHAINED = 12
STEPS = PANELS + BLOCKS + UNITS - PANELS
AFTER_STEP = {
    3: (0, 1, 2, 3),
    4: (4,),
    5: (5, 100),
    6: (6, 101),
    7: (7, 102),
    8: (8, 103, 200, 201),
    9: (9, 104, 202),
    10: (10, 203),
    11: (105, 300, 301, 204),
    12: (106, 302, 303, 107),
    13: (205, 108, 304),
    14: (206, 207, 109, 305),
    15: (208, 110, 306),
    16: (209, 400, 401, 307),
    17: (210, 402, 403),
    18: (404,),
    19: (11, 405),
    20: (12,),
    21: (13, 111, 406),
    22: (14, 112, 500, 501, 407, 113, 506),
    23: (15, 211, 502, 503, 600, 601, 606, 114, 507, 308, 309, 212),
}
TAIL = (602, 310, 603, 504, 505, 607, 408, 409, 115, 213, 311, 604, 605, 508, 214, 509, 410, 312, 608, 609, 411, 215, 510, 313, 314, 511, 612, 315, 610, 611, 613, 614, 615)
OUT_AT = (6, 9, 11, 13, 15, 17, 19, 21)


def last_kernel(
    x_ref, qkv_ref, pt_ref, vec_ref, sums_ref, wqkv_ref, wo_ref, z_ref, g_ref, a3_ref, dh_ref, ot_ref, gt_ref, a2_ref,
    dp_ref, a1_ref, o_ref, rest_ref, out_ref, g1_in_place, out_in_place, dx_ref, sqkv_out, so_out, tqkv_out, to_out, win_out, wout_out, vec_out, home_ref,
    dps_ref, g1_home, lbuf, rbuf, pieces, core, one, two, zsend, zgot, dpbuf, gbuf, ssum, held, got, lsem, rsem, send, recv, vsend, vrecv,
    dpsem, gsem, osend, orecv, rsend, rrecv,
):
    step = pl.program_id(0)
    z = lax.axis_index("seq")
    peers = partners()
    width = x_ref.shape[2]
    rows = core.shape[2]
    small = zsend.shape[2]
    blocks, frames, part, _ = out_ref.shape
    clips, per, places, _ = home_ref.shape
    chunks, mine = blocks // clips, places // 4
    vec = Sum(peers, held, got, vsend, vrecv)

    def columns(i):
        return pl.ds(pl.multiple_of(i * width, width), width)

    def out_of(u):
        if u < 4:
            return wout_out.at[pl.ds(u * small, small)]
        if u == 8:
            return to_out
        if u == 12:
            return so_out
        ref, i = (win_out, u - 4) if u < 8 else (tqkv_out, u - 9) if u < 12 else (sqkv_out, u - 13)
        return ref.at[:, pl.ds(i * width, width)]

    work = [
        Scatter(
            peers, u >= CHAINED, pieces.at[u % SLOTS], core.at[u], one.at[u], two.at[u], zsend.at[u % 8], zgot.at[u], out_of(u), send.at[u],
            recv.at[u],
        )
        for u in range(UNITS)
    ]

    def event(code):
        w = work[code % 100]
        (w.step0, w.step1, w.step2, w.step3, w.stepb, w.stepc, w.step4)[code // 100]()

    def swap(b):
        return Swap(
            peers, lambda to: out_ref.at[b, pl.ds(to * per, per)],
            home_ref.at[b // chunks, :, rows_at(z * mine + (b % chunks) * part, part)], None, osend.at[b], orecv.at[b],
        )

    def rest(b):
        return Swap(
            peers, lambda to: rest_ref.at[b - KEPT, pl.ds(to * per, per)],
            g1_home.at[b // chunks, :, rows_at(z * mine + (b % chunks) * part, part)], None, rsend.at[b - KEPT],
            rrecv.at[b - KEPT],
        )

    def load(ref, at, buf, sem, slot):
        src = ref if at is None else ref.at[:, columns(at)]
        return pltpu.make_async_copy(src, buf.at[slot], sem.at[slot])

    def fetch(p, left, l_at, right, r_at):
        slot = lax.rem(p, 2)
        load(left, l_at, lbuf, lsem, slot).start()
        if right is g1_home:
            n = x_ref.shape[1]
            for b in range(clips * per):
                src = g1_home.at[b // per, b % per]
                pltpu.make_async_copy(src, rbuf.at[slot, pl.ds(b * n, n)], rsem.at[slot]).start()
        else:
            load(right, r_at, rbuf, rsem, slot).start()

    def fetch_panel(p):
        for least, most, left, right, which in (
            (0, 4, z_ref, g_ref, "l"), (4, 8, a3_ref, dh_ref, "r"), (8, 9, ot_ref, gt_ref, ""), (9, 12, a2_ref, dp_ref, "r"),
            (12, 13, o_ref, g1_home, ""), (13, 16, a1_ref, dps_ref, "r"),
        ):

            @pl.when((p >= least) & (p < most))
            def _():
                at = p - least
                fetch(p, left, at if which == "l" else None, right, at if which == "r" else None)

    def dp_out(b):
        return pltpu.make_async_copy(dpbuf.at[b % 2], dps_ref.at[rows_at(b * x_ref.shape[1], x_ref.shape[1])], dpsem.at[b % 2])

    def g1_in(b):
        return pltpu.make_async_copy(g1_home.at[b // per, b % per], gbuf.at[b % 2], gsem.at[b % 2])

    is_block = (step >= PANELS) & (step < PANELS + BLOCKS)
    panel = jnp.where(step < PANELS, step, step - BLOCKS)

    @pl.when(step == 0)
    def _():
        ssum[...] = sums_ref[...]
        fetch_panel(step)
        enter(peers)
        for b in range(KEPT, blocks):
            rest(b).start()

    for b, at in enumerate(OUT_AT):

        @pl.when(step == at)
        def _(b=b):
            swap(b).start()

    @pl.when((step < PANELS - 1) | (step >= PANELS + BLOCKS - 1) & (step < STEPS - 1))
    def _():
        fetch_panel(jnp.where(step < PANELS, step + 1, step + 1 - BLOCKS))

    @pl.when(jnp.logical_not(is_block))
    def _():
        slot = lax.rem(panel, 2)
        load(z_ref, 0, lbuf, lsem, slot).wait()
        load(z_ref, 0, rbuf, rsem, slot).wait()
        total = outer_sum(lbuf[slot], rbuf[slot])

        @pl.when(panel >= 4)
        def _():
            pieces[lax.rem(panel, SLOTS)] = total.astype(BF16)

        @pl.when(panel < 4)
        def _():
            cut = total.reshape(2, 4, 4, small, width)
            for d in range(2):
                for i in range(4):
                    both = jnp.concatenate([cut[d, k, i] for k in range(4)], axis=0)
                    pieces[i, rows_at((2 * panel + d) * rows, rows)] = both.astype(BF16)

    @pl.when(is_block)
    def _():
        b = step - PANELS

        @pl.when(b >= 2)
        def _():
            dp_out(b - 2).wait()

        slot = lax.rem(b, 2)

        @pl.when(b == 0)
        def _():
            g1_in(b).start()

        @pl.when(b == per - 1)
        def _():
            for k in range(KEPT, blocks):
                rest(k).arrive()

        g1_in(b).wait()

        @pl.when(b < BLOCKS - 1)
        def _():
            g1_in(b + 1).start()

        dx_ref[0] = space_back_rows(
            x_ref[0].astype(F32), gbuf[slot], qkv_ref, pt_ref.at[0], vec_ref, wqkv_ref, wo_ref, dpbuf.at[lax.rem(b, 2)], ssum
        )
        dp_out(b).start()

    @pl.when(step == PANELS + BLOCKS - 1)
    def _():
        dp_out(step - PANELS - 1).wait()
        dp_out(step - PANELS).wait()
        held[0] = jnp.concatenate([jnp.sum(ssum[i], axis=0, keepdims=True) for i in range(SUM_ROWS)], axis=0)
        vec.start(0)

    for k, names in AFTER_STEP.items():

        @pl.when(step == k)
        def _(k=k, names=names):
            for name in names:
                event(name)
            if k >= PANELS + BLOCKS:
                level = k - PANELS - BLOCKS
                if level < 4:
                    vec.finish(level)
                if level < 3:
                    vec.start(level + 1)

    @pl.when(step == STEPS - 1)
    def _():
        for name in TAIL:
            event(name)
        vec_out[...] = held[4]
        vec.drain()
        for b in range(KEPT, blocks):
            rest(b).drain()
        for w in work:
            w.drain()

        def finish(b, _):
            swap(b).arrive()
            swap(b).drain()
            return 0

        lax.fori_loop(0, blocks, finish, 0)


def last(x, home, outs, saved, vec, wqkv, wo, shapes):
    z, g, a3, dh, ot, gt, a2, dp, a1, o, qkv, pt, sums = saved
    out, out_home, rest = outs
    blocks, rows, width = x.shape
    tok = blocks * rows
    dma = pltpu.SemaphoreType.DMA
    in_vmem = pl.BlockSpec(memory_space=pltpu.VMEM)

    def at(s):
        return jnp.minimum(jnp.maximum(s - PANELS, 0), BLOCKS - 1)

    seq = pl.BlockSpec((1, rows, width), lambda s: (at(s), 0, 0))
    small = width // 32
    result = pl.pallas_call(
        last_kernel,
        grid=(STEPS,),
        in_specs=[
            seq, pl.BlockSpec((rows, 3 * width), lambda s: (at(s), 0)),
            pl.BlockSpec((1, HEADS // 2, 2 * rows, rows), lambda s: (at(s), 0, 0, 0)),
        ] + [whole(v.shape) for v in (vec, sums, wqkv, wo)] + [ANYWHERE] * 14,
        out_specs=[seq] + [in_vmem] * 7 + [ANYWHERE] * 3,
        out_shape=[sds(*x.shape)] + [sds(*s, dtype=F32) for s in shapes]
        + [sds(SUM_ROWS, width, dtype=F32), sds(*home.shape), sds(tok, 3 * width), sds(*home.shape)],
        scratch_shapes=[
            pltpu.VMEM((2, tok, width), BF16), pltpu.VMEM((2, tok, width), BF16), pltpu.VMEM((SLOTS, width, width), BF16),
            pltpu.VMEM((UNITS, 4, 4 * small, width), BF16),
            pltpu.VMEM((UNITS, 2, 2, 4 * small, width // 2), BF16), pltpu.VMEM((UNITS, 2, 4 * small, width // 2), BF16),
            pltpu.VMEM((8, 4, small, width), BF16),
            pltpu.VMEM((UNITS, 5, small, width), BF16), pltpu.VMEM((2, rows, 3 * width), BF16),
            pltpu.VMEM((2, rows, width), BF16),
            pltpu.VMEM((SUM_ROWS, 8, width), F32), pltpu.VMEM((5, SUM_ROWS, width), F32), pltpu.VMEM((6, SUM_ROWS, width), F32),
            dma((2,)), dma((2,)), dma((UNITS, 16)), dma((UNITS, 16)), dma((6,)), dma((6,)), dma((2,)), dma((2,)),
            dma((blocks, 3)), dma((blocks, 3)), dma((blocks - KEPT, 3)), dma((blocks - KEPT, 3)),
        ],
        input_output_aliases={19: 10, 20: 8},
        compiler_params=params(2),
        name="last",
    )(x, qkv, pt, vec, sums, wqkv, wo, z, g, a3, dh, ot, gt, a2, dp, a1, o, rest, out, home, out_home)
    return result[0], result[1:7], result[7], result[8]


def ring_layer(inputs, cotangent, shards, vec):
    clips, frames, places, width = inputs.shape
    x = inputs.reshape(clips * frames, places, width)
    (a1, qkv, pt, o), home, (wqkv, wo), vec, outs, (g, a2, dp, ot, gt, a3, z, dh, sums) = front(x, cotangent, vec, shards)
    saved = (z, g.reshape(a2.shape), a3, dh, ot, gt, a2, dp, a1, o, qkv, pt, sums)
    dx, grads, rows, output = last(x, home, outs, saved, vec, wqkv, wo, [s.shape for s in shards])
    return output, dx.reshape(inputs.shape), grads, rows


def my_index():
    return lax.axis_index("dp") * lax.axis_size("seq") + lax.axis_index("seq")


def spread_vectors(shards, width):
    devices = lax.axis_size("dp") * lax.axis_size("seq")
    me = my_index()
    rows = []
    for items in (NARROW, WIDE, (LONG,)):
        part = jnp.stack([shards[i] for i in items]).astype(F32)
        size = part.shape[1]
        zero = jnp.zeros((len(items), devices * size), F32)
        rows.append(lax.dynamic_update_slice(zero, part, (0, me * size)).reshape(-1, width))
    rows = jnp.concatenate(rows)
    return jnp.pad(rows, ((0, VEC_ROWS - rows.shape[0]), (0, 0)))


def own_vectors(rows):
    devices = lax.axis_size("dp") * lax.axis_size("seq")
    me = my_index()
    out, at = {}, 0
    width = rows.shape[1]
    for items, height in ((NARROW, 1), (WIDE, 2), ((LONG,), 4)):
        block = rows[at : at + height * len(items)].reshape(len(items), height * width)
        size = height * width // devices
        part = lax.dynamic_slice(block, (0, me * size), (len(items), size))
        for k, item in enumerate(items):
            out[item] = part[k]
        at += height * len(items)
    return [out[i] for i in range(12)]


def on_device(
    ring, inputs, norm_one_gain, norm_one_shift, space_qkv, space_qv_bias, space_out, space_out_bias,
    norm_two_gain, norm_two_shift, time_qkv, time_qv_bias, time_out, time_out_bias,
    norm_three_gain, norm_three_shift, mlp_in, mlp_in_bias, mlp_out, mlp_out_bias, cotangent,
):
    width = inputs.shape[-1]
    vec = spread_vectors(
        (norm_one_gain, norm_one_shift, space_qv_bias, space_out_bias, norm_two_gain, norm_two_shift,
         time_qv_bias, time_out_bias, norm_three_gain, norm_three_shift, mlp_in_bias, mlp_out_bias), width
    )
    shards = (space_qkv, space_out, time_qkv, time_out, mlp_in, mlp_out)
    layer = ring_layer if ring else plain_layer
    output, dx, grads, rows = layer(inputs, cotangent, shards, vec)
    gsqkv, gso, gtqkv, gto, gin, gout = grads
    vecs = own_vectors(rows)
    return (
        output, dx, vecs[0], vecs[1], gsqkv, vecs[2], gso, vecs[3], vecs[4], vecs[5], gtqkv,
        vecs[6], gto, vecs[7], vecs[8], vecs[9], gin, vecs[10], gout, vecs[11],
    )


def solution(mesh):
    tokens = P("dp", "seq", None, None)
    vector, matrix = P(("dp", "seq")), P(("dp", "seq"), None)
    weights = (vector, vector, matrix, vector, matrix, vector) * 3
    ring = mesh.shape["dp"] == 8 and mesh.shape["seq"] == 4
    return jax.shard_map(
        functools.partial(on_device, ring),
        mesh=mesh,
        in_specs=(tokens,) + weights + (tokens,),
        out_specs=(tokens, tokens) + weights,
        check_vma=False,
    )
```

```python
import functools
import jax
import jax.numpy as jnp
from jax import lax
from jax.experimental import pallas as pl
from jax.experimental.pallas import tpu as pltpu
from jax.sharding import PartitionSpec as P

HEADS = 12
HD = 64
EPS = 1e-06
SCALE = 0.125
F32 = jnp.float32
BF16 = jnp.bfloat16
RSQRT2 = 0.7071067811865476
RSQRT2PI = 0.3989422804014327


def dot(a, b):
    return jnp.dot(a, b, preferred_element_type=F32)


def dot_nt(a, b):
    return lax.dot_general(a, b, (((1,), (1,)), ((), ())), preferred_element_type=F32)


def fold(rows):
    return jnp.sum(rows.reshape(rows.shape[0] // 8, 8, rows.shape[1]), axis=0)


def norm(rows):
    center = rows - jnp.mean(rows, axis=-1, keepdims=True)
    rstd = lax.rsqrt(jnp.mean(center * center, axis=-1, keepdims=True) + EPS)
    return center * rstd, rstd


def norm_back(du, hat, rstd, gain):
    e = du * gain
    return rstd * (
        e - jnp.mean(e, axis=-1, keepdims=True) - hat * jnp.mean(e * hat, axis=-1, keepdims=True)
    )


def split_heads(pair):
    low = lax.broadcasted_iota(jnp.int32, (1, 2 * HD), 1) < HD
    zero = jnp.zeros_like(pair)
    return jnp.concatenate([jnp.where(low, pair, zero), jnp.where(low, zero, pair)], axis=0)


def join_heads(both):
    n = both.shape[0] // 2
    low = lax.broadcasted_iota(jnp.int32, (1, 2 * HD), 1) < HD
    return jnp.where(low, both[:n], both[n:])


def by_head(left, right):
    n = right.shape[0] // 2
    top = dot(left[:HD], right[:n])
    bottom = dot(left[HD:], right[n:])
    return jnp.concatenate([top, bottom], axis=0)


def attend(qkv_ref, pt_ref, o_ref, period):
    width = HEADS * HD
    n = qkv_ref.shape[0]
    for pair in range(HEADS // 2):
        at = pair * 2 * HD
        q = qkv_ref[:, at : at + 2 * HD] * jnp.asarray(SCALE, BF16)
        k = qkv_ref[:, width + at : width + at + 2 * HD]
        v = qkv_ref[:, 2 * width + at : 2 * width + at + 2 * HD]
        s = dot_nt(split_heads(k), q)
        if period:
            keys = lax.broadcasted_iota(jnp.int32, s.shape, 0) % period
            queries = lax.broadcasted_iota(jnp.int32, s.shape, 1) % period
            s = jnp.where(keys == queries, s, -1e30)
        probs = []
        for half in (s[:n], s[n:]):
            e = jnp.exp(half - jnp.max(half, axis=0, keepdims=True))
            probs.append((e * (1.0 / jnp.sum(e, axis=0, keepdims=True))).astype(BF16))
        p = jnp.concatenate(probs, axis=0)
        pt_ref[pair] = p
        o_ref[:, at : at + 2 * HD] = by_head(v.T, p).astype(BF16).T


def attend_back(qkv_ref, pt_ref, do, dp_ref):
    width = HEADS * HD
    n = qkv_ref.shape[0]
    for pair in range(HEADS // 2):
        at = pair * 2 * HD
        q = qkv_ref[:, at : at + 2 * HD] * jnp.asarray(SCALE, BF16)
        k = qkv_ref[:, width + at : width + at + 2 * HD]
        v = qkv_ref[:, 2 * width + at : 2 * width + at + 2 * HD]
        g = do[:, at : at + 2 * HD]
        p = pt_ref[pair]
        dp = dot_nt(split_heads(v), g)
        wide = p.astype(F32)
        ds = []
        for sl in (slice(0, n), slice(n, 2 * n)):
            t = wide[sl] * dp[sl]
            ds.append((t - wide[sl] * jnp.sum(t, axis=0, keepdims=True)).astype(BF16))
        ds = jnp.concatenate(ds, axis=0)
        dp_ref[:, 2 * width + at : 2 * width + at + 2 * HD] = join_heads(dot(p, g)).astype(BF16)
        dp_ref[:, width + at : width + at + 2 * HD] = join_heads(dot(ds, q)).astype(BF16)
        dp_ref[:, at : at + 2 * HD] = (by_head(k.T, ds) * SCALE).astype(BF16).T


GAIN1, SHIFT1, BO1, GAIN2, SHIFT2, BO2, GAIN3, SHIFT3, BOUT, BQ1, BV1, BQ2, BV2, BIN = range(14)
NARROW = (0, 1, 3, 4, 5, 7, 8, 9, 11)
WIDE = (2, 6)
LONG = 10
VEC_ROWS = 32
SUM_ROWS = 24
VMEM_LIMIT = 62 * 2**20


def row(vec_ref, i):
    return vec_ref[i : i + 1]


def project(a, wqkv_ref, bq, bv, qkv_ref):
    width = a.shape[1]
    for i, bias in enumerate((bq, None, bv)):
        sl = slice(i * width, (i + 1) * width)
        part = dot(a, wqkv_ref[:, sl])
        qkv_ref[:, sl] = (part if bias is None else part + bias).astype(BF16)


def space_rows(x, vec_ref, wqkv_ref, wo_ref, a_ref, qkv_ref, pt_ref, o_ref):
    hat, _ = norm(x)
    a = (hat * row(vec_ref, GAIN1) + row(vec_ref, SHIFT1)).astype(BF16)
    a_ref[...] = a
    project(a, wqkv_ref, row(vec_ref, BQ1), row(vec_ref, BV1), qkv_ref)
    attend(qkv_ref, pt_ref, o_ref, 0)
    return (x + dot(o_ref[...], wo_ref[...]) + row(vec_ref, BO1)).astype(BF16)


def place_rows(
    x1, take_g, midway, period, vec_ref, wqkv_ref, wo_ref, win_ref, wout_ref, a2_ref, dp_ref, o_ref, gt_ref, a3_ref, z_ref, dh_ref,
    sum_ref, qkv_ref, pt_ref,
):
    rows, width = x1.shape
    hat2, rstd2 = norm(x1)
    a2 = (hat2 * row(vec_ref, GAIN2) + row(vec_ref, SHIFT2)).astype(BF16)
    a2_ref[...] = a2
    project(a2, wqkv_ref, row(vec_ref, BQ2), row(vec_ref, BV2), qkv_ref)
    attend(qkv_ref, pt_ref, o_ref, period)
    t = (dot(o_ref[...], wo_ref[...]) + row(vec_ref, BO2)).astype(BF16).astype(F32)
    x2 = x1 + t
    hat3, rstd3 = norm(x2)
    a3 = (hat3 * row(vec_ref, GAIN3) + row(vec_ref, SHIFT3)).astype(BF16)
    a3_ref[...] = a3
    g16 = take_g()
    g = g16.astype(F32)
    sum_ref[BOUT] += fold(g)
    y = x2 + row(vec_ref, BOUT)
    da3 = jnp.zeros((rows, width), F32)
    for i in range(win_ref.shape[1] // width):
        sl = slice(i * width, (i + 1) * width)
        h = dot(a3, win_ref[:, sl]) + row(vec_ref, BIN + i)
        cdf = 0.5 + 0.5 * lax.erf(h * RSQRT2)
        z = (h * cdf).astype(BF16)
        z_ref[:, sl] = z
        y = y + dot(z, wout_ref[sl, :])
        dz = dot_nt(g16, wout_ref[sl, :])
        dh = (dz * (cdf + h * (RSQRT2PI * jnp.exp(-0.5 * h * h)))).astype(BF16)
        dh_ref[:, sl] = dh
        sum_ref[BIN + i] += fold(dh.astype(F32))
        da3 = da3 + dot_nt(dh, win_ref[:, sl])
        if i == 1:
            midway()
    sum_ref[GAIN3] += fold(da3 * hat3)
    sum_ref[SHIFT3] += fold(da3)
    dx2 = g + norm_back(da3, hat3, rstd3, row(vec_ref, GAIN3))
    gt = dx2.astype(BF16)
    gt_ref[...] = gt
    sum_ref[BO2] += fold(gt.astype(F32))
    do = dot_nt(gt, wo_ref[...]).astype(BF16)
    attend_back(qkv_ref, pt_ref, do, dp_ref)
    sum_ref[BQ2] += fold(dp_ref[:, :width].astype(F32))
    sum_ref[BV2] += fold(dp_ref[:, 2 * width :].astype(F32))
    da2 = dot_nt(dp_ref[...], wqkv_ref[...]).astype(BF16).astype(F32)
    sum_ref[GAIN2] += fold(da2 * hat2)
    sum_ref[SHIFT2] += fold(da2)
    dx1 = dx2 + norm_back(da2, hat2, rstd2, row(vec_ref, GAIN2))
    return y.astype(BF16), dx1.astype(BF16)


def space_back_rows(x, g, qkv_ref, pt_ref, vec_ref, wqkv_ref, wo_ref, dp_ref, sum_ref):
    width = x.shape[1]
    sum_ref[BO1] += fold(g.astype(F32))
    do = dot_nt(g, wo_ref[...]).astype(BF16)
    attend_back(qkv_ref, pt_ref, do, dp_ref)
    sum_ref[BQ1] += fold(dp_ref[:, :width].astype(F32))
    sum_ref[BV1] += fold(dp_ref[:, 2 * width :].astype(F32))
    da = dot_nt(dp_ref[...], wqkv_ref[...])
    hat, rstd = norm(x)
    sum_ref[GAIN1] += fold(da * hat)
    sum_ref[SHIFT1] += fold(da)
    return (g.astype(F32) + norm_back(da, hat, rstd, row(vec_ref, GAIN1))).astype(BF16)


def params(collective=None):
    extra = {} if collective is None else {"collective_id": collective, "has_side_effects": True}
    return pltpu.CompilerParams(vmem_limit_bytes=VMEM_LIMIT, dimension_semantics=("arbitrary",), **extra)


def whole(shape):
    return pl.BlockSpec(shape, lambda b: (0,) * len(shape), pipeline_mode=pl.Buffered(1))


def rows_spec(rows, cols):
    return pl.BlockSpec((rows, cols), lambda b: (b, 0))


def sds(*shape, dtype=BF16):
    return jax.ShapeDtypeStruct(shape, dtype)


ANYWHERE = pl.BlockSpec(memory_space=pl.ANY)


def space_kernel(x_ref, vec_ref, wqkv_ref, wo_ref, x1_ref, a_ref, qkv_ref, pt_ref, o_ref):
    x1_ref[0] = space_rows(x_ref[0].astype(F32), vec_ref, wqkv_ref, wo_ref, a_ref, qkv_ref, pt_ref.at[0], o_ref)


def place_kernel(x1_ref, g_ref, vec_ref, wqkv_ref, wo_ref, win_ref, wout_ref, out_ref, dx1_ref, *rest):
    _, frames, places, width = x1_ref.shape
    rows = frames * places
    sum_ref = rest[7]

    @pl.when(pl.program_id(0) == 0)
    def _():
        sum_ref[...] = jnp.zeros_like(sum_ref)

    x1 = x1_ref[0].reshape(rows, width).astype(F32)

    def take_g():
        return g_ref[0].reshape(rows, width)

    out, dx1 = place_rows(x1, take_g, lambda: None, places, vec_ref, wqkv_ref, wo_ref, win_ref, wout_ref, *rest)
    out_ref[0] = out.reshape(frames, places, width)
    dx1_ref[0] = dx1.reshape(frames, places, width)


def space_back_kernel(x_ref, g_ref, qkv_ref, pt_ref, vec_ref, wqkv_ref, wo_ref, dx_ref, dp_ref, sum_ref):
    @pl.when(pl.program_id(0) == 0)
    def _():
        sum_ref[...] = jnp.zeros_like(sum_ref)

    dx_ref[0] = space_back_rows(
        x_ref[0].astype(F32), g_ref[0], qkv_ref, pt_ref.at[0], vec_ref, wqkv_ref, wo_ref, dp_ref, sum_ref
    )


def probs_spec(rows):
    return pl.BlockSpec((1, HEADS // 2, 2 * rows, rows), lambda b: (b, 0, 0, 0))


def space_fwd(x, vec, wqkv, wo):
    blocks, rows, width = x.shape
    tok = blocks * rows
    seq = pl.BlockSpec((1, rows, width), lambda b: (b, 0, 0))
    return pl.pallas_call(
        space_kernel,
        grid=(blocks,),
        in_specs=[seq, whole(vec.shape), whole(wqkv.shape), whole(wo.shape)],
        out_specs=[seq, rows_spec(rows, width), rows_spec(rows, 3 * width), probs_spec(rows), rows_spec(rows, width)],
        out_shape=[
            sds(*x.shape), sds(tok, width), sds(tok, 3 * width), sds(blocks, HEADS // 2, 2 * rows, rows), sds(tok, width)
        ],
        compiler_params=params(),
        name="space_fwd",
    )(x, vec, wqkv, wo)


def place_all(x1, g, vec, wqkv, wo, win, wout):
    clips, frames, places, width = x1.shape
    rows = 256
    part = rows // frames
    per = places // part
    blocks = clips * per
    tok = blocks * rows
    ff = win.shape[1]
    spec = pl.BlockSpec((1, frames, part, width), lambda b: (b // per, 0, b % per, 0))
    n = rows_spec(rows, width)
    return pl.pallas_call(
        place_kernel,
        grid=(blocks,),
        in_specs=[spec, spec] + [whole(w.shape) for w in (vec, wqkv, wo, win, wout)],
        out_specs=[
            spec, spec, n, rows_spec(rows, 3 * width), n, n, n, rows_spec(rows, ff), rows_spec(rows, ff),
            pl.BlockSpec((SUM_ROWS, 8, width), lambda b: (0, 0, 0)),
        ],
        out_shape=[
            sds(*x1.shape), sds(*x1.shape), sds(tok, width), sds(tok, 3 * width), sds(tok, width), sds(tok, width),
            sds(tok, width), sds(tok, ff), sds(tok, ff), sds(SUM_ROWS, 8, width, dtype=F32),
        ],
        scratch_shapes=[pltpu.VMEM((rows, 3 * width), BF16), pltpu.VMEM((HEADS // 2, 2 * rows, rows), BF16)],
        compiler_params=params(),
        name="place_all",
    )(x1, g, vec, wqkv, wo, win, wout)


def space_bwd(x, g, qkv, pt, vec, wqkv, wo):
    blocks, rows, width = x.shape
    tok = blocks * rows
    seq = pl.BlockSpec((1, rows, width), lambda b: (b, 0, 0))
    return pl.pallas_call(
        space_back_kernel,
        grid=(blocks,),
        in_specs=[
            seq, seq, rows_spec(rows, 3 * width), probs_spec(rows), whole(vec.shape), whole(wqkv.shape), whole(wo.shape)
        ],
        out_specs=[seq, rows_spec(rows, 3 * width), pl.BlockSpec((SUM_ROWS, 8, width), lambda b: (0, 0, 0))],
        out_shape=[sds(*x.shape), sds(tok, 3 * width), sds(SUM_ROWS, 8, width, dtype=F32)],
        compiler_params=params(),
        name="space_bwd",
    )(x, g, qkv, pt, vec, wqkv, wo)


def outer_sum(left, right):
    return lax.dot_general(left, right, (((0,), (0,)), ((), ())), preferred_element_type=F32)


def plain_layer(inputs, cotangent, shards, vec):
    clips, frames, places, width = inputs.shape

    def out_there(rows):
        return lax.all_to_all(rows, "seq", split_axis=2, concat_axis=1, tiled=True)

    def back_home(rows):
        return lax.all_to_all(rows, "seq", split_axis=1, concat_axis=2, tiled=True)

    wqkv, wo, tqkv, to, win, wout = [lax.all_gather(s, ("dp", "seq"), axis=0, tiled=True) for s in shards]
    vec = lax.psum(vec, ("dp", "seq"))
    x = inputs.reshape(clips * frames, places, width)
    cot = out_there(cotangent)
    x1, a1, qkv, pt, o = space_fwd(x, vec, wqkv, wo)
    x1 = out_there(x1.reshape(inputs.shape))
    out, dx1, a2, dp, ot, gt, a3, z, dh, sums = place_all(x1, cot, vec, tqkv, to, win, wout)
    output = back_home(out)
    g1 = back_home(dx1).reshape(x.shape)
    dx, dps, space_sums = space_bwd(x, g1, qkv, pt, vec, wqkv, wo)
    part = 256 // cot.shape[1]
    g = cot.reshape(clips, cot.shape[1], -1, part, width).transpose(0, 2, 1, 3, 4).reshape(-1, width)
    pairs = ((a1, dps), (o, g1.reshape(-1, width)), (a2, dp), (ot, gt), (a3, dh), (z, g))
    grads = []
    for left, right in pairs:
        part = lax.psum_scatter(outer_sum(left, right).astype(BF16), "dp", scatter_dimension=0, tiled=True)
        grads.append(lax.psum_scatter(part, "seq", scatter_dimension=0, tiled=True).astype(F32))
    return output, dx.reshape(inputs.shape), grads, lax.psum((sums + space_sums).sum(1), ("dp", "seq"))


MESH = pl.DeviceIdType.MESH


def position():
    d, z = lax.axis_index("dp"), lax.axis_index("seq")
    return d // 4, lax.rem(d // 2, 2), lax.rem(d, 2), z


def partner(z):
    return z + 1 - 2 * lax.rem(z, 2)


def partners():
    y, x, c, z = position()
    return {
        "x": (4 * y + 2 * (1 - x) + c, z),
        "y": (4 * (1 - y) + 2 * x + c, z),
        "core": (4 * y + 2 * x + 1 - c, z),
        "pair": (4 * y + 2 * x + c, partner(z)),
        "across": (4 * y + 2 * x + c, 3 - z),
        "z1": (4 * y + 2 * x + c, lax.rem(z + 1, 4)),
        "z2": (4 * y + 2 * x + c, lax.rem(z + 2, 4)),
        "z3": (4 * y + 2 * x + c, lax.rem(z + 3, 4)),
    }


def enter(peers):
    barrier = pltpu.get_barrier_semaphore()
    greeted = [peer for kind, peer in peers.items() if kind not in ("pair", "across")]
    for peer in greeted:
        pl.semaphore_signal(barrier, inc=1, device_id=peer, device_id_type=MESH)
    pl.semaphore_wait(barrier, len(greeted))


class Sum:
    def __init__(self, peers, held, got, send, recv):
        self.peers, self.held, self.got, self.send, self.recv = peers, held, got, send, recv

    def copy(self, i, kind, level):
        return pltpu.make_async_remote_copy(
            src_ref=self.held.at[level], dst_ref=self.got.at[i], send_sem=self.send.at[i], recv_sem=self.recv.at[i],
            device_id=self.peers[kind], device_id_type=MESH,
        )

    STAGES = ((("z1", 0), ("z2", 1), ("z3", 2)), (("x", 3),), (("y", 4),), (("core", 5),))

    def start(self, level):
        for kind, i in self.STAGES[level]:
            self.copy(i, kind, level).start()

    def finish(self, level):
        total = self.held[level].astype(F32)
        for kind, i in self.STAGES[level]:
            self.copy(i, kind, level).wait_recv()
            total = total + self.got[i].astype(F32)
        self.held[level + 1] = total.astype(self.held.dtype)

    def drain(self):
        for level, stage in enumerate(self.STAGES):
            for kind, i in stage:
                self.copy(i, kind, level).wait_send()


class Gather:
    def __init__(self, peers, direct, shard, zbuf, group, full, local, send, recv):
        self.peers, self.shard, self.zbuf, self.group, self.full = peers, shard, zbuf, group, full
        self.local, self.send, self.recv = local, send, recv
        self.direct = direct
        self.rows, self.cols = group.shape
        z = lax.axis_index("seq")
        self.inner = (z == 1) | (z == 2)

    def place(self, which, half):
        y, x, c, _ = position()
        y, x = {"own": (y, x), "x": (y, 1 - x), "y": (1 - y, x), "xy": (1 - y, 1 - x)}[which]
        rows = pl.ds(pl.multiple_of((4 * y + 2 * x + c) * self.rows, self.rows), self.rows)
        n = self.cols // 2
        return (rows, pl.ds(0, self.cols)) if half is None else (rows, pl.ds(half * n, n))

    PLAN = {
        5: ("own", 0, "x"), 6: ("own", 1, "y"), 7: ("own", 0, "y"), 8: ("x", 0, "y"), 9: ("own", 1, "x"), 10: ("y", 1, "x"),
        11: ("own", None, "core"), 12: ("x", 0, "core"), 13: ("y", 1, "core"), 14: ("y", 0, "core"), 15: ("xy", 0, "core"),
        16: ("x", 1, "core"), 17: ("xy", 1, "core"),
    }

    def copy(self, i):
        if i < 5:
            z = lax.axis_index("seq")
            if self.direct:
                return self.remote(self.shard, self.zbuf.at[z], i, ("z1", "z2", "z3")[i])
            whose = (z, z, partner(z), 3 - z, partner(3 - z))[i]
            dst = self.zbuf.at[whose]
            src = self.shard if i < 2 else dst
            kind = ("pair", "across", "across", "pair", "pair")[i]
        else:
            which, half, kind = self.PLAN[i]
            at = self.place(which, half)
            src = dst = self.full.at[at]
            if which == "own":
                src = self.group if half is None else self.group.at[:, pl.ds(half * (self.cols // 2), self.cols // 2)]
        return self.remote(src, dst, i, kind)

    def remote(self, src, dst, i, kind):
        return pltpu.make_async_remote_copy(
            src_ref=src, dst_ref=dst, send_sem=self.send.at[i], recv_sem=self.recv.at[i], device_id=self.peers[kind],
            device_id_type=MESH,
        )

    def own_in(self):
        return pltpu.make_async_copy(self.shard, self.zbuf.at[lax.axis_index("seq")], self.local.at[0])

    def own_out(self):
        return pltpu.make_async_copy(self.group, self.full.at[self.place("own", None)], self.local.at[1])

    def start(self, items):
        for i in items:
            self.copy(i).start()

    def arrive(self, items):
        for i in items:
            self.copy(i).wait_recv()

    def step0(self):
        self.own_in().start()
        if self.direct:
            self.start((0, 1, 2))
            return
        self.start((0,))

        @pl.when(self.inner)
        def _():
            self.start((1,))

    def stepa(self):
        self.arrive((0,))

        @pl.when(self.inner)
        def _():
            self.start((2,))

    def stepb(self):
        @pl.when(self.inner)
        def _():
            self.arrive((1,))
            self.start((3,))
            self.arrive((2,))
            self.start((4,))

    def step1(self):
        if self.direct:
            self.arrive((0, 1, 2))
        else:

            @pl.when(jnp.logical_not(self.inner))
            def _():
                self.arrive((3, 4))

        self.own_in().wait()
        self.group[...] = jnp.concatenate([self.zbuf[i].astype(F32) for i in range(4)], axis=0).astype(BF16)
        self.own_out().start()
        self.start((5, 6, 7, 9, 11))

    def step2(self):
        self.arrive((5, 6))
        self.start((8, 10, 12, 13))

    def step3(self):
        self.arrive((7, 9, 8, 10))
        self.start((14, 16, 15, 17))

    def step4(self):
        self.arrive((11, 12, 13, 14, 16, 15, 17))
        self.own_out().wait()

    def drain(self):
        for i in (*range(3 if self.direct else 1), *range(5, 18)):
            self.copy(i).wait_send()
        if self.direct:
            return

        @pl.when(self.inner)
        def _():
            for i in range(1, 5):
                self.copy(i).wait_send()


class Swap:
    def __init__(self, peers, pick, land, local, send, recv):
        self.peers, self.pick, self.land, self.local, self.send, self.recv = peers, pick, land, local, send, recv

    def copies(self):
        z = lax.axis_index("seq")
        for j in range(3):
            yield pltpu.make_async_remote_copy(
                src_ref=self.pick(lax.rem(z + j + 1, 4)), dst_ref=self.land, send_sem=self.send.at[j], recv_sem=self.recv.at[j],
                device_id=self.peers[f"z{j + 1}"], device_id_type=MESH,
            )

    def own(self):
        return pltpu.make_async_copy(self.pick(lax.axis_index("seq")), self.land, self.local)

    def start(self):
        for copy in self.copies():
            copy.start()
        if self.local is not None:
            self.own().start()

    def arrive(self):
        for copy in self.copies():
            copy.wait_recv()
        if self.local is not None:
            self.own().wait()

    def drain(self):
        for copy in self.copies():
            copy.wait_send()


def rows_at(start, size):
    return pl.ds(pl.multiple_of(start, size), size)


GATHERED = ((0, 0), (0, 1), (0, 2), (1, 0), (2, 0), (2, 1), (2, 2), (3, 0), (5, 0), (4, 0), (4, 1), (4, 2), (4, 3))
BEFORE = {
    0: (0, 1, 2, 3, 300, 301, 4, 5, 400, 6, 302, 7, 8, 401, 303, 104, 105, 500, 106, 402, 107, 9, 600, 108, 501, 403, 204, 109, 10, 601, 205, 206, 11, 502, 207, 503, 304, 110, 12, 602, 208, 603),
    1: (404, 305, 306, 209, 210, 111, 112),
    2: (504, 405, 307),
    3: (604, 406, 308, 211, 212, 505, 407),
    4: (605, 506),
    5: (606,),
    6: (408,),
    7: (507, 309),
}
EARLY = (310, 311, 312, 607)
LATE = (508, 409, 410, 608, 411, 412, 509, 510, 609, 511, 610, 512, 611, 612)
VEC_AT = (300, 302, 401, 501)
AFTER_SPACE = {0: (0,), 1: (1,), 2: (2,), 3: (3,), 7: (100,)}
AT_PLACE = {
    (0, 0): (101,), (0, 1): (4,), (0, 2): (102,), (1, 0): (5,), (1, 2): (103,),
    (2, 0): (6,), (2, 2): (7,), (3, 0): (104,), (3, 2): (105,), (4, 0): (106,),
    (4, 2): (107,), (5, 2): (200,), (6, 0): (201,), (6, 2): (202,), (7, 0): (203,), (7, 2): (204,),
}
KEPT = 5


def front_kernel(x_ref, vec_ref, cot_ref, *refs):
    shards = refs[:6]
    a_ref, qkv_ref, pt_ref, o_ref = refs[6:10]
    land_ref, home_ref, wqkv_out, wo_out, vec_out = refs[10:15]
    out_all, out_home, rest_all, g_ref = refs[15:19]
    kept_refs = refs[19:27]
    sum_ref = kept_refs[7]
    weights = refs[27:33]
    x1_ref, tqkv_ref, tpt_ref, gland, dx1_ref, xin, out_ref = refs[33:40]
    count = len(GATHERED)
    refs = refs[40:]
    zbufs, groups = refs[:count], refs[count : 2 * count]
    held, got, local, send, recv, vsend, vrecv, keep, xlocal, xsend, xrecv = refs[2 * count : 2 * count + 11]
    glocal, gsend, grecv, dlocal, dsend, drecv, xload, gkeep, okeep, dkeep = refs[2 * count + 11 :]
    step = pl.program_id(0)
    blocks, rows, width = x1_ref.shape
    _, frames, part, _ = gland.shape
    clips, per, places, _ = cot_ref.shape
    chunks, mine = blocks // clips, places // 4
    z = lax.axis_index("seq")
    peers = partners()
    vec = Sum(peers, held, got, vsend, vrecv)

    def piece(u):
        w, at = GATHERED[u]
        return (ref.at[:, pl.ds(at * width, width)] for ref in (shards[w], weights[w]))

    work = []
    for u in range(count):
        shard, full = piece(u)
        work.append(Gather(peers, u < 4, shard, zbufs[u], groups[u], full, local.at[u], send.at[u], recv.at[u]))

    def swap_x1(b):
        return Swap(
            peers, lambda to: x1_ref.at[b, rows_at(to * mine, mine)], land_ref.at[b // per, z * per + lax.rem(b, per)],
            xlocal.at[b], xsend.at[b], xrecv.at[b],
        )

    def swap_cot(b):
        return Swap(
            peers, lambda to: cot_ref.at[b // chunks, :, rows_at(to * mine + (b % chunks) * part, part)],
            gland.at[b, pl.ds(z * per, per)], glocal.at[b], gsend.at[b], grecv.at[b],
        )

    def swap_dx1(b):
        return Swap(
            peers, lambda to: dx1_ref.at[b, pl.ds(to * per, per)],
            home_ref.at[b // chunks, :, rows_at(z * mine + (b % chunks) * part, part)], dlocal.at[b], dsend.at[b], drecv.at[b],
        )

    def out_copies(b):
        own = out_home.at[b // chunks, :, rows_at(z * mine + (b % chunks) * part, part)]
        return (
            pltpu.make_async_copy(out_ref.at[b % 2], out_all.at[b], okeep.at[b % 2, 0]),
            pltpu.make_async_copy(out_ref.at[b % 2, pl.ds(z * per, per)], own, okeep.at[b % 2, 1]),
        )

    def dx1_copies(b):
        own = home_ref.at[b // chunks, :, rows_at(z * mine + (b % chunks) * part, part)]
        return (
            pltpu.make_async_copy(dx1_ref.at[KEPT + b % 2], rest_all.at[b - KEPT], dkeep.at[b % 2, 0]),
            pltpu.make_async_copy(dx1_ref.at[KEPT + b % 2, pl.ds(z * per, per)], own, dkeep.at[b % 2, 1]),
        )

    def load_x1(b):
        src = land_ref.at[b // chunks, :, rows_at((b % chunks) * part, part)]
        return pltpu.make_async_copy(src, xin.at[b % 2], xload.at[b % 2])

    def g_out(b):
        return pltpu.make_async_copy(gland.at[b], g_ref.at[b], gkeep.at[b])

    def kept(i):
        return pltpu.make_async_copy(weights[i], (wqkv_out, wo_out)[i], keep.at[i])

    def event(code):
        w = work[code % 100]
        (w.step0, w.stepa, w.stepb, w.step1, w.step2, w.step3, w.step4)[code // 100]()

    @pl.when(step == 0)
    def _():
        sum_ref[...] = jnp.zeros_like(sum_ref)
        held[0] = vec_ref[...]
        enter(peers)
        vec.start(0)
        for name in BEFORE[0]:
            event(name)
            if name in VEC_AT:
                level = VEC_AT.index(name)
                vec.finish(level)
                if level < 3:
                    vec.start(level + 1)
        vec_out[...] = held[4].astype(F32)
        kept(0).start()
        kept(1).start()

    for k in range(1, 8):

        @pl.when(step == k)
        def _(k=k):
            for name in BEFORE[k]:
                event(name)

    def exchange(code):
        (swap_x1, swap_cot, swap_dx1)[code // 100](code % 100).start()

    def at(point):
        for (b, where), names in AT_PLACE.items():
            if where == point:

                @pl.when(step == blocks + b)
                def _(names=names):
                    for name in names:
                        exchange(name)

    @pl.when(step < blocks)
    def _():
        x1_ref[step] = space_rows(
            x_ref[0].astype(F32), vec_out, weights[0], weights[1], a_ref, qkv_ref, pt_ref.at[0], o_ref
        )

        for k, names in AFTER_SPACE.items():

            @pl.when(step == k)
            def _(names=names):
                for name in names:
                    exchange(name)

    @pl.when(step >= blocks)
    def _():
        b = step - blocks
        slot = lax.rem(b, 2)
        at(0)

        @pl.when(b == 0)
        def _():
            for name in EARLY:
                event(name)

        @pl.when(lax.rem(b, chunks) == 0)
        def _():
            def arrived(k, _):
                swap_x1((b // chunks) * per + k).arrive()
                return 0

            lax.fori_loop(0, per, arrived, 0)
            load_x1(b).start()

        load_x1(b).wait()

        @pl.when(lax.rem(b, chunks) < chunks - 1)
        def _():
            load_x1(b + 1).start()

        def take_g():
            at(1)

            @pl.when(b == 0)
            def _():
                for name in LATE:
                    event(name)

            swap_cot(b).arrive()
            g_out(b).start()
            return gland[b].reshape(rows, width)

        x1 = xin[slot].reshape(rows, width).astype(F32)
        out, dx1 = place_rows(x1, take_g, lambda: at(2), part, vec_out, *weights[2:], *kept_refs, tqkv_ref, tpt_ref)

        @pl.when(b >= 2)
        def _():
            for copy in out_copies(b - 2):
                copy.wait()

        out_ref[slot] = out.reshape(frames, part, width)
        for copy in out_copies(b):
            copy.start()

        @pl.when(b >= KEPT + 2)
        def _():
            for copy in dx1_copies(b - 2):
                copy.wait()

        dx1_ref[jnp.where(b < KEPT, b, KEPT + slot)] = dx1.reshape(frames, part, width)

        @pl.when(b >= KEPT)
        def _():
            for copy in dx1_copies(b):
                copy.start()

    @pl.when(step == 2 * blocks - 1)
    def _():
        kept(0).wait()
        kept(1).wait()
        vec.drain()
        for w in work:
            w.drain()

        def finish(b, _):
            swap_x1(b).drain()
            swap_cot(b).drain()
            g_out(b).wait()
            return 0

        lax.fori_loop(0, blocks, finish, 0)

        for b in (blocks - 2, blocks - 1):
            for copy in out_copies(b) + dx1_copies(b):
                copy.wait()

        def finish_dx1(b, _):
            swap_dx1(b).arrive()
            swap_dx1(b).drain()
            return 0

        lax.fori_loop(0, KEPT, finish_dx1, 0)


def front(x, cot, vec, shards):
    blocks, rows, width = x.shape
    clips, per, places, _ = cot.shape
    frames = 4 * per
    part = rows // frames
    tok = blocks * rows
    count = len(GATHERED)
    dma = pltpu.SemaphoreType.DMA

    def one(s):
        return jnp.minimum(s, blocks - 1)

    def two(s):
        return jnp.maximum(s - blocks, 0)

    def early(*shape):
        return pl.BlockSpec(shape, lambda s: (one(s),) + (0,) * (len(shape) - 1))

    def late(*shape):
        return pl.BlockSpec(shape, lambda s: (two(s),) + (0,) * (len(shape) - 1))

    fixed = pl.BlockSpec((VEC_ROWS, width), lambda s: (0, 0))
    full = [(32 * s.shape[0], s.shape[1]) for s in shards]
    ff = full[4][1]
    place = (blocks, frames, part, width)
    token_widths = (width, 3 * width, width, width, width, ff, ff)
    out = pl.pallas_call(
        front_kernel,
        grid=(2 * blocks,),
        in_specs=[early(1, rows, width), whole(vec.shape)] + [ANYWHERE] * 7,
        out_specs=[
            early(rows, width), early(rows, 3 * width), early(1, HEADS // 2, 2 * rows, rows), early(rows, width),
            ANYWHERE, ANYWHERE, ANYWHERE, ANYWHERE, fixed, ANYWHERE, ANYWHERE, ANYWHERE, ANYWHERE,
        ] + [late(rows, w) for w in token_widths] + [pl.BlockSpec((SUM_ROWS, 8, width), lambda s: (0, 0, 0))],
        out_shape=[
            sds(tok, width), sds(tok, 3 * width), sds(blocks, HEADS // 2, 2 * rows, rows), sds(tok, width),
            sds(clips, frames, places // 4, width), sds(*cot.shape), sds(*full[0]), sds(*full[1]),
            sds(VEC_ROWS, width, dtype=F32), sds(*place), sds(*cot.shape), sds(blocks - KEPT, *place[1:]),
            sds(*place),
        ] + [sds(tok, w) for w in token_widths] + [sds(SUM_ROWS, 8, width, dtype=F32)],
        scratch_shapes=[pltpu.VMEM(s, BF16) for s in full]
        + [
            pltpu.VMEM((blocks, rows, width), BF16), pltpu.VMEM((rows, 3 * width), BF16),
            pltpu.VMEM((HEADS // 2, 2 * rows, rows), BF16), pltpu.VMEM(place, BF16),
            pltpu.VMEM((KEPT + 2, *place[1:]), BF16), pltpu.VMEM((2, *place[1:]), BF16), pltpu.VMEM((2, *place[1:]), BF16),
        ]
        + [pltpu.VMEM((4, shards[w].shape[0], width), BF16) for w, _ in GATHERED]
        + [pltpu.VMEM((4 * shards[w].shape[0], width), BF16) for w, _ in GATHERED]
        + [
            pltpu.VMEM((5, *vec.shape), BF16), pltpu.VMEM((6, *vec.shape), BF16), dma((count, 2)), dma((count, 18)),
            dma((count, 18)), dma((6,)), dma((6,)), dma((2,)), dma((blocks,)), dma((blocks, 3)), dma((blocks, 3)),
            dma((blocks,)), dma((blocks, 3)), dma((blocks, 3)), dma((KEPT,)), dma((KEPT, 3)), dma((KEPT, 3)), dma((2,)), dma((blocks,)),
            dma((2, 2)), dma((2, 2)),
        ],
        compiler_params=params(0),
        name="front",
    )(x, vec.astype(BF16), cot, *shards)
    return out[:4], out[5], out[6:8], out[8], out[9:12], out[12:]


class Scatter:
    def __init__(self, peers, direct, piece, core, first, second, zsend, zgot, out, send, recv):
        self.peers, self.piece, self.core = peers, piece, core
        self.first, self.second, self.zsend, self.zgot, self.out = first, second, zsend, zgot, out
        self.send, self.recv = send, recv
        self.direct = direct
        z = lax.axis_index("seq")
        self.inner = (z == 1) | (z == 2)
        self.rows, self.half = core.shape[1], core.shape[2] // 2

    def block(self, i, c):
        return rows_at((2 * i + c) * self.rows, self.rows)

    def copy(self, i):
        y, x, c, z = position()
        if i < 4:
            src, dst, kind = self.piece.at[self.block(i, 1 - c)], self.core.at[i], "core"
        elif i < 6:
            src, dst, kind = self.core.at[2 * (i - 4) + 1 - x, :, pl.ds(0, self.half)], self.first.at[0, i - 4], "x"
        elif i < 8:
            src, dst, kind = self.core.at[2 * (1 - y) + i - 6, :, pl.ds(self.half, self.half)], self.first.at[1, i - 6], "y"
        elif i == 8:
            src, dst, kind = self.first.at[0, 1 - y], self.second.at[0], "y"
        elif i == 9:
            src, dst, kind = self.first.at[1, 1 - x], self.second.at[1], "x"
        elif self.direct:
            j = i - 9
            src, dst, kind = self.zsend.at[lax.rem(z + j, 4)], self.zgot.at[j - 1], f"z{j}"
        else:
            near, far = partner(z), 3 - partner(z)
            whose = (near, far, partner(far), 3 - z, partner(3 - z), near)[i - 10]
            src, dst = self.zsend.at[whose], self.zgot.at[(0, 1, 2, 3, 4, 0)[i - 10]]
            kind = "across" if i in (13, 14) else "pair"
        return pltpu.make_async_remote_copy(
            src_ref=src, dst_ref=dst, send_sem=self.send.at[i], recv_sem=self.recv.at[i], device_id=self.peers[kind],
            device_id_type=MESH,
        )

    def start(self, items):
        for i in items:
            self.copy(i).start()

    def arrive(self, items):
        for i in items:
            self.copy(i).wait_recv()

    def sent(self, items):
        for i in items:
            self.copy(i).wait_send()

    def step0(self):
        self.start(range(4))

    def step1(self):
        _, _, c, _ = position()
        self.arrive(range(4))

        def add(i, _):
            self.core[i] = self.piece[self.block(i, c)] + self.core[i]
            return 0

        lax.fori_loop(0, 4, add, 0)
        self.start(range(4, 8))
        self.sent(range(4))

    def step2(self):
        y, x, _, _ = position()
        n = self.half
        self.arrive(range(4, 8))
        for i in range(2):
            self.first[0, i] = self.first[0, i] + self.core[2 * i + x, :, :n]
            self.first[1, i] = self.first[1, i] + self.core[2 * y + i, :, n:]
        self.start((8, 9))

    def step3(self):
        y, x, _, _ = position()
        self.arrive((8, 9))
        r = self.zsend.shape[1]
        for k, at in ((0, y), (1, x)):
            total = self.first[k, at].astype(F32) + self.second[k].astype(F32)
            for i in range(4):
                self.zsend[i, :, k * self.half : (k + 1) * self.half] = total[i * r : (i + 1) * r].astype(BF16)
        if self.direct:
            self.start((10, 11, 12))
            return

        @pl.when(jnp.logical_not(self.inner))
        def _():
            self.start((10, 11, 12))

    def stepb(self):
        @pl.when(self.inner)
        def _():
            z = lax.axis_index("seq")
            self.arrive((10, 11, 12))
            for whose, i in ((3 - z, 1), (partner(3 - z), 2)):
                self.zsend[whose] = self.zsend[whose] + self.zgot[i]
            self.start((13, 14))

    def stepc(self):
        @pl.when(self.inner)
        def _():
            z = lax.axis_index("seq")
            self.arrive((13, 14))
            near = partner(z)
            self.zsend[near] = self.zsend[near] + self.zgot[4]
            self.start((15,))

    def step4(self):
        z = lax.axis_index("seq")
        if self.direct:
            self.arrive((10, 11, 12))
            total = self.zsend[z].astype(F32)
            for i in range(3):
                total = total + self.zgot[i].astype(F32)
            self.out[...] = total
            self.sent((10, 11, 12))
            return

        @pl.when(self.inner)
        def _():
            self.out[...] = self.zsend[z].astype(F32) + self.zgot[0].astype(F32) + self.zgot[3].astype(F32)
            self.sent((13, 14, 15))

        @pl.when(jnp.logical_not(self.inner))
        def _():
            self.arrive((15,))
            self.out[...] = self.zsend[z].astype(F32) + self.zgot[0].astype(F32)
            self.sent((10, 11, 12))

    def drain(self):
        self.sent(range(4, 10))


PANELS, BLOCKS, UNITS, SLOTS = 11, 8, 16, 6
CHAINED = 8
STEPS = PANELS + BLOCKS + UNITS - PANELS
AFTER_STEP = {
    3: (0, 1, 2, 3),
    4: (4,),
    5: (5, 100),
    6: (6, 101),
    7: (7, 102),
    8: (8, 103, 200, 201),
    9: (9, 104, 202),
    10: (10, 203),
    11: (105, 300, 301, 204),
    12: (106, 302, 303, 107),
    13: (205, 108, 304),
    14: (206, 207, 109, 305),
    15: (208, 110, 306),
    16: (209, 400, 401, 307),
    17: (210, 402, 403),
    18: (404,),
    19: (11, 405),
    20: (12,),
    21: (13, 111, 406),
    22: (14, 112, 500, 501, 407, 113, 506),
    23: (15, 211, 502, 503, 600, 601, 606, 114, 507, 308, 309, 212),
}
TAIL = (602, 310, 603, 504, 505, 607, 115, 213, 311, 604, 605, 214, 312, 608, 609, 215, 313, 314, 612, 315, 610, 611, 613, 614, 615)
OUT_AT = (6, 9, 11, 13, 15, 17, 19, 21)


def last_kernel(
    x_ref, qkv_ref, pt_ref, vec_ref, sums_ref, wqkv_ref, wo_ref, z_ref, g_ref, a3_ref, dh_ref, ot_ref, gt_ref, a2_ref,
    dp_ref, a1_ref, o_ref, rest_ref, out_ref, g1_in_place, out_in_place, dx_ref, sqkv_out, so_out, tqkv_out, to_out, win_out, wout_out, vec_out, home_ref,
    dps_ref, g1_home, lbuf, rbuf, pieces, core, one, two, zsend, zgot, dpbuf, gbuf, ssum, held, got, lsem, rsem, send, recv, vsend, vrecv,
    dpsem, gsem, osend, orecv, rsend, rrecv,
):
    step = pl.program_id(0)
    z = lax.axis_index("seq")
    peers = partners()
    width = x_ref.shape[2]
    rows = core.shape[2]
    small = zsend.shape[2]
    blocks, frames, part, _ = out_ref.shape
    clips, per, places, _ = home_ref.shape
    chunks, mine = blocks // clips, places // 4
    vec = Sum(peers, held, got, vsend, vrecv)

    def columns(i):
        return pl.ds(pl.multiple_of(i * width, width), width)

    def out_of(u):
        if u < 4:
            return wout_out.at[pl.ds(u * small, small)]
        if u == 8:
            return to_out
        if u == 12:
            return so_out
        ref, i = (win_out, u - 4) if u < 8 else (tqkv_out, u - 9) if u < 12 else (sqkv_out, u - 13)
        return ref.at[:, pl.ds(i * width, width)]

    work = [
        Scatter(
            peers, u >= CHAINED, pieces.at[u % SLOTS], core.at[u], one.at[u], two.at[u], zsend.at[u % 8], zgot.at[u], out_of(u), send.at[u],
            recv.at[u],
        )
        for u in range(UNITS)
    ]

    def event(code):
        w = work[code % 100]
        (w.step0, w.step1, w.step2, w.step3, w.stepb, w.stepc, w.step4)[code // 100]()

    def swap(b):
        return Swap(
            peers, lambda to: out_ref.at[b, pl.ds(to * per, per)],
            home_ref.at[b // chunks, :, rows_at(z * mine + (b % chunks) * part, part)], None, osend.at[b], orecv.at[b],
        )

    def rest(b):
        return Swap(
            peers, lambda to: rest_ref.at[b - KEPT, pl.ds(to * per, per)],
            g1_home.at[b // chunks, :, rows_at(z * mine + (b % chunks) * part, part)], None, rsend.at[b - KEPT],
            rrecv.at[b - KEPT],
        )

    def load(ref, at, buf, sem, slot):
        src = ref if at is None else ref.at[:, columns(at)]
        return pltpu.make_async_copy(src, buf.at[slot], sem.at[slot])

    def fetch(p, left, l_at, right, r_at):
        slot = lax.rem(p, 2)
        load(left, l_at, lbuf, lsem, slot).start()
        if right is g1_home:
            n = x_ref.shape[1]
            for b in range(clips * per):
                src = g1_home.at[b // per, b % per]
                pltpu.make_async_copy(src, rbuf.at[slot, pl.ds(b * n, n)], rsem.at[slot]).start()
        else:
            load(right, r_at, rbuf, rsem, slot).start()

    def fetch_panel(p):
        for least, most, left, right, which in (
            (0, 4, z_ref, g_ref, "l"), (4, 8, a3_ref, dh_ref, "r"), (8, 9, ot_ref, gt_ref, ""), (9, 12, a2_ref, dp_ref, "r"),
            (12, 13, o_ref, g1_home, ""), (13, 16, a1_ref, dps_ref, "r"),
        ):

            @pl.when((p >= least) & (p < most))
            def _():
                at = p - least
                fetch(p, left, at if which == "l" else None, right, at if which == "r" else None)

    def dp_out(b):
        return pltpu.make_async_copy(dpbuf.at[b % 2], dps_ref.at[rows_at(b * x_ref.shape[1], x_ref.shape[1])], dpsem.at[b % 2])

    def g1_in(b):
        return pltpu.make_async_copy(g1_home.at[b // per, b % per], gbuf.at[b % 2], gsem.at[b % 2])

    is_block = (step >= PANELS) & (step < PANELS + BLOCKS)
    panel = jnp.where(step < PANELS, step, step - BLOCKS)

    @pl.when(step == 0)
    def _():
        ssum[...] = sums_ref[...]
        fetch_panel(step)
        enter(peers)
        for b in range(KEPT, blocks):
            rest(b).start()

    for b, at in enumerate(OUT_AT):

        @pl.when(step == at)
        def _(b=b):
            swap(b).start()

    @pl.when((step < PANELS - 1) | (step >= PANELS + BLOCKS - 1) & (step < STEPS - 1))
    def _():
        fetch_panel(jnp.where(step < PANELS, step + 1, step + 1 - BLOCKS))

    @pl.when(jnp.logical_not(is_block))
    def _():
        slot = lax.rem(panel, 2)
        load(z_ref, 0, lbuf, lsem, slot).wait()
        load(z_ref, 0, rbuf, rsem, slot).wait()
        total = outer_sum(lbuf[slot], rbuf[slot])

        @pl.when(panel >= 4)
        def _():
            pieces[lax.rem(panel, SLOTS)] = total.astype(BF16)

        @pl.when(panel < 4)
        def _():
            cut = total.reshape(2, 4, 4, small, width)
            for d in range(2):
                for i in range(4):
                    both = jnp.concatenate([cut[d, k, i] for k in range(4)], axis=0)
                    pieces[i, rows_at((2 * panel + d) * rows, rows)] = both.astype(BF16)

    @pl.when(is_block)
    def _():
        b = step - PANELS

        @pl.when(b >= 2)
        def _():
            dp_out(b - 2).wait()

        slot = lax.rem(b, 2)

        @pl.when(b == 0)
        def _():
            g1_in(b).start()

        @pl.when(b == per - 1)
        def _():
            for k in range(KEPT, blocks):
                rest(k).arrive()

        g1_in(b).wait()

        @pl.when(b < BLOCKS - 1)
        def _():
            g1_in(b + 1).start()

        dx_ref[0] = space_back_rows(
            x_ref[0].astype(F32), gbuf[slot], qkv_ref, pt_ref.at[0], vec_ref, wqkv_ref, wo_ref, dpbuf.at[lax.rem(b, 2)], ssum
        )
        dp_out(b).start()

    @pl.when(step == PANELS + BLOCKS - 1)
    def _():
        dp_out(step - PANELS - 1).wait()
        dp_out(step - PANELS).wait()
        held[0] = jnp.concatenate([jnp.sum(ssum[i], axis=0, keepdims=True) for i in range(SUM_ROWS)], axis=0)
        vec.start(0)

    for k, names in AFTER_STEP.items():

        @pl.when(step == k)
        def _(k=k, names=names):
            for name in names:
                event(name)
            if k >= PANELS + BLOCKS:
                level = k - PANELS - BLOCKS
                if level < 4:
                    vec.finish(level)
                if level < 3:
                    vec.start(level + 1)

    @pl.when(step == STEPS - 1)
    def _():
        for name in TAIL:
            event(name)
        vec_out[...] = held[4]
        vec.drain()
        for b in range(KEPT, blocks):
            rest(b).drain()
        for w in work:
            w.drain()

        def finish(b, _):
            swap(b).arrive()
            swap(b).drain()
            return 0

        lax.fori_loop(0, blocks, finish, 0)


def last(x, home, outs, saved, vec, wqkv, wo, shapes):
    z, g, a3, dh, ot, gt, a2, dp, a1, o, qkv, pt, sums = saved
    out, out_home, rest = outs
    blocks, rows, width = x.shape
    tok = blocks * rows
    dma = pltpu.SemaphoreType.DMA
    in_vmem = pl.BlockSpec(memory_space=pltpu.VMEM)

    def at(s):
        return jnp.minimum(jnp.maximum(s - PANELS, 0), BLOCKS - 1)

    seq = pl.BlockSpec((1, rows, width), lambda s: (at(s), 0, 0))
    small = width // 32
    result = pl.pallas_call(
        last_kernel,
        grid=(STEPS,),
        in_specs=[
            seq, pl.BlockSpec((rows, 3 * width), lambda s: (at(s), 0)),
            pl.BlockSpec((1, HEADS // 2, 2 * rows, rows), lambda s: (at(s), 0, 0, 0)),
        ] + [whole(v.shape) for v in (vec, sums, wqkv, wo)] + [ANYWHERE] * 14,
        out_specs=[seq] + [in_vmem] * 7 + [ANYWHERE] * 3,
        out_shape=[sds(*x.shape)] + [sds(*s, dtype=F32) for s in shapes]
        + [sds(SUM_ROWS, width, dtype=F32), sds(*home.shape), sds(tok, 3 * width), sds(*home.shape)],
        scratch_shapes=[
            pltpu.VMEM((2, tok, width), BF16), pltpu.VMEM((2, tok, width), BF16), pltpu.VMEM((SLOTS, width, width), BF16),
            pltpu.VMEM((UNITS, 4, 4 * small, width), BF16),
            pltpu.VMEM((UNITS, 2, 2, 4 * small, width // 2), BF16), pltpu.VMEM((UNITS, 2, 4 * small, width // 2), BF16),
            pltpu.VMEM((8, 4, small, width), BF16),
            pltpu.VMEM((UNITS, 5, small, width), BF16), pltpu.VMEM((2, rows, 3 * width), BF16),
            pltpu.VMEM((2, rows, width), BF16),
            pltpu.VMEM((SUM_ROWS, 8, width), F32), pltpu.VMEM((5, SUM_ROWS, width), F32), pltpu.VMEM((6, SUM_ROWS, width), F32),
            dma((2,)), dma((2,)), dma((UNITS, 16)), dma((UNITS, 16)), dma((6,)), dma((6,)), dma((2,)), dma((2,)),
            dma((blocks, 3)), dma((blocks, 3)), dma((blocks - KEPT, 3)), dma((blocks - KEPT, 3)),
        ],
        input_output_aliases={19: 10, 20: 8},
        compiler_params=params(2),
        name="last",
    )(x, qkv, pt, vec, sums, wqkv, wo, z, g, a3, dh, ot, gt, a2, dp, a1, o, rest, out, home, out_home)
    return result[0], result[1:7], result[7], result[8]


def ring_layer(inputs, cotangent, shards, vec):
    clips, frames, places, width = inputs.shape
    x = inputs.reshape(clips * frames, places, width)
    (a1, qkv, pt, o), home, (wqkv, wo), vec, outs, (g, a2, dp, ot, gt, a3, z, dh, sums) = front(x, cotangent, vec, shards)
    saved = (z, g.reshape(a2.shape), a3, dh, ot, gt, a2, dp, a1, o, qkv, pt, sums)
    dx, grads, rows, output = last(x, home, outs, saved, vec, wqkv, wo, [s.shape for s in shards])
    return output, dx.reshape(inputs.shape), grads, rows


def my_index():
    return lax.axis_index("dp") * lax.axis_size("seq") + lax.axis_index("seq")


def spread_vectors(shards, width):
    devices = lax.axis_size("dp") * lax.axis_size("seq")
    me = my_index()
    rows = []
    for items in (NARROW, WIDE, (LONG,)):
        part = jnp.stack([shards[i] for i in items]).astype(F32)
        size = part.shape[1]
        zero = jnp.zeros((len(items), devices * size), F32)
        rows.append(lax.dynamic_update_slice(zero, part, (0, me * size)).reshape(-1, width))
    rows = jnp.concatenate(rows)
    return jnp.pad(rows, ((0, VEC_ROWS - rows.shape[0]), (0, 0)))


def own_vectors(rows):
    devices = lax.axis_size("dp") * lax.axis_size("seq")
    me = my_index()
    out, at = {}, 0
    width = rows.shape[1]
    for items, height in ((NARROW, 1), (WIDE, 2), ((LONG,), 4)):
        block = rows[at : at + height * len(items)].reshape(len(items), height * width)
        size = height * width // devices
        part = lax.dynamic_slice(block, (0, me * size), (len(items), size))
        for k, item in enumerate(items):
            out[item] = part[k]
        at += height * len(items)
    return [out[i] for i in range(12)]


def on_device(
    ring, inputs, norm_one_gain, norm_one_shift, space_qkv, space_qv_bias, space_out, space_out_bias,
    norm_two_gain, norm_two_shift, time_qkv, time_qv_bias, time_out, time_out_bias,
    norm_three_gain, norm_three_shift, mlp_in, mlp_in_bias, mlp_out, mlp_out_bias, cotangent,
):
    width = inputs.shape[-1]
    vec = spread_vectors(
        (norm_one_gain, norm_one_shift, space_qv_bias, space_out_bias, norm_two_gain, norm_two_shift,
         time_qv_bias, time_out_bias, norm_three_gain, norm_three_shift, mlp_in_bias, mlp_out_bias), width
    )
    shards = (space_qkv, space_out, time_qkv, time_out, mlp_in, mlp_out)
    layer = ring_layer if ring else plain_layer
    output, dx, grads, rows = layer(inputs, cotangent, shards, vec)
    gsqkv, gso, gtqkv, gto, gin, gout = grads
    vecs = own_vectors(rows)
    return (
        output, dx, vecs[0], vecs[1], gsqkv, vecs[2], gso, vecs[3], vecs[4], vecs[5], gtqkv,
        vecs[6], gto, vecs[7], vecs[8], vecs[9], gin, vecs[10], gout, vecs[11],
    )


def solution(mesh):
    tokens = P("dp", "seq", None, None)
    vector, matrix = P(("dp", "seq")), P(("dp", "seq"), None)
    weights = (vector, vector, matrix, vector, matrix, vector) * 3
    ring = mesh.shape["dp"] == 8 and mesh.shape["seq"] == 4
    return jax.shard_map(
        functools.partial(on_device, ring),
        mesh=mesh,
        in_specs=(tokens,) + weights + (tokens,),
        out_specs=(tokens, tokens) + weights,
        check_vma=False,
    )
```
